256 devices in a mesh: row: 32 (over z, x), col: 8 (over y, core).
Axes of the slice: x: 4, y: 4, z: 8, core: 2. Of those that a mesh axis runs over, the one named last changes fastest.
Arguments:
- src_points: float32 [3, 8192], P(None, 'row'), may hold values from 0 to 3
- tgt_points: float32 [3, 262144], P(None, 'col'), may hold values from 0 to 1
- src_mass: float32 [8192], P('row'), may hold values from 1 to 90
- tgt_mass: float32 [262144], P('col'), may hold values from 1 to 90
Outputs:
- src_pot: float32 [8192], P('row')
- tgt_pot: float32 [262144], P('col')
The draws below stay inside these ranges and needn't reach their ends.
All inputs are finite; a program needn't handle non-finite values.
Results may differ from the reference program's by a relative error of at most 0.0003.
Values sent between devices are 32-bit elements; how exact they have to be, the bound alone decides.
No kernel may reach another device: no remote copies, remote signals or barrier semaphores. Data moves between devices by JAX's collectives and lax.ppermute only.
A program may use at most 64 MiB of HBM per device.

```python
import jax
import jax.numpy as jnp
from jax import lax

ITERS = 2
NSRC = 8192
NTGT = 262144


def ramped_masses(key, count, upper):
    base = jnp.exp(jax.random.uniform(key, (count,), jnp.float32, 0.0, jnp.log(upper)))
    ramp = 1.0 + 2.0 * jnp.arange(count, dtype=jnp.float32) / max(count - 1, 1)
    return base * ramp


def draw_src_points(key, part):
    key = jax.random.fold_in(key, 11)
    points = jax.random.uniform(key, (3, NSRC), jnp.float32)
    return points


def draw_tgt_points(key, part):
    key = jax.random.fold_in(key, 12)
    points = jax.random.uniform(key, (3, NTGT), jnp.float32)
    return points


def draw_src_mass(key, part):
    key = jax.random.fold_in(key, 13)
    return ramped_masses(key, NSRC, 10.0)


def draw_tgt_mass(key, part):
    key = jax.random.fold_in(key, 14)
    return ramped_masses(key, NTGT, 10.0)


def setup_inputs(seed: int = 0) -> dict:
    key_list = jax.random.split(jax.random.key(seed), 5)
    return {
        "src_points": draw_src_points(jax.random.fold_in(key_list[4], 71), 0),
        "tgt_points": draw_tgt_points(jax.random.fold_in(key_list[4], 71), 0),
        "src_mass": draw_src_mass(jax.random.fold_in(key_list[4], 71), 0),
        "tgt_mass": draw_tgt_mass(jax.random.fold_in(key_list[4], 71), 0),
    }


epsilon = 0.01


def cost_block(sources, targets):
    total = (sources[0][:, None] - targets[0][None, :]) ** 2
    total = total + (sources[1][:, None] - targets[1][None, :]) ** 2
    total = total + (sources[2][:, None] - targets[2][None, :]) ** 2
    return total


def reference(src_points, tgt_points, src_mass, tgt_mass):
    log_src = jnp.log(src_mass) - jnp.log(jnp.sum(src_mass))
    log_tgt = jnp.log(tgt_mass) - jnp.log(jnp.sum(tgt_mass))
    src_pot = jnp.zeros((NSRC,), jnp.float32)
    tgt_pot = jnp.zeros((NTGT,), jnp.float32)
    row_block = min(64, NSRC)
    col_block = min(2048, NTGT)
    row_starts = jnp.arange(NSRC // row_block, dtype=jnp.int32) * row_block
    col_starts = jnp.arange(NTGT // col_block, dtype=jnp.int32) * col_block
    for sweep_index in range(ITERS):
        col_term = tgt_pot + log_tgt

        def row_update(start):
            sources = lax.dynamic_slice_in_dim(src_points, start, row_block, 1)
            scores = col_term[None, :] - cost_block(sources, tgt_points) / epsilon
            peak = jnp.max(scores, axis=1)
            return -(peak + jnp.log(jnp.sum(jnp.exp(scores - peak[:, None]), axis=1)))

        src_pot = lax.map(row_update, row_starts).reshape(NSRC)
        row_term = src_pot + log_src

        def col_update(start):
            targets = lax.dynamic_slice_in_dim(tgt_points, start, col_block, 1)
            scores = row_term[:, None] - cost_block(src_points, targets) / epsilon
            peak = jnp.max(scores, axis=0)
            return -(peak + jnp.log(jnp.sum(jnp.exp(scores - peak[None, :]), axis=0)))

        tgt_pot = lax.map(col_update, col_starts).reshape(NTGT)
    return src_pot, tgt_pot
```

```python
import functools
import math

import jax
import jax.numpy as jnp
from jax import lax
from jax.experimental import pallas as pl
from jax.experimental.pallas import tpu as pltpu
from jax.sharding import PartitionSpec as P

EPSILON = 0.01
LN2 = math.log(2.0)
SCALE = 1.0 / (EPSILON * LN2)
CENTER = 0.5
FLOOR1 = 2.0**-60
FLOOR2 = 2.0**-40
HIGH = 96 * 1024 * 1024 // 2
BF16 = jnp.bfloat16
F32 = jnp.float32


def pieces(v):
    p1 = v.astype(BF16).astype(F32)
    r = v - p1
    p2 = r.astype(BF16).astype(F32)
    p3 = (r - p2).astype(BF16).astype(F32)
    return p1, p2, p3


def stack_src(v):
    p1, p2, p3 = pieces(v)
    return [
        jnp.concatenate([p1, p2], axis=0),
        jnp.concatenate([p3, p1], axis=0),
        jnp.concatenate([p2, p1], axis=0),
    ]


def stack_tgt(v):
    p1, p2, p3 = pieces(v)
    return [
        jnp.concatenate([p1, p1], axis=0),
        jnp.concatenate([p1, p2], axis=0),
        jnp.concatenate([p2, p3], axis=0),
    ]


def norm_rows(ref):
    a, b, c = ref[0:1, :], ref[1:2, :], ref[2:3, :]
    return -SCALE * (a * a + b * b + c * c)


def scores(lhs, rhs):
    return lax.dot_general(
        lhs, rhs, (((1,), (0,)), ((), ())), preferred_element_type=F32
    )


def fold(v, op):
    out = v[:, 0:128]
    for k in range(128, v.shape[1], 128):
        out = op(out, v[:, k : k + 128])
    return out


def to_row(col128):
    return jnp.transpose(col128)[0:1, :]


def set_src(x_ref, points, bias):
    n = points.shape[1]
    x_ref[0:3, :] = points - CENTER
    x_ref[4:5, :] = norm_rows(x_ref) + bias
    x_ref[0:3, :] = x_ref[0:3, :] * (2.0 * SCALE)
    x_ref[3:4, :] = jnp.ones((1, n), F32)
    x_ref[5:8, :] = jnp.zeros((3, n), F32)


def set_tgt(t_ref, points, bias):
    n = points.shape[1]
    t_ref[0:3, :] = points - CENTER
    t_ref[3:4, :] = norm_rows(t_ref) + bias
    t_ref[4:5, :] = jnp.ones((1, n), F32)
    t_ref[5:8, :] = jnp.zeros((3, n), F32)


def row_kernel(src_ref, tgt_ref, mass_ref, out_ref, x_ref, t_ref, w_ref, acc_ref):
    n = tgt_ref.shape[1]
    rows = src_ref.shape[1]
    chunk = 1024
    mass = mass_ref[...]
    set_src(x_ref, src_ref[...], 0.0)
    set_tgt(t_ref, tgt_ref[...], jnp.log2(mass))
    for k, part in enumerate(stack_tgt(t_ref[...])):
        w_ref[16 * k : 16 * k + 16, :] = part.astype(BF16)
    xt = jnp.transpose(jnp.concatenate(stack_src(x_ref[...]), axis=0)).astype(BF16)

    def block(k):
        cols = pl.ds(pl.multiple_of(k * chunk, chunk), chunk)
        return scores(xt, w_ref[:, cols])

    def step(k, acc):
        return acc + fold(jnp.exp2(block(k)), jnp.add)

    acc = lax.fori_loop(0, n // chunk, step, jnp.zeros((rows, 128), F32))
    acc_ref[...] = acc
    total = jnp.sum(jnp.transpose(acc), axis=0, keepdims=True)
    out_ref[0:1, :] = jnp.log2(total)
    out_ref[1:2, :] = jnp.full((1, rows), jnp.sum(mass), F32)
    out_ref[2:8, :] = jnp.zeros((6, rows), F32)

    @pl.when(jnp.min(total) < FLOOR1)
    def _():
        def top(k, m):
            return jnp.maximum(m, fold(block(k), jnp.maximum))

        m = lax.fori_loop(0, n // chunk, top, jnp.full((rows, 128), -jnp.inf, F32))
        m = jnp.max(m, axis=1, keepdims=True)

        def shifted(k, acc):
            return acc + fold(jnp.exp2(block(k) - m), jnp.add)

        acc = lax.fori_loop(0, n // chunk, shifted, jnp.zeros((rows, 128), F32))
        total = jnp.sum(jnp.transpose(acc), axis=0, keepdims=True)
        out_ref[0:1, :] = jnp.log2(total) + to_row(jnp.broadcast_to(m, (rows, 128)))


def prepare(gath_ref, ratio, tgt_ref, shift, mass_ref, x_ref, t_ref, w_ref):
    set_src(
        x_ref,
        gath_ref[0:3, :],
        jnp.log2(gath_ref[3:4, :]) - gath_ref[4:5, :] + ratio,
    )
    for k, part in enumerate(stack_src(x_ref[...])):
        w_ref[16 * k : 16 * k + 16, :] = part.astype(BF16)
    set_tgt(t_ref, tgt_ref[...], shift)
    tt = jnp.transpose(jnp.concatenate(stack_tgt(t_ref[...]), axis=0)).astype(BF16)
    return tt


TILE = 256


def middle_kernel(
    gath_ref, tgt_ref, mass_ref, out_ref, shift_ref, x_ref, t_ref, w_ref, q_ref, r_ref, m_ref, l_ref
):
    n = gath_ref.shape[1]
    chunk = 1024
    tt = prepare(gath_ref, 0.0, tgt_ref, 0.0, mass_ref, x_ref, t_ref, w_ref)
    mass_col = jnp.transpose(jnp.broadcast_to(mass_ref[...], (128, mass_ref.shape[1])))
    r_ref[...] = jnp.zeros((8, n), F32)
    for t in range(tgt_ref.shape[1] // TILE):
        lhs = tt[t * TILE : (t + 1) * TILE]

        def block(k, lhs=lhs):
            cols = pl.ds(pl.multiple_of(k * chunk, chunk), chunk)
            return cols, scores(lhs, w_ref[:, cols])

        def step(k, acc):
            cols, s = block(k)
            q = jnp.exp2(s)
            q_ref[:, cols] = q
            return acc + fold(q, jnp.add)

        acc = lax.fori_loop(0, n // chunk, step, jnp.zeros((TILE, 128), F32))
        total = jnp.sum(acc, axis=1, keepdims=True)
        l_ref[...] = jnp.broadcast_to(total, (TILE, 128))
        m_ref[...] = jnp.zeros((TILE, 128), F32)

        @pl.when(jnp.min(total) < FLOOR2)
        def _():
            def top(k, m):
                return jnp.maximum(m, fold(block(k)[1], jnp.maximum))

            m = lax.fori_loop(
                0, n // chunk, top, jnp.full((TILE, 128), -jnp.inf, F32)
            )
            m = jnp.max(m, axis=1, keepdims=True)

            def shifted(k, acc):
                cols, s = block(k)
                q = jnp.exp2(s - m)
                q_ref[:, cols] = q
                return acc + fold(q, jnp.add)

            acc = lax.fori_loop(0, n // chunk, shifted, jnp.zeros((TILE, 128), F32))
            l_ref[...] = jnp.broadcast_to(
                jnp.sum(acc, axis=1, keepdims=True), (TILE, 128)
            )
            m_ref[...] = jnp.broadcast_to(m, (TILE, 128))

        weight = mass_col[t * TILE : (t + 1) * TILE] / l_ref[...]
        shift_ref[0:1, t * TILE : (t + 1) * TILE] = to_row(m_ref[...])

        def spread(k, carry):
            cols = pl.ds(pl.multiple_of(k * 128, 128), 128)
            v = q_ref[:, cols] * weight
            out = v[0:8]
            for g in range(8, TILE, 8):
                out = out + v[g : g + 8]
            r_ref[:, cols] += out
            return carry

        lax.fori_loop(0, n // 128, spread, 0, unroll=4)
    out_ref[...] = jnp.sum(r_ref[...], axis=0, keepdims=True)


def last_kernel(
    gath_ref, ratio_ref, tgt_ref, shift_ref, mass_ref, out_ref, x_ref, t_ref, w_ref
):
    n = gath_ref.shape[1]
    chunk = 1024
    ratio = jnp.log2(gath_ref[3:4, :]) - jnp.log2(ratio_ref[...])
    tt = prepare(gath_ref, ratio, tgt_ref, -shift_ref[...], mass_ref, x_ref, t_ref, w_ref)
    for t in range(tgt_ref.shape[1] // TILE):
        lhs = tt[t * TILE : (t + 1) * TILE]

        def step(k, acc, lhs=lhs):
            cols = pl.ds(pl.multiple_of(k * chunk, chunk), chunk)
            return acc + fold(jnp.exp2(scores(lhs, w_ref[:, cols])), jnp.add)

        acc = lax.fori_loop(0, n // chunk, step, jnp.zeros((TILE, 128), F32))
        total = jnp.sum(jnp.transpose(acc), axis=0, keepdims=True)
        here = pl.ds(t * TILE, TILE)
        out_ref[0:1, here] = -LN2 * (jnp.log2(total) + shift_ref[0:1, here])


def kernel_call(body, out_shape, scratch, args):
    n_out = len(out_shape)
    vmem = pl.BlockSpec(memory_space=pltpu.VMEM)
    return pl.pallas_call(
        body,
        out_shape=[jax.ShapeDtypeStruct(s, F32) for s in out_shape],
        in_specs=[vmem] * len(args),
        out_specs=[vmem] * n_out,
        scratch_shapes=scratch,
        compiler_params=pltpu.CompilerParams(vmem_limit_bytes=HIGH),
    )(*args)


def spread_to(v, axis, count):
    return lax.all_to_all(jnp.broadcast_to(v[None], (count,) + v.shape), axis, 0, 0)


def on_device(n_row, n_col, src_points, tgt_points, src_mass, tgt_mass):
    rows = src_points.shape[1]
    cols = tgt_points.shape[1]
    nsrc = rows * n_row
    mine = cols // n_row
    row = lax.axis_index("row")

    (first,) = kernel_call(
        row_kernel,
        [(8, rows)],
        [
            pltpu.VMEM((8, rows), F32),
            pltpu.VMEM((8, cols), F32),
            pltpu.VMEM((48, cols), BF16),
            pltpu.VMEM((rows, 128), F32),
        ],
        (src_points, tgt_points, tgt_mass.reshape(1, cols)),
    )
    first = spread_to(first[0:2], "col", n_col)
    part, sums = first[:, 0], first[:, 1, 0]
    tgt_total = jnp.sum(sums)
    peak = jnp.max(part, axis=0)
    log_sum = peak + jnp.log2(jnp.sum(jnp.exp2(part - peak), axis=0))
    payload = jnp.concatenate(
        [src_points, src_mass[None], log_sum[None], jnp.zeros((3, rows), F32)], axis=0
    )
    gath = spread_to(payload, "row", n_row)
    gath = jnp.transpose(gath, (1, 0, 2)).reshape(8, nsrc)
    my_tgt = lax.dynamic_slice_in_dim(tgt_points, row * mine, mine, 1)
    my_mass = lax.dynamic_slice_in_dim(tgt_mass, row * mine, mine, 0).reshape(1, mine)
    src_total = jnp.sum(gath[3])

    common = [
        pltpu.VMEM((8, nsrc), F32),
        pltpu.VMEM((8, mine), F32),
        pltpu.VMEM((48, nsrc), BF16),
    ]
    ratio, shift = kernel_call(
        middle_kernel,
        [(1, nsrc), (1, mine)],
        common
        + [
            pltpu.VMEM((TILE, nsrc), F32),
            pltpu.VMEM((8, nsrc), F32),
            pltpu.VMEM((TILE, 128), F32),
            pltpu.VMEM((TILE, 128), F32),
        ],
        (gath, my_tgt, my_mass),
    )
    ratio = lax.all_to_all(ratio.reshape(n_col, nsrc // n_col), "col", 0, 0)
    ratio = jnp.sum(spread_to(jnp.sum(ratio, axis=0), "row", n_row), axis=0)
    ratio = spread_to(ratio, "col", n_col).reshape(1, nsrc)

    (pot,) = kernel_call(
        last_kernel, [(1, mine)], common, (gath, ratio, my_tgt, shift, my_mass)
    )
    log_src_total, log_tgt_total = jnp.log(src_total), jnp.log(tgt_total)
    pot = pot[0] + 2.0 * (log_src_total - log_tgt_total)
    tgt_pot = spread_to(pot, "row", n_row).reshape(cols)
    my_ratio = lax.dynamic_slice_in_dim(ratio[0], row * rows, rows, 0)
    src_pot = (
        -LN2 * log_sum
        + jnp.log(src_mass)
        - jnp.log(my_ratio)
        + 2.0 * log_tgt_total
        - log_src_total
    )
    return (src_pot, tgt_pot)


def solution(mesh):
    placed = (P(None, "row"), P(None, "col"), P("row"), P("col"))
    body = functools.partial(on_device, mesh.shape["row"], mesh.shape["col"])
    return jax.shard_map(
        body, mesh=mesh, in_specs=placed, out_specs=(P("row"), P("col")), check_vma=False
    )
```

```python
import functools
import math

import jax
import jax.numpy as jnp
from jax import lax
from jax.experimental import pallas as pl
from jax.experimental.pallas import tpu as pltpu
from jax.sharding import Mesh, PartitionSpec as P

EPSILON = 0.01
LN2 = math.log(2.0)
SCALE = 1.0 / (EPSILON * LN2)
CENTER = 0.5
FLOOR1 = 2.0**-60
FLOOR2 = 2.0**-40
VMEM_BYTES = 48 * 1024 * 1024
BF16 = jnp.bfloat16
F32 = jnp.float32

Z, X, Y, C = 8, 4, 4, 2
NCOL = Y * C
GROUP = X * NCOL


def pieces(v):
    p1 = v.astype(BF16).astype(F32)
    r = v - p1
    p2 = r.astype(BF16).astype(F32)
    p3 = (r - p2).astype(BF16).astype(F32)
    return p1, p2, p3


def stack_src(v):
    p1, p2, p3 = pieces(v)
    return [
        jnp.concatenate([p1, p2], axis=0),
        jnp.concatenate([p3, p1], axis=0),
        jnp.concatenate([p2, p1], axis=0),
    ]


def stack_tgt(v):
    p1, p2, p3 = pieces(v)
    return [
        jnp.concatenate([p1, p1], axis=0),
        jnp.concatenate([p1, p2], axis=0),
        jnp.concatenate([p2, p3], axis=0),
    ]


def scores(lhs, rhs):
    return lax.dot_general(
        lhs, rhs, (((1,), (0,)), ((), ())), preferred_element_type=F32
    )


def fold(v, op):
    out = v[:, 0:128]
    for k in range(128, v.shape[1], 128):
        out = op(out, v[:, k : k + 128])
    return out


def norm_rows(ref):
    a, b, c = ref[0:1, :], ref[1:2, :], ref[2:3, :]
    return -SCALE * (a * a + b * b + c * c)


def src_side(x_ref):
    n = x_ref.shape[1]
    x_ref[0:3, :] = x_ref[0:3, :] - CENTER
    x_ref[4:5, :] = x_ref[4:5, :] + norm_rows(x_ref)
    x_ref[0:3, :] = x_ref[0:3, :] * (2.0 * SCALE)
    x_ref[3:4, :] = jnp.ones((1, n), F32)
    x_ref[5:8, :] = jnp.zeros((3, n), F32)
    stacked = jnp.concatenate(stack_src(x_ref[...]), axis=0)
    return jnp.transpose(stacked).astype(BF16)


def tgt_side(t_ref, w_ref, points):
    n = points.shape[1]
    t_ref[0:3, :] = points - CENTER
    t_ref[3:4, :] = t_ref[3:4, :] + norm_rows(t_ref)
    t_ref[4:5, :] = jnp.ones((1, n), F32)
    t_ref[5:8, :] = jnp.zeros((3, n), F32)
    for k, part in enumerate(stack_tgt(t_ref[...])):
        w_ref[16 * k : 16 * k + 16, :] = part.astype(BF16)


def row_of(tile):
    return jnp.concatenate([tile[s : s + 1, :] for s in range(tile.shape[0])], axis=1)


def set_tile(ref, row):
    for s in range(row.shape[1] // 128):
        ref[s : s + 1, :] = row[:, 128 * s : 128 * s + 128]


def row_kernel(src_ref, src_mass_ref, tgt_ref, mass_ref, out_ref, x_ref, t_ref, w_ref, o_ref):
    n = tgt_ref.shape[1]
    rows = src_ref.shape[1]
    chunk = 8192
    x_ref[0:3, :] = src_ref[...]
    x_ref[4:5, :] = jnp.zeros((1, rows), F32)
    lhs = src_side(x_ref)
    t_ref[3:4, :] = jnp.log2(mass_ref[...])
    tgt_side(t_ref, w_ref, tgt_ref[...])

    def block(k):
        return scores(lhs, w_ref[:, pl.ds(pl.multiple_of(k * chunk, chunk), chunk)])

    def step(k, acc):
        return acc + fold(jnp.exp2(block(k)), jnp.add)

    acc = lax.fori_loop(0, n // chunk, step, jnp.zeros((rows, 128), F32))
    total = jnp.sum(jnp.transpose(acc), axis=0, keepdims=True)
    o_ref[...] = jnp.zeros((8, 128), F32)
    set_tile(o_ref, jnp.log2(total))

    @pl.when(jnp.min(total) < FLOOR1)
    def _():
        def top(k, m):
            return jnp.maximum(m, fold(block(k), jnp.maximum))

        m = lax.fori_loop(0, n // chunk, top, jnp.full((rows, 128), -jnp.inf, F32))
        m = jnp.max(m, axis=1, keepdims=True)

        def shifted(k, acc):
            return acc + fold(jnp.exp2(block(k) - m), jnp.add)

        acc = lax.fori_loop(0, n // chunk, shifted, jnp.zeros((rows, 128), F32))
        total = jnp.sum(jnp.transpose(acc), axis=0, keepdims=True)
        peak = jnp.transpose(jnp.broadcast_to(m, (rows, 128)))[0:1, :]
        set_tile(o_ref, jnp.log2(total) + peak)

    col = lax.axis_index("y") * C + lax.axis_index("c")
    info = src_mass_ref[...]
    for d in range(3):
        info = jnp.where(col == d, src_ref[d : d + 1, :], info)
    for s in range(rows // 128):
        o_ref[2 + s : 3 + s, :] = info[:, 128 * s : 128 * s + 128]
    for p in range(out_ref.shape[0]):
        out_ref[p] = o_ref[...]


def set_src(first_ref, x_ref):
    logs, masses = [], []
    for x in range(X):
        parts = [first_ref[x * NCOL + q] for q in range(NCOL)]
        peak = functools.reduce(jnp.maximum, parts)
        total = functools.reduce(jnp.add, [jnp.exp2(v - peak) for v in parts])
        log_sum = peak + jnp.log2(total)
        for s in range(2):
            lanes = slice(256 * x + 128 * s, 256 * x + 128 * s + 128)
            for d in range(3):
                x_ref[d : d + 1, lanes] = parts[d][2 + s : 3 + s, :]
            logs.append(log_sum[s : s + 1, :])
            masses.append(parts[3][2 + s : 3 + s, :])
    mass = jnp.concatenate(masses, axis=1)
    return jnp.log2(mass), mass, jnp.concatenate(logs, axis=1)


def my_targets(tgt_ref, count):
    start = pl.multiple_of(lax.axis_index("x") * count, count)
    return tgt_ref[:, pl.ds(start, count)]


def col_kernel(first_ref, tgt_ref, out_ref, x_ref, t_ref, w_ref, s_ref):
    n = t_ref.shape[1]
    chunk = n // 8
    log_mass, _, log_sum = set_src(first_ref, x_ref)
    x_ref[4:5, :] = log_mass - log_sum
    lhs = src_side(x_ref)
    t_ref[3:4, :] = jnp.zeros((1, n), F32)
    tgt_side(t_ref, w_ref, my_targets(tgt_ref, n))

    def block(k):
        return scores(lhs, w_ref[:, pl.ds(pl.multiple_of(k * chunk, chunk), chunk)])

    def step(k, carry):
        q = jnp.exp2(block(k))
        s_ref[pl.ds(k, 1), :] = jnp.sum(q, axis=0, keepdims=True)
        return carry

    lax.fori_loop(0, 8, step, 0)
    total = s_ref[...]
    s_ref[...] = jnp.log2(total)

    @pl.when(jnp.min(total) < FLOOR2)
    def _():
        def shifted(k, carry):
            s = block(k)
            m = jnp.max(s, axis=0, keepdims=True)
            l = jnp.sum(jnp.exp2(s - m), axis=0, keepdims=True)
            s_ref[pl.ds(k, 1), :] = m + jnp.log2(l)
            return carry

        lax.fori_loop(0, 8, shifted, 0)

    for p in range(Z):
        out_ref[p] = s_ref[...]


def mid_kernel(first_ref, cols_ref, tgt_ref, mass_ref, out_ref, log_ref, x_ref, t_ref, w_ref, o_ref):
    n = t_ref.shape[1]
    rows = x_ref.shape[1]
    chunk = n // 8
    log_mass, _, log_sum = set_src(first_ref, x_ref)
    x_ref[4:5, :] = log_mass - log_sum
    lhs = src_side(x_ref)
    parts = [cols_ref[z] for z in range(Z)]
    peak = functools.reduce(jnp.maximum, parts)
    total = functools.reduce(jnp.add, [jnp.exp2(v - peak) for v in parts])
    log_col = peak + jnp.log2(total)
    log_ref[...] = log_col
    for k in range(8):
        lanes = slice(k * chunk, (k + 1) * chunk)
        t_ref[3:4, lanes] = -log_col[k : k + 1, :]
    t_ref[3:4, :] = t_ref[3:4, :] + jnp.log2(my_targets(mass_ref, n))
    tgt_side(t_ref, w_ref, my_targets(tgt_ref, n))
    w = w_ref[...]
    tile = 256
    sums = []
    for r in range(0, rows, tile):
        acc = fold(jnp.exp2(scores(lhs[r : r + tile], w)), jnp.add)
        sums.append(jnp.sum(jnp.transpose(acc), axis=0, keepdims=True))
    set_tile(o_ref, jnp.concatenate(sums, axis=1))
    for p in range(out_ref.shape[0]):
        out_ref[p] = o_ref[...]


def last_kernel(
    first_ref, log_ref, ratio_ref, tgt_ref, out_ref, pot_ref, x_ref, t_ref, w_ref, s_ref
):
    n = t_ref.shape[1]
    chunk = n // 8
    log_mass, mass, log_sum = set_src(first_ref, x_ref)
    ratio = ratio_ref[0]
    for p in range(1, ratio_ref.shape[0]):
        ratio = ratio + ratio_ref[p]
    ratio = row_of(ratio)
    base = log_mass - log_sum - jnp.log2(ratio)
    x_ref[4:5, :] = base + log_mass
    s_ref[0:1, :] = LN2 * base
    rows = pot_ref.shape[1]
    mine = pl.multiple_of(lax.axis_index("x") * rows, rows)
    pot_ref[...] = s_ref[0:1, pl.ds(mine, rows)]
    lhs = src_side(x_ref)
    for k in range(8):
        t_ref[3:4, k * chunk : (k + 1) * chunk] = -log_ref[k : k + 1, :]
    tgt_side(t_ref, w_ref, my_targets(tgt_ref, n))

    def step(k, carry):
        cols = pl.ds(pl.multiple_of(k * chunk, chunk), chunk)
        q = jnp.exp2(scores(lhs, w_ref[:, cols]))
        s_ref[pl.ds(k, 1), :] = jnp.sum(q, axis=0, keepdims=True)
        return carry

    lax.fori_loop(0, 8, step, 0)
    row = lax.broadcasted_iota(jnp.int32, (8, 128), 0)
    extra = jnp.where(row == 0, jnp.sum(mass), jnp.sum(ratio))
    for p in range(Z):
        out_ref[p, :, 0:chunk] = s_ref[...]
        out_ref[p, :, chunk : chunk + 128] = extra


def end_kernel(cols_ref, log_ref, pot_ref, out_ref, src_ref, o_ref):
    chunk = log_ref.shape[1]
    total = cols_ref[0]
    for z in range(1, Z):
        total = total + cols_ref[z]
    sums = jnp.log(total[:, chunk : chunk + 128])
    log_src, log_tgt = sums[0:1, 0:1], sums[1:2, 0:1]
    src_ref[...] = pot_ref[...] + (2.0 * log_tgt - log_src)
    pot = -LN2 * (jnp.log2(total[:, 0:chunk]) + log_ref[...]) + 2.0 * (log_src - log_tgt)
    per = chunk // 128
    for k in range(8):
        for s in range(per):
            o_ref[per * k + s : per * k + s + 1, :] = pot[k : k + 1, 128 * s : 128 * s + 128]
    for p in range(X):
        out_ref[p] = o_ref[...]


def kernel_call(body, out_shape, scratch, args):
    vmem = pl.BlockSpec(memory_space=pltpu.VMEM)
    return pl.pallas_call(
        body,
        out_shape=[jax.ShapeDtypeStruct(s, F32) for s in out_shape],
        in_specs=[vmem] * len(args),
        out_specs=[vmem] * len(out_shape),
        scratch_shapes=scratch,
        compiler_params=pltpu.CompilerParams(vmem_limit_bytes=VMEM_BYTES),
    )(*args)


def trade(v, axes):
    return lax.all_to_all(v, axes, 0, 0)


def on_device(src_points, tgt_points, src_mass, tgt_mass):
    rows = src_points.shape[1]
    cols = tgt_points.shape[1]
    nsrc = rows * X
    ntgt = cols // X
    chunk = ntgt // 8
    tgt_mass = tgt_mass.reshape(1, cols)

    (first,) = kernel_call(
        row_kernel,
        [(GROUP, 8, 128)],
        [
            pltpu.VMEM((8, rows), F32),
            pltpu.VMEM((8, cols), F32),
            pltpu.VMEM((48, cols), BF16),
            pltpu.VMEM((8, 128), F32),
        ],
        (src_points, src_mass.reshape(1, rows), tgt_points, tgt_mass),
    )
    first = trade(first, ("x", "y", "c"))
    scratch = [
        pltpu.VMEM((8, nsrc), F32),
        pltpu.VMEM((8, ntgt), F32),
        pltpu.VMEM((48, ntgt), BF16),
    ]
    sums = pltpu.VMEM((8, chunk), F32)
    (logs,) = kernel_call(
        col_kernel, [(Z, 8, chunk)], scratch + [sums], (first, tgt_points)
    )
    logs = trade(logs, "z")
    ratio, log_col = kernel_call(
        mid_kernel,
        [(GROUP, 8, 128), (8, chunk)],
        scratch + [pltpu.VMEM((8, 128), F32)],
        (first, logs, tgt_points, tgt_mass),
    )
    ratio = trade(ratio, ("x", "y", "c"))
    col_sums, base = kernel_call(
        last_kernel,
        [(Z, 8, chunk + 128), (1, rows)],
        scratch + [sums],
        (first, log_col, ratio, tgt_points),
    )
    col_sums = trade(col_sums, "z")
    tgt_pot, src_pot = kernel_call(
        end_kernel,
        [(X, ntgt // 128, 128), (1, rows)],
        [pltpu.VMEM((ntgt // 128, 128), F32)],
        (col_sums, log_col, base),
    )
    return (src_pot.reshape(rows), trade(tgt_pot, "x").reshape(cols))


def solution(mesh):
    fine = Mesh(mesh.devices.reshape(Z, X, Y, C), ("z", "x", "y", "c"))
    row, col = ("z", "x"), ("y", "c")
    placed = (P(None, row), P(None, col), P(row), P(col))
    return jax.shard_map(
        on_device, mesh=fine, in_specs=placed, out_specs=(P(row), P(col)), check_vma=False
    )
```

```python
import functools
import math

import jax
import jax.numpy as jnp
from jax import lax
from jax.experimental import pallas as pl
from jax.experimental.pallas import tpu as pltpu
from jax.sharding import Mesh, PartitionSpec as P

EPSILON = 0.01
LN2 = math.log(2.0)
SCALE = 1.0 / (EPSILON * LN2)
CENTER = 0.5
FLOOR1 = 2.0**-60
FLOOR2 = 2.0**-40
BF16 = jnp.bfloat16
F32 = jnp.float32

Z, X, Y, C = 8, 4, 4, 2
NCOL = Y * C
GROUP = X * NCOL


def pieces(v):
    p1 = v.astype(BF16).astype(F32)
    r = v - p1
    p2 = r.astype(BF16).astype(F32)
    p3 = (r - p2).astype(BF16).astype(F32)
    return p1, p2, p3


def stack_src(v):
    p1, p2, p3 = pieces(v)
    return [
        jnp.concatenate([p1, p2], axis=0),
        jnp.concatenate([p3, p1], axis=0),
        jnp.concatenate([p2, p1], axis=0),
    ]


def stack_tgt(v):
    p1, p2, p3 = pieces(v)
    return [
        jnp.concatenate([p1, p1], axis=0),
        jnp.concatenate([p1, p2], axis=0),
        jnp.concatenate([p2, p3], axis=0),
    ]


def scores(lhs, rhs):
    return lax.dot_general(
        lhs, rhs, (((1,), (0,)), ((), ())), preferred_element_type=F32
    )


def fold(v, op):
    out = v[:, 0:128]
    for k in range(128, v.shape[1], 128):
        out = op(out, v[:, k : k + 128])
    return out


def norm_rows(ref):
    a, b, c = ref[0:1, :], ref[1:2, :], ref[2:3, :]
    return -SCALE * (a * a + b * b + c * c)


def src_side(x_ref):
    n = x_ref.shape[1]
    x_ref[0:3, :] = x_ref[0:3, :] - CENTER
    x_ref[4:5, :] = x_ref[4:5, :] + norm_rows(x_ref)
    x_ref[0:3, :] = x_ref[0:3, :] * (2.0 * SCALE)
    x_ref[3:4, :] = jnp.ones((1, n), F32)
    x_ref[5:8, :] = jnp.zeros((3, n), F32)
    stacked = jnp.concatenate(stack_src(x_ref[...]), axis=0)
    return jnp.transpose(stacked).astype(BF16)


def tgt_side(t_ref, w_ref, lanes):
    for k, part in enumerate(stack_tgt(t_ref[:, lanes])):
        w_ref[16 * k : 16 * k + 16, lanes] = part.astype(BF16)


def row_of(tile):
    return jnp.concatenate([tile[s : s + 1, :] for s in range(tile.shape[0])], axis=1)


def set_tile(ref, row):
    for s in range(row.shape[1] // 128):
        ref[s : s + 1, :] = row[:, 128 * s : 128 * s + 128]


def row_kernel(
    src_hbm,
    src_mass_hbm,
    tgt_hbm,
    mass_hbm,
    out_ref,
    base_ref,
    src_ref,
    src_mass_ref,
    tgt_ref,
    mass_ref,
    sem,
    x_ref,
    t_ref,
    w_ref,
    o_ref,
):
    n = tgt_ref.shape[1]
    rows = src_ref.shape[1]
    chunk = n // 4
    moves = [
        pltpu.make_async_copy(a, b, sem.at[i])
        for i, (a, b) in enumerate(
            [
                (src_hbm, src_ref),
                (src_mass_hbm, src_mass_ref),
                (tgt_hbm, tgt_ref),
                (mass_hbm, mass_ref),
            ]
        )
    ]
    for move in moves:
        move.start()
    moves[0].wait()
    x_ref[0:3, :] = src_ref[...]
    x_ref[4:5, :] = jnp.zeros((1, rows), F32)
    lhs = src_side(x_ref)
    for move in moves[1:]:
        move.wait()

    acc = jnp.zeros((rows, 128), F32)
    for k in range(4):
        lanes = slice(k * chunk, (k + 1) * chunk)
        points = tgt_ref[:, lanes] - CENTER
        t_ref[0:3, lanes] = points
        log_mass = jnp.log2(mass_ref[:, lanes])
        norm = -SCALE * jnp.sum(points * points, axis=0, keepdims=True)
        t_ref[3:4, lanes] = norm + log_mass
        t_ref[4:5, lanes] = jnp.ones((1, chunk), F32)
        t_ref[5:6, lanes] = log_mass
        t_ref[6:8, lanes] = jnp.zeros((2, chunk), F32)
        tgt_side(t_ref, w_ref, lanes)
        acc = acc + fold(jnp.exp2(scores(lhs, w_ref[:, lanes])), jnp.add)
    total = jnp.sum(jnp.transpose(acc), axis=0, keepdims=True)
    o_ref[...] = jnp.zeros((8, 128), F32)
    set_tile(o_ref, jnp.log2(total))

    @pl.when(jnp.min(total) < FLOOR1)
    def _():
        small = 1024

        def block(k):
            return scores(lhs, w_ref[:, pl.ds(pl.multiple_of(k * small, small), small)])

        def top(k, m):
            return jnp.maximum(m, fold(block(k), jnp.maximum))

        m = lax.fori_loop(0, n // small, top, jnp.full((rows, 128), -jnp.inf, F32))
        m = jnp.max(m, axis=1, keepdims=True)

        def shifted(k, acc):
            return acc + fold(jnp.exp2(block(k) - m), jnp.add)

        acc = lax.fori_loop(0, n // small, shifted, jnp.zeros((rows, 128), F32))
        total = jnp.sum(jnp.transpose(acc), axis=0, keepdims=True)
        peak = jnp.transpose(jnp.broadcast_to(m, (rows, 128)))[0:1, :]
        set_tile(o_ref, jnp.log2(total) + peak)

    col = lax.axis_index("y") * C + lax.axis_index("c")
    info = src_mass_ref[...]
    for d in range(3):
        info = jnp.where(col == d, src_ref[d : d + 1, :], info)
    for s in range(rows // 128):
        o_ref[2 + s : 3 + s, :] = info[:, 128 * s : 128 * s + 128]
    for p in range(out_ref.shape[0]):
        out_ref[p] = o_ref[...]
    share = base_ref.shape[1]
    base_ref[...] = t_ref[:, pl.ds(pl.multiple_of(lax.axis_index("x") * share, share), share)]


def set_src(first_ref, x_ref):
    logs, masses = [], []
    for x in range(X):
        parts = [first_ref[x * NCOL + q] for q in range(NCOL)]
        peak = functools.reduce(jnp.maximum, parts)
        total = functools.reduce(jnp.add, [jnp.exp2(v - peak) for v in parts])
        log_sum = peak + jnp.log2(total)
        for s in range(2):
            lanes = slice(256 * x + 128 * s, 256 * x + 128 * s + 128)
            for d in range(3):
                x_ref[d : d + 1, lanes] = parts[d][2 + s : 3 + s, :]
            logs.append(log_sum[s : s + 1, :])
            masses.append(parts[3][2 + s : 3 + s, :])
    mass = jnp.concatenate(masses, axis=1)
    return jnp.log2(mass), mass, jnp.concatenate(logs, axis=1)


def col_kernel(
    first_ref, base_ref, qa_ref, qb_ref, out_ref, shift_ref, src_ref, x_ref, t_ref, w_ref, s_ref
):
    n = t_ref.shape[1]
    chunk = n // 8
    log_mass, mass, log_sum = set_src(first_ref, x_ref)
    src_ref[...] = jnp.zeros(src_ref.shape, F32)
    src_ref[0:1, :] = log_mass - log_sum
    src_ref[1:2, :] = mass
    x_ref[4:5, :] = log_mass - log_sum
    lhs = src_side(x_ref)
    t_ref[...] = base_ref[...]
    t_ref[3:4, :] = base_ref[3:4, :] - base_ref[5:6, :]
    tgt_side(t_ref, w_ref, slice(0, n))

    def block(k):
        return scores(lhs, w_ref[:, pl.ds(pl.multiple_of(k * chunk, chunk), chunk)])

    for half, q_ref in enumerate((qa_ref, qb_ref)):

        def step(k, carry, half=half, q_ref=q_ref):
            q = jnp.exp2(block(4 * half + k))
            q_ref[:, pl.ds(pl.multiple_of(k * chunk, chunk), chunk)] = q
            s_ref[pl.ds(4 * half + k, 1), :] = jnp.sum(q, axis=0, keepdims=True)
            return carry

        lax.fori_loop(0, 4, step, 0, unroll=4)
    total = s_ref[...]
    s_ref[...] = jnp.log2(total)
    shift_ref[...] = jnp.zeros(shift_ref.shape, F32)

    @pl.when(jnp.min(total) < FLOOR2)
    def _():
        for half, q_ref in enumerate((qa_ref, qb_ref)):

            def shifted(k, carry, half=half, q_ref=q_ref):
                s = block(4 * half + k)
                m = jnp.max(s, axis=0, keepdims=True)
                q = jnp.exp2(s - m)
                q_ref[:, pl.ds(pl.multiple_of(k * chunk, chunk), chunk)] = q
                l = jnp.sum(q, axis=0, keepdims=True)
                s_ref[pl.ds(4 * half + k, 1), :] = m + jnp.log2(l)
                shift_ref[pl.ds(4 * half + k, 1), :] = m
                return carry

            lax.fori_loop(0, 4, shifted, 0)

    for p in range(Z):
        out_ref[p] = s_ref[...]


def mid_kernel(
    cols_ref, qa_ref, qb_ref, shift_ref, base_ref, out_ref, scale_ref, log_ref, acc_ref, o_ref
):
    chunk = log_ref.shape[1]
    parts = [cols_ref[z] for z in range(Z)]
    peak = functools.reduce(jnp.maximum, parts)
    total = functools.reduce(jnp.add, [jnp.exp2(v - peak) for v in parts])
    log_col = peak + jnp.log2(total)
    log_ref[...] = log_col
    scale_ref[...] = shift_ref[...] - log_col
    acc_ref[...] = jnp.zeros(acc_ref.shape, F32)

    for half, q_ref in enumerate((qa_ref, qb_ref)):

        def step(k, carry, half=half, q_ref=q_ref):
            log_mass = base_ref[5:6, pl.ds(pl.multiple_of((4 * half + k) * chunk, chunk), chunk)]
            w = jnp.exp2(log_mass + scale_ref[pl.ds(4 * half + k, 1), :])
            q = q_ref[:, pl.ds(pl.multiple_of(k * chunk, chunk), chunk)]
            acc_ref[...] += fold(q * w, jnp.add)
            return carry

        lax.fori_loop(0, 4, step, 0)
    scale_ref[...] = jnp.exp2(scale_ref[...])
    set_tile(o_ref, jnp.sum(jnp.transpose(acc_ref[...]), axis=0, keepdims=True))
    for p in range(out_ref.shape[0]):
        out_ref[p] = o_ref[...]


def last_kernel(ratio_ref, qa_ref, qb_ref, src_ref, scale_ref, out_ref, pot_ref, r_ref, s_ref):
    chunk = s_ref.shape[1]
    ratio = ratio_ref[0]
    for p in range(1, ratio_ref.shape[0]):
        ratio = ratio + ratio_ref[p]
    ratio = row_of(ratio)
    mass = src_ref[1:2, :]
    r_ref[...] = jnp.transpose(jnp.broadcast_to(mass / ratio, (128, ratio.shape[1])))
    s_ref[0:1, :] = LN2 * (src_ref[0:1, :] - jnp.log2(ratio))
    rows = pot_ref.shape[1]
    mine = pl.multiple_of(lax.axis_index("x") * rows, rows)
    pot_ref[...] = s_ref[0:1, pl.ds(mine, rows)]
    tile = 256

    for half, q_ref in enumerate((qa_ref, qb_ref)):

        def step(k, carry, half=half, q_ref=q_ref):
            cols = pl.ds(pl.multiple_of(k * chunk, chunk), chunk)

            def inner(g, acc):
                here = pl.ds(pl.multiple_of(g * tile, tile), tile)
                r = r_ref[here, :]
                q = q_ref[here, cols]
                out = []
                for j in range(0, chunk, 128):
                    v = q[:, j : j + 128] * r
                    a = acc[:, j : j + 128]
                    for h in range(0, tile, 8):
                        a = a + v[h : h + 8]
                    out.append(a)
                return jnp.concatenate(out, axis=1)

            acc = lax.fori_loop(0, r_ref.shape[0] // tile, inner, jnp.zeros((8, chunk), F32))
            s_ref[pl.ds(4 * half + k, 1), :] = jnp.sum(acc, axis=0, keepdims=True)
            return carry

        lax.fori_loop(0, 4, step, 0)
    row = lax.broadcasted_iota(jnp.int32, (8, 128), 0)
    extra = jnp.where(row == 0, jnp.sum(mass), jnp.sum(ratio))
    sums = s_ref[...] * scale_ref[...]
    for p in range(Z):
        out_ref[p, :, 0:chunk] = sums
        out_ref[p, :, chunk : chunk + 128] = extra


def end_kernel(cols_ref, log_ref, pot_ref, out_ref, src_ref, o_ref):
    chunk = log_ref.shape[1]
    total = cols_ref[0]
    for z in range(1, Z):
        total = total + cols_ref[z]
    sums = jnp.log(total[:, chunk : chunk + 128])
    log_src, log_tgt = sums[0:1, 0:1], sums[1:2, 0:1]
    src_ref[...] = pot_ref[...] + (2.0 * log_tgt - log_src)
    pot = -LN2 * (jnp.log2(total[:, 0:chunk]) + log_ref[...]) + 2.0 * (log_src - log_tgt)
    per = chunk // 128
    for k in range(8):
        for s in range(per):
            o_ref[per * k + s : per * k + s + 1, :] = pot[k : k + 1, 128 * s : 128 * s + 128]
    for p in range(X):
        out_ref[p] = o_ref[...]


def kernel_call(body, out_shape, scratch, args, space=pltpu.VMEM, megabytes=8):
    vmem = pl.BlockSpec(memory_space=pltpu.VMEM)
    return pl.pallas_call(
        body,
        out_shape=[
            jax.ShapeDtypeStruct(s, F32) if isinstance(s, tuple) else s for s in out_shape
        ],
        in_specs=[pl.BlockSpec(memory_space=space)] * len(args),
        out_specs=[vmem] * len(out_shape),
        scratch_shapes=scratch,
        compiler_params=pltpu.CompilerParams(vmem_limit_bytes=megabytes * 2**20),
    )(*args)


def trade(v, axes):
    return lax.all_to_all(v, axes, 0, 0)


def on_device(src_points, tgt_points, src_mass, tgt_mass):
    rows = src_points.shape[1]
    cols = tgt_points.shape[1]
    nsrc = rows * X
    ntgt = cols // X
    chunk = ntgt // 8

    first, base = kernel_call(
        row_kernel,
        [(GROUP, 8, 128), (8, ntgt)],
        [
            pltpu.VMEM((3, rows), F32),
            pltpu.VMEM((1, rows), F32),
            pltpu.VMEM((3, cols), F32),
            pltpu.VMEM((1, cols), F32),
            pltpu.SemaphoreType.DMA((4,)),
            pltpu.VMEM((8, rows), F32),
            pltpu.VMEM((8, cols), F32),
            pltpu.VMEM((48, cols), BF16),
            pltpu.VMEM((8, 128), F32),
        ],
        [
            pltpu.with_memory_space_constraint(v, pltpu.HBM)
            for v in (src_points, src_mass.reshape(1, rows), tgt_points, tgt_mass.reshape(1, cols))
        ],
        space=pltpu.HBM,
        megabytes=40,
    )
    first = trade(first, ("x", "y", "c"))
    half = pltpu.VMEM((nsrc, ntgt // 2), F32)
    *q, logs, shift, src_rows = kernel_call(
        col_kernel,
        [half, half, (Z, 8, chunk), (8, chunk), (8, nsrc)],
        [
            pltpu.VMEM((8, nsrc), F32),
            pltpu.VMEM((8, ntgt), F32),
            pltpu.VMEM((48, ntgt), BF16),
            pltpu.VMEM((8, chunk), F32),
        ],
        (first, base),
    )
    q = [pltpu.with_memory_space_constraint(v, pltpu.VMEM) for v in q]
    logs = trade(logs, "z")
    ratio, scale, log_col = kernel_call(
        mid_kernel,
        [(GROUP, 8, 128), (8, chunk), (8, chunk)],
        [pltpu.VMEM((nsrc, 128), F32), pltpu.VMEM((8, 128), F32)],
        (logs, *q, shift, base),
        megabytes=4,
    )
    ratio = trade(ratio, ("x", "y", "c"))
    col_sums, pot = kernel_call(
        last_kernel,
        [(Z, 8, chunk + 128), (1, rows)],
        [pltpu.VMEM((nsrc, 128), F32), pltpu.VMEM((8, chunk), F32)],
        (ratio, *q, src_rows, scale),
        megabytes=4,
    )
    col_sums = trade(col_sums, "z")
    tgt_pot, src_pot = kernel_call(
        end_kernel,
        [(X, ntgt // 128, 128), (1, rows)],
        [pltpu.VMEM((ntgt // 128, 128), F32)],
        (col_sums, log_col, pot),
        megabytes=4,
    )
    return (src_pot.reshape(rows), trade(tgt_pot, "x").reshape(cols))


def solution(mesh):
    fine = Mesh(mesh.devices.reshape(Z, X, Y, C), ("z", "x", "y", "c"))
    row, col = ("z", "x"), ("y", "c")
    placed = (P(None, row), P(None, col), P(row), P(col))
    return jax.shard_map(
        on_device, mesh=fine, in_specs=placed, out_specs=(P(row), P(col)), check_vma=False
    )
```

```python
import functools
import math

import jax
import jax.numpy as jnp
from jax import lax
from jax.experimental import pallas as pl
from jax.experimental.pallas import tpu as pltpu
from jax.sharding import Mesh, PartitionSpec as P

EPSILON = 0.01
LN2 = math.log(2.0)
SCALE = 1.0 / (EPSILON * LN2)
CENTER = 0.5
FLOOR1 = 2.0**-60
FLOOR2 = 2.0**-40
BF16 = jnp.bfloat16
F32 = jnp.float32

Z, X, Y, C = 8, 4, 4, 2
NCOL = Y * C
GROUP = X * NCOL


def pieces(v):
    p1 = v.astype(BF16).astype(F32)
    r = v - p1
    p2 = r.astype(BF16).astype(F32)
    p3 = (r - p2).astype(BF16).astype(F32)
    return p1, p2, p3


def stack_src(v):
    p1, p2, p3 = pieces(v)
    return [
        jnp.concatenate([p1, p2], axis=0),
        jnp.concatenate([p3, p1], axis=0),
        jnp.concatenate([p2, p1], axis=0),
    ]


def stack_tgt(v):
    p1, p2, p3 = pieces(v)
    return [
        jnp.concatenate([p1, p1], axis=0),
        jnp.concatenate([p1, p2], axis=0),
        jnp.concatenate([p2, p3], axis=0),
    ]


def scores(lhs, rhs):
    return lax.dot_general(
        lhs, rhs, (((1,), (0,)), ((), ())), preferred_element_type=F32
    )


def fold(v, op):
    out = v[:, 0:128]
    for k in range(128, v.shape[1], 128):
        out = op(out, v[:, k : k + 128])
    return out


def norm_rows(ref):
    a, b, c = ref[0:1, :], ref[1:2, :], ref[2:3, :]
    return -SCALE * (a * a + b * b + c * c)


def src_side(x_ref):
    n = x_ref.shape[1]
    x_ref[0:3, :] = x_ref[0:3, :] - CENTER
    x_ref[4:5, :] = x_ref[4:5, :] + norm_rows(x_ref)
    x_ref[0:3, :] = x_ref[0:3, :] * (2.0 * SCALE)
    x_ref[3:4, :] = jnp.ones((1, n), F32)
    x_ref[5:8, :] = jnp.zeros((3, n), F32)
    stacked = jnp.concatenate(stack_src(x_ref[...]), axis=0)
    return jnp.transpose(stacked).astype(BF16)


def tgt_side(t_ref, w_ref, lanes):
    for k, part in enumerate(stack_tgt(t_ref[:, lanes])):
        w_ref[16 * k : 16 * k + 16, lanes] = part.astype(BF16)


def row_of(tile):
    return jnp.concatenate([tile[s : s + 1, :] for s in range(tile.shape[0])], axis=1)


def set_tile(ref, row):
    for s in range(row.shape[1] // 128):
        ref[s : s + 1, :] = row[:, 128 * s : 128 * s + 128]


def row_kernel(
    src_hbm,
    src_mass_hbm,
    tgt_hbm,
    mass_hbm,
    out_ref,
    base_ref,
    src_ref,
    src_mass_ref,
    tgt_ref,
    mass_ref,
    sem,
    x_ref,
    t_ref,
    w_ref,
    o_ref,
):
    n = tgt_ref.shape[1]
    rows = src_ref.shape[1]
    chunk = n // 4
    quarters = [slice(k * chunk, (k + 1) * chunk) for k in range(4)]
    pairs = [(src_hbm, src_ref), (src_mass_hbm, src_mass_ref)]
    for lanes in quarters:
        pairs += [(tgt_hbm.at[:, lanes], tgt_ref.at[:, lanes])]
        pairs += [(mass_hbm.at[:, lanes], mass_ref.at[:, lanes])]
    moves = [pltpu.make_async_copy(a, b, sem.at[i]) for i, (a, b) in enumerate(pairs)]
    for move in moves:
        move.start()
    moves[0].wait()
    x_ref[0:3, :] = src_ref[...]
    x_ref[4:5, :] = jnp.zeros((1, rows), F32)
    lhs = src_side(x_ref)
    for move in moves[1:4]:
        move.wait()

    acc = jnp.zeros((rows, 128), F32)
    for k, lanes in enumerate(quarters):
        if k == 1:
            for move in moves[4:]:
                move.wait()
        points = tgt_ref[:, lanes] - CENTER
        t_ref[0:3, lanes] = points
        log_mass = jnp.log2(mass_ref[:, lanes])
        norm = -SCALE * jnp.sum(points * points, axis=0, keepdims=True)
        t_ref[3:4, lanes] = norm + log_mass
        t_ref[4:5, lanes] = jnp.ones((1, chunk), F32)
        t_ref[5:6, lanes] = log_mass
        t_ref[6:8, lanes] = jnp.zeros((2, chunk), F32)
        tgt_side(t_ref, w_ref, lanes)
        acc = acc + fold(jnp.exp2(scores(lhs, w_ref[:, lanes])), jnp.add)
    total = jnp.sum(jnp.transpose(acc), axis=0, keepdims=True)
    o_ref[...] = jnp.zeros((8, 128), F32)
    set_tile(o_ref, jnp.log2(total))

    @pl.when(jnp.min(total) < FLOOR1)
    def _():
        small = 1024

        def block(k):
            return scores(lhs, w_ref[:, pl.ds(pl.multiple_of(k * small, small), small)])

        def top(k, m):
            return jnp.maximum(m, fold(block(k), jnp.maximum))

        m = lax.fori_loop(0, n // small, top, jnp.full((rows, 128), -jnp.inf, F32))
        m = jnp.max(m, axis=1, keepdims=True)

        def shifted(k, acc):
            return acc + fold(jnp.exp2(block(k) - m), jnp.add)

        acc = lax.fori_loop(0, n // small, shifted, jnp.zeros((rows, 128), F32))
        total = jnp.sum(jnp.transpose(acc), axis=0, keepdims=True)
        peak = jnp.transpose(jnp.broadcast_to(m, (rows, 128)))[0:1, :]
        set_tile(o_ref, jnp.log2(total) + peak)

    col = lax.axis_index("y") * C + lax.axis_index("c")
    info = src_mass_ref[...]
    for d in range(3):
        info = jnp.where(col == d, src_ref[d : d + 1, :], info)
    for s in range(rows // 128):
        o_ref[2 + s : 3 + s, :] = info[:, 128 * s : 128 * s + 128]
    for p in range(out_ref.shape[0]):
        out_ref[p] = o_ref[...]
    share = base_ref.shape[1]
    base_ref[...] = t_ref[:, pl.ds(pl.multiple_of(lax.axis_index("x") * share, share), share)]


def set_src(first_ref, x_ref):
    logs, masses = [], []
    for x in range(X):
        parts = [first_ref[x * NCOL + q] for q in range(NCOL)]
        peak = functools.reduce(jnp.maximum, parts)
        total = functools.reduce(jnp.add, [jnp.exp2(v - peak) for v in parts])
        log_sum = peak + jnp.log2(total)
        for s in range(2):
            lanes = slice(256 * x + 128 * s, 256 * x + 128 * s + 128)
            for d in range(3):
                x_ref[d : d + 1, lanes] = parts[d][2 + s : 3 + s, :]
            logs.append(log_sum[s : s + 1, :])
            masses.append(parts[3][2 + s : 3 + s, :])
    mass = jnp.concatenate(masses, axis=1)
    return jnp.log2(mass), mass, jnp.concatenate(logs, axis=1)


def col_kernel(
    first_ref, base_ref, qa_ref, qb_ref, out_ref, shift_ref, src_ref, x_ref, t_ref, w_ref, s_ref
):
    n = t_ref.shape[1]
    chunk = n // 8
    log_mass, mass, log_sum = set_src(first_ref, x_ref)
    src_ref[...] = jnp.zeros(src_ref.shape, F32)
    src_ref[0:1, :] = log_mass - log_sum
    src_ref[1:2, :] = mass
    x_ref[4:5, :] = log_mass - log_sum
    lhs = src_side(x_ref)
    t_ref[...] = base_ref[...]
    t_ref[3:4, :] = base_ref[3:4, :] - base_ref[5:6, :]
    tgt_side(t_ref, w_ref, slice(0, n))

    def block(k):
        return scores(lhs, w_ref[:, pl.ds(pl.multiple_of(k * chunk, chunk), chunk)])

    for half, q_ref in enumerate((qa_ref, qb_ref)):

        def step(k, carry, half=half, q_ref=q_ref):
            q = jnp.exp2(block(4 * half + k))
            q_ref[:, pl.ds(pl.multiple_of(k * chunk, chunk), chunk)] = q
            s_ref[pl.ds(4 * half + k, 1), :] = jnp.sum(q, axis=0, keepdims=True)
            return carry

        lax.fori_loop(0, 4, step, 0, unroll=4)
    total = s_ref[...]
    s_ref[...] = jnp.log2(total)
    shift_ref[...] = jnp.zeros(shift_ref.shape, F32)

    @pl.when(jnp.min(total) < FLOOR2)
    def _():
        for half, q_ref in enumerate((qa_ref, qb_ref)):

            def shifted(k, carry, half=half, q_ref=q_ref):
                s = block(4 * half + k)
                m = jnp.max(s, axis=0, keepdims=True)
                q = jnp.exp2(s - m)
                q_ref[:, pl.ds(pl.multiple_of(k * chunk, chunk), chunk)] = q
                l = jnp.sum(q, axis=0, keepdims=True)
                s_ref[pl.ds(4 * half + k, 1), :] = m + jnp.log2(l)
                shift_ref[pl.ds(4 * half + k, 1), :] = m
                return carry

            lax.fori_loop(0, 4, shifted, 0)

    for p in range(Z):
        out_ref[p] = s_ref[...]


def mid_kernel(
    cols_ref, qa_ref, qb_ref, shift_ref, base_ref, out_ref, scale_ref, log_ref, acc_ref, o_ref
):
    chunk = log_ref.shape[1]
    parts = [cols_ref[z] for z in range(Z)]
    peak = functools.reduce(jnp.maximum, parts)
    total = functools.reduce(jnp.add, [jnp.exp2(v - peak) for v in parts])
    log_col = peak + jnp.log2(total)
    log_ref[...] = log_col
    scale_ref[...] = shift_ref[...] - log_col
    acc_ref[...] = jnp.zeros(acc_ref.shape, F32)

    for half, q_ref in enumerate((qa_ref, qb_ref)):

        def step(k, carry, half=half, q_ref=q_ref):
            log_mass = base_ref[5:6, pl.ds(pl.multiple_of((4 * half + k) * chunk, chunk), chunk)]
            w = jnp.exp2(log_mass + scale_ref[pl.ds(4 * half + k, 1), :])
            q = q_ref[:, pl.ds(pl.multiple_of(k * chunk, chunk), chunk)]
            acc_ref[...] += fold(q * w, jnp.add)
            return carry

        lax.fori_loop(0, 4, step, 0)
    scale_ref[...] = jnp.exp2(scale_ref[...])
    set_tile(o_ref, jnp.sum(jnp.transpose(acc_ref[...]), axis=0, keepdims=True))
    for p in range(out_ref.shape[0]):
        out_ref[p] = o_ref[...]


def last_kernel(ratio_ref, qa_ref, qb_ref, src_ref, scale_ref, out_ref, pot_ref, r_ref, s_ref):
    chunk = s_ref.shape[1]
    ratio = ratio_ref[0]
    for p in range(1, ratio_ref.shape[0]):
        ratio = ratio + ratio_ref[p]
    ratio = row_of(ratio)
    mass = src_ref[1:2, :]
    r_ref[...] = jnp.transpose(jnp.broadcast_to(mass / ratio, (128, ratio.shape[1])))
    s_ref[0:1, :] = LN2 * (src_ref[0:1, :] - jnp.log2(ratio))
    rows = pot_ref.shape[1]
    mine = pl.multiple_of(lax.axis_index("x") * rows, rows)
    pot_ref[...] = s_ref[0:1, pl.ds(mine, rows)]
    for half, q_ref in enumerate((qa_ref, qb_ref)):

        def step(k, carry, half=half, q_ref=q_ref):
            cols = pl.ds(pl.multiple_of(k * chunk, chunk), chunk)
            accs = [jnp.zeros((8, 128), F32)] * (chunk // 128)
            for h in range(0, r_ref.shape[0], 8):
                r = r_ref[h : h + 8, :]
                q = q_ref[h : h + 8, cols]
                for j in range(chunk // 128):
                    accs[j] = accs[j] + q[:, 128 * j : 128 * j + 128] * r
            acc = jnp.concatenate(accs, axis=1)
            s_ref[pl.ds(4 * half + k, 1), :] = jnp.sum(acc, axis=0, keepdims=True)
            return carry

        lax.fori_loop(0, 4, step, 0)
    row = lax.broadcasted_iota(jnp.int32, (8, 128), 0)
    extra = jnp.where(row == 0, jnp.sum(mass), jnp.sum(ratio))
    sums = s_ref[...] * scale_ref[...]
    for p in range(Z):
        out_ref[p, :, 0:chunk] = sums
        out_ref[p, :, chunk : chunk + 128] = extra


def end_kernel(cols_ref, log_ref, pot_ref, out_ref, src_ref):
    chunk = log_ref.shape[1]
    total = cols_ref[0]
    for z in range(1, Z):
        total = total + cols_ref[z]
    sums = jnp.log(total[:, chunk : chunk + 128])
    log_src, log_tgt = sums[0:1, 0:1], sums[1:2, 0:1]
    src_ref[...] = pot_ref[...] + (2.0 * log_tgt - log_src)
    pot = -LN2 * (jnp.log2(total[:, 0:chunk]) + log_ref[...]) + 2.0 * (log_src - log_tgt)
    per = chunk // 128
    for k in range(8):
        for s in range(per):
            out_ref[per * k + s : per * k + s + 1, :] = pot[k : k + 1, 128 * s : 128 * s + 128]


def place_kernel(*refs):
    *pieces, out_ref, sem = refs
    size = pieces[0].shape[0]
    moves = []
    for s, piece in enumerate(pieces):
        start = pl.multiple_of(lax.rem(lax.axis_index("x") + X - s, X) * size, size)
        moves.append(pltpu.make_async_copy(piece, out_ref.at[pl.ds(start, size), :], sem.at[s]))
        moves[-1].start()
    for move in moves:
        move.wait()


def kernel_call(body, out_shape, scratch, args, space=pltpu.VMEM, megabytes=8):
    vmem = pl.BlockSpec(memory_space=pltpu.VMEM)
    return pl.pallas_call(
        body,
        out_shape=[
            jax.ShapeDtypeStruct(s, F32) if isinstance(s, tuple) else s for s in out_shape
        ],
        in_specs=[pl.BlockSpec(memory_space=space)] * len(args),
        out_specs=[vmem] * len(out_shape),
        scratch_shapes=scratch,
        compiler_params=pltpu.CompilerParams(vmem_limit_bytes=megabytes * 2**20),
    )(*args)


def trade(v, axes):
    return lax.all_to_all(v, axes, 0, 0)


def on_device(src_points, tgt_points, src_mass, tgt_mass):
    rows = src_points.shape[1]
    cols = tgt_points.shape[1]
    nsrc = rows * X
    ntgt = cols // X
    chunk = ntgt // 8

    first, base = kernel_call(
        row_kernel,
        [(GROUP, 8, 128), (8, ntgt)],
        [
            pltpu.VMEM((3, rows), F32),
            pltpu.VMEM((1, rows), F32),
            pltpu.VMEM((3, cols), F32),
            pltpu.VMEM((1, cols), F32),
            pltpu.SemaphoreType.DMA((10,)),
            pltpu.VMEM((8, rows), F32),
            pltpu.VMEM((8, cols), F32),
            pltpu.VMEM((48, cols), BF16),
            pltpu.VMEM((8, 128), F32),
        ],
        [
            pltpu.with_memory_space_constraint(v, pltpu.HBM)
            for v in (src_points, src_mass.reshape(1, rows), tgt_points, tgt_mass.reshape(1, cols))
        ],
        space=pltpu.HBM,
        megabytes=40,
    )
    first = trade(first, ("x", "y", "c"))
    half = pltpu.VMEM((nsrc, ntgt // 2), F32)
    *q, logs, shift, src_rows = kernel_call(
        col_kernel,
        [half, half, (Z, 8, chunk), (8, chunk), (8, nsrc)],
        [
            pltpu.VMEM((8, nsrc), F32),
            pltpu.VMEM((8, ntgt), F32),
            pltpu.VMEM((48, ntgt), BF16),
            pltpu.VMEM((8, chunk), F32),
        ],
        (first, base),
    )
    q = [pltpu.with_memory_space_constraint(v, pltpu.VMEM) for v in q]
    logs = trade(logs, "z")
    ratio, scale, log_col = kernel_call(
        mid_kernel,
        [(GROUP, 8, 128), (8, chunk), (8, chunk)],
        [pltpu.VMEM((nsrc, 128), F32), pltpu.VMEM((8, 128), F32)],
        (logs, *q, shift, base),
        megabytes=4,
    )
    ratio = trade(ratio, ("x", "y", "c"))
    col_sums, pot = kernel_call(
        last_kernel,
        [(Z, 8, chunk + 128), (1, rows)],
        [pltpu.VMEM((nsrc, 128), F32), pltpu.VMEM((8, chunk), F32)],
        (ratio, *q, src_rows, scale),
        megabytes=4,
    )
    col_sums = trade(col_sums, "z")
    tgt_pot, src_pot = kernel_call(
        end_kernel,
        [(ntgt // 128, 128), (1, rows)],
        [],
        (col_sums, log_col, pot),
        megabytes=4,
    )
    pieces = [tgt_pot]
    for s in range(1, X):
        pieces.append(lax.ppermute(tgt_pot, "x", [(x, (x + s) % X) for x in range(X)]))
    anywhere = pl.BlockSpec(memory_space=pl.ANY)
    tgt_pot = pl.pallas_call(
        place_kernel,
        out_shape=pltpu.HBM((cols // 128, 128), F32),
        in_specs=[anywhere] * X,
        out_specs=anywhere,
        scratch_shapes=[pltpu.SemaphoreType.DMA((X,))],
    )(*pieces)
    return (src_pot.reshape(rows), tgt_pot.reshape(cols))


def solution(mesh):
    fine = Mesh(mesh.devices.reshape(Z, X, Y, C), ("z", "x", "y", "c"))
    row, col = ("z", "x"), ("y", "c")
    placed = (P(None, row), P(None, col), P(row), P(col))
    return jax.shard_map(
        on_device, mesh=fine, in_specs=placed, out_specs=(P(row), P(col)), check_vma=False
    )
```

```python
import functools
import math

import jax
import jax.numpy as jnp
from jax import lax
from jax.experimental import pallas as pl
from jax.experimental.pallas import tpu as pltpu
from jax.sharding import Mesh, PartitionSpec as P

EPSILON = 0.01
LN2 = math.log(2.0)
SCALE = 1.0 / (EPSILON * LN2)
CENTER = 0.5
FLOOR1 = 2.0**-60
FLOOR2 = 2.0**-40
BF16 = jnp.bfloat16
F32 = jnp.float32

Z, X, Y, C = 8, 4, 4, 2
NCOL = Y * C
GROUP = X * NCOL


def pieces(v):
    p1 = v.astype(BF16).astype(F32)
    r = v - p1
    p2 = r.astype(BF16).astype(F32)
    p3 = (r - p2).astype(BF16).astype(F32)
    return p1, p2, p3


def stack_src(v):
    p1, p2, p3 = pieces(v)
    return [
        jnp.concatenate([p1, p2], axis=0),
        jnp.concatenate([p3, p1], axis=0),
        jnp.concatenate([p2, p1], axis=0),
    ]


def stack_tgt(v):
    p1, p2, p3 = pieces(v)
    return [
        jnp.concatenate([p1, p1], axis=0),
        jnp.concatenate([p1, p2], axis=0),
        jnp.concatenate([p2, p3], axis=0),
    ]


def scores(lhs, rhs):
    return lax.dot_general(
        lhs, rhs, (((1,), (0,)), ((), ())), preferred_element_type=F32
    )


def fold(v, op):
    out = v[:, 0:128]
    for k in range(128, v.shape[1], 128):
        out = op(out, v[:, k : k + 128])
    return out


def norm_rows(ref):
    a, b, c = ref[0:1, :], ref[1:2, :], ref[2:3, :]
    return -SCALE * (a * a + b * b + c * c)


def src_side(x_ref):
    n = x_ref.shape[1]
    x_ref[0:3, :] = x_ref[0:3, :] - CENTER
    x_ref[4:5, :] = x_ref[4:5, :] + norm_rows(x_ref)
    x_ref[0:3, :] = x_ref[0:3, :] * (2.0 * SCALE)
    x_ref[3:4, :] = jnp.ones((1, n), F32)
    x_ref[5:8, :] = jnp.zeros((3, n), F32)
    stacked = jnp.concatenate(stack_src(x_ref[...]), axis=0)
    return jnp.transpose(stacked).astype(BF16)


def tgt_side(t_ref, w_ref, lanes):
    for k, part in enumerate(stack_tgt(t_ref[:, lanes])):
        w_ref[16 * k : 16 * k + 16, lanes] = part.astype(BF16)


def row_of(tile):
    return jnp.concatenate([tile[s : s + 1, :] for s in range(tile.shape[0])], axis=1)


def set_tile(ref, row):
    for s in range(row.shape[1] // 128):
        ref[s : s + 1, :] = row[:, 128 * s : 128 * s + 128]


def row_kernel(
    src_hbm,
    src_mass_hbm,
    tgt_hbm,
    mass_hbm,
    out_ref,
    base_ref,
    src_ref,
    src_mass_ref,
    tgt_ref,
    mass_ref,
    sem,
    x_ref,
    t_ref,
    w_ref,
    o_ref,
):
    n = tgt_ref.shape[1]
    rows = src_ref.shape[1]
    chunk = n // 4
    quarters = [slice(k * chunk, (k + 1) * chunk) for k in range(4)]
    pairs = [(src_hbm, src_ref), (src_mass_hbm, src_mass_ref)]
    for lanes in quarters:
        pairs += [(tgt_hbm.at[:, lanes], tgt_ref.at[:, lanes])]
        pairs += [(mass_hbm.at[:, lanes], mass_ref.at[:, lanes])]
    moves = [pltpu.make_async_copy(a, b, sem.at[i]) for i, (a, b) in enumerate(pairs)]
    for move in moves:
        move.start()
    moves[0].wait()
    x_ref[0:3, :] = src_ref[...]
    x_ref[4:5, :] = jnp.zeros((1, rows), F32)
    lhs = src_side(x_ref)
    for move in moves[1:4]:
        move.wait()

    acc = jnp.zeros((rows, 128), F32)
    for k, lanes in enumerate(quarters):
        if k == 1:
            for move in moves[4:]:
                move.wait()
        points = tgt_ref[:, lanes] - CENTER
        t_ref[0:3, lanes] = points
        log_mass = jnp.log2(mass_ref[:, lanes])
        norm = -SCALE * jnp.sum(points * points, axis=0, keepdims=True)
        t_ref[3:4, lanes] = norm + log_mass
        t_ref[4:5, lanes] = jnp.ones((1, chunk), F32)
        t_ref[5:6, lanes] = log_mass
        t_ref[6:8, lanes] = jnp.zeros((2, chunk), F32)
        tgt_side(t_ref, w_ref, lanes)
        acc = acc + fold(jnp.exp2(scores(lhs, w_ref[:, lanes])), jnp.add)
    total = jnp.sum(jnp.transpose(acc), axis=0, keepdims=True)
    o_ref[...] = jnp.zeros((8, 128), F32)
    set_tile(o_ref, jnp.log2(total))

    @pl.when(jnp.min(total) < FLOOR1)
    def _():
        small = 1024

        def block(k):
            return scores(lhs, w_ref[:, pl.ds(pl.multiple_of(k * small, small), small)])

        def top(k, m):
            return jnp.maximum(m, fold(block(k), jnp.maximum))

        m = lax.fori_loop(0, n // small, top, jnp.full((rows, 128), -jnp.inf, F32))
        m = jnp.max(m, axis=1, keepdims=True)

        def shifted(k, acc):
            return acc + fold(jnp.exp2(block(k) - m), jnp.add)

        acc = lax.fori_loop(0, n // small, shifted, jnp.zeros((rows, 128), F32))
        total = jnp.sum(jnp.transpose(acc), axis=0, keepdims=True)
        peak = jnp.transpose(jnp.broadcast_to(m, (rows, 128)))[0:1, :]
        set_tile(o_ref, jnp.log2(total) + peak)

    col = lax.axis_index("y") * C + lax.axis_index("c")
    info = src_mass_ref[...]
    for d in range(3):
        info = jnp.where(col == d, src_ref[d : d + 1, :], info)
    for s in range(rows // 128):
        o_ref[2 + s : 3 + s, :] = info[:, 128 * s : 128 * s + 128]
    for p in range(out_ref.shape[0]):
        out_ref[p] = o_ref[...]
    share = base_ref.shape[1]
    base_ref[...] = t_ref[:, pl.ds(pl.multiple_of(lax.axis_index("x") * share, share), share)]


def set_src(first_ref, x_ref):
    logs, masses = [], []
    for x in range(X):
        parts = [first_ref[x * NCOL + q] for q in range(NCOL)]
        peak = functools.reduce(jnp.maximum, parts)
        total = functools.reduce(jnp.add, [jnp.exp2(v - peak) for v in parts])
        log_sum = peak + jnp.log2(total)
        for s in range(2):
            lanes = slice(256 * x + 128 * s, 256 * x + 128 * s + 128)
            for d in range(3):
                x_ref[d : d + 1, lanes] = parts[d][2 + s : 3 + s, :]
            logs.append(log_sum[s : s + 1, :])
            masses.append(parts[3][2 + s : 3 + s, :])
    mass = jnp.concatenate(masses, axis=1)
    return jnp.log2(mass), mass, jnp.concatenate(logs, axis=1)


def col_kernel(
    first_ref, base_ref, qa_ref, qb_ref, out_ref, shift_ref, src_ref, x_ref, t_ref, w_ref, s_ref
):
    n = t_ref.shape[1]
    chunk = n // 8
    log_mass, mass, log_sum = set_src(first_ref, x_ref)
    src_ref[...] = jnp.zeros(src_ref.shape, F32)
    src_ref[0:1, :] = log_mass - log_sum
    src_ref[1:2, :] = mass
    x_ref[4:5, :] = log_mass - log_sum
    lhs = src_side(x_ref)
    t_ref[...] = base_ref[...]
    t_ref[3:4, :] = base_ref[3:4, :] - base_ref[5:6, :]
    tgt_side(t_ref, w_ref, slice(0, n))

    def block(k):
        return scores(lhs, w_ref[:, pl.ds(pl.multiple_of(k * chunk, chunk), chunk)])

    for half, q_ref in enumerate((qa_ref, qb_ref)):

        def step(k, carry, half=half, q_ref=q_ref):
            q = jnp.exp2(block(4 * half + k))
            q_ref[:, pl.ds(pl.multiple_of(k * chunk, chunk), chunk)] = q
            s_ref[pl.ds(4 * half + k, 1), :] = jnp.sum(q, axis=0, keepdims=True)
            return carry

        lax.fori_loop(0, 4, step, 0, unroll=4)
    total = s_ref[...]
    s_ref[...] = jnp.log2(total)
    shift_ref[...] = jnp.zeros(shift_ref.shape, F32)

    @pl.when(jnp.min(total) < FLOOR2)
    def _():
        for half, q_ref in enumerate((qa_ref, qb_ref)):

            def shifted(k, carry, half=half, q_ref=q_ref):
                s = block(4 * half + k)
                m = jnp.max(s, axis=0, keepdims=True)
                q = jnp.exp2(s - m)
                q_ref[:, pl.ds(pl.multiple_of(k * chunk, chunk), chunk)] = q
                l = jnp.sum(q, axis=0, keepdims=True)
                s_ref[pl.ds(4 * half + k, 1), :] = m + jnp.log2(l)
                shift_ref[pl.ds(4 * half + k, 1), :] = m
                return carry

            lax.fori_loop(0, 4, shifted, 0)

    for p in range(Z):
        out_ref[p] = s_ref[...]


def mid_kernel(
    cols_ref, qa_ref, qb_ref, shift_ref, base_ref, out_ref, scale_ref, log_ref, acc_ref, o_ref
):
    chunk = log_ref.shape[1]
    parts = [cols_ref[z] for z in range(Z)]
    peak = functools.reduce(jnp.maximum, parts)
    total = functools.reduce(jnp.add, [jnp.exp2(v - peak) for v in parts])
    log_col = peak + jnp.log2(total)
    log_ref[...] = log_col
    scale_ref[...] = shift_ref[...] - log_col
    acc_ref[...] = jnp.zeros(acc_ref.shape, F32)

    for half, q_ref in enumerate((qa_ref, qb_ref)):

        def step(k, carry, half=half, q_ref=q_ref):
            log_mass = base_ref[5:6, pl.ds(pl.multiple_of((4 * half + k) * chunk, chunk), chunk)]
            w = jnp.exp2(log_mass + scale_ref[pl.ds(4 * half + k, 1), :])
            q = q_ref[:, pl.ds(pl.multiple_of(k * chunk, chunk), chunk)]
            acc_ref[...] += fold(q * w, jnp.add)
            return carry

        lax.fori_loop(0, 4, step, 0)
    scale_ref[...] = jnp.exp2(scale_ref[...])
    set_tile(o_ref, jnp.sum(jnp.transpose(acc_ref[...]), axis=0, keepdims=True))
    for p in range(out_ref.shape[0]):
        out_ref[p] = o_ref[...]


def last_kernel(ratio_ref, qa_ref, qb_ref, src_ref, scale_ref, out_ref, pot_ref, r_ref, s_ref):
    chunk = s_ref.shape[1]
    ratio = ratio_ref[0]
    for p in range(1, ratio_ref.shape[0]):
        ratio = ratio + ratio_ref[p]
    ratio = row_of(ratio)
    mass = src_ref[1:2, :]
    r_ref[...] = jnp.transpose(jnp.broadcast_to(mass / ratio, (128, ratio.shape[1])))
    s_ref[0:1, :] = LN2 * (src_ref[0:1, :] - jnp.log2(ratio))
    rows = pot_ref.shape[1]
    mine = pl.multiple_of(lax.axis_index("x") * rows, rows)
    pot_ref[...] = s_ref[0:1, pl.ds(mine, rows)]
    for half, q_ref in enumerate((qa_ref, qb_ref)):

        def step(k, carry, half=half, q_ref=q_ref):
            cols = pl.ds(pl.multiple_of(k * chunk, chunk), chunk)
            accs = [jnp.zeros((8, 128), F32)] * (chunk // 128)
            for h in range(0, r_ref.shape[0], 8):
                r = r_ref[h : h + 8, :]
                q = q_ref[h : h + 8, cols]
                for j in range(chunk // 128):
                    accs[j] = accs[j] + q[:, 128 * j : 128 * j + 128] * r
            acc = jnp.concatenate(accs, axis=1)
            s_ref[pl.ds(4 * half + k, 1), :] = jnp.sum(acc, axis=0, keepdims=True)
            return carry

        lax.fori_loop(0, 4, step, 0)
    row = lax.broadcasted_iota(jnp.int32, (8, 128), 0)
    extra = jnp.where(row == 0, jnp.sum(mass), jnp.sum(ratio))
    sums = s_ref[...] * scale_ref[...]
    for p in range(Z):
        out_ref[p, :, 0:chunk] = sums
        out_ref[p, :, chunk : chunk + 128] = extra


def end_kernel(cols_ref, log_ref, pot_ref, out_ref, src_ref):
    chunk = log_ref.shape[1]
    total = cols_ref[0]
    for z in range(1, Z):
        total = total + cols_ref[z]
    sums = jnp.log(total[:, chunk : chunk + 128])
    log_src, log_tgt = sums[0:1, 0:1], sums[1:2, 0:1]
    src_ref[...] = pot_ref[...] + (2.0 * log_tgt - log_src)
    pot = -LN2 * (jnp.log2(total[:, 0:chunk]) + log_ref[...]) + 2.0 * (log_src - log_tgt)
    per = chunk // 128
    for k in range(8):
        for s in range(per):
            out_ref[per * k + s : per * k + s + 1, :] = pot[k : k + 1, 128 * s : 128 * s + 128]


def place_kernel(*refs):
    *pieces, out_ref, sem = refs
    size = pieces[0].shape[0]
    moves = []
    for s, piece in enumerate(pieces):
        start = pl.multiple_of(lax.rem(lax.axis_index("x") + X - s, X) * size, size)
        moves.append(pltpu.make_async_copy(piece, out_ref.at[pl.ds(start, size), :], sem.at[s]))
        moves[-1].start()
    for move in moves:
        move.wait()


def kernel_call(body, out_shape, scratch, args, space=pltpu.VMEM, megabytes=8):
    vmem = pl.BlockSpec(memory_space=pltpu.VMEM)
    return pl.pallas_call(
        body,
        out_shape=[
            jax.ShapeDtypeStruct(s, F32) if isinstance(s, tuple) else s for s in out_shape
        ],
        in_specs=[pl.BlockSpec(memory_space=space)] * len(args),
        out_specs=[vmem] * len(out_shape),
        scratch_shapes=scratch,
        compiler_params=pltpu.CompilerParams(vmem_limit_bytes=megabytes * 2**20),
    )(*args)


def trade(v, axes):
    return lax.all_to_all(v, axes, 0, 0)


def on_device(src_points, tgt_points, src_mass, tgt_mass):
    rows = src_points.shape[1]
    cols = tgt_points.shape[1]
    nsrc = rows * X
    ntgt = cols // X
    chunk = ntgt // 8

    first, base = kernel_call(
        row_kernel,
        [(GROUP, 8, 128), (8, ntgt)],
        [
            pltpu.VMEM((3, rows), F32),
            pltpu.VMEM((1, rows), F32),
            pltpu.VMEM((3, cols), F32),
            pltpu.VMEM((1, cols), F32),
            pltpu.SemaphoreType.DMA((10,)),
            pltpu.VMEM((8, rows), F32),
            pltpu.VMEM((8, cols), F32),
            pltpu.VMEM((48, cols), BF16),
            pltpu.VMEM((8, 128), F32),
        ],
        [
            pltpu.with_memory_space_constraint(v, pltpu.HBM)
            for v in (src_points, src_mass.reshape(1, rows), tgt_points, tgt_mass.reshape(1, cols))
        ],
        space=pltpu.HBM,
        megabytes=40,
    )
    first = trade(first, ("x", "y", "c"))
    half = pltpu.VMEM((nsrc, ntgt // 2), F32)
    *q, logs, shift, src_rows = kernel_call(
        col_kernel,
        [half, half, (Z, 8, chunk), (8, chunk), (8, nsrc)],
        [
            pltpu.VMEM((8, nsrc), F32),
            pltpu.VMEM((8, ntgt), F32),
            pltpu.VMEM((48, ntgt), BF16),
            pltpu.VMEM((8, chunk), F32),
        ],
        (first, base),
    )
    q = [pltpu.with_memory_space_constraint(v, pltpu.VMEM) for v in q]
    logs = trade(logs, "z")
    ratio, scale, log_col = kernel_call(
        mid_kernel,
        [(GROUP, 8, 128), (8, chunk), (8, chunk)],
        [pltpu.VMEM((nsrc, 128), F32), pltpu.VMEM((8, 128), F32)],
        (logs, *q, shift, base),
        megabytes=4,
    )
    ratio = trade(ratio, ("x", "y", "c"))
    col_sums, pot = kernel_call(
        last_kernel,
        [(Z, 8, chunk + 128), (1, rows)],
        [pltpu.VMEM((nsrc, 128), F32), pltpu.VMEM((8, chunk), F32)],
        (ratio, *q, src_rows, scale),
        megabytes=4,
    )
    col_sums = trade(col_sums, "z")
    tgt_pot, src_pot = kernel_call(
        end_kernel,
        [(ntgt // 128, 128), (1, rows)],
        [],
        (col_sums, log_col, pot),
        megabytes=4,
    )
    pieces = [tgt_pot]
    for s in range(1, X):
        pieces.append(lax.ppermute(tgt_pot, "x", [(x, (x + s) % X) for x in range(X)]))
    tgt_pot = pl.pallas_call(
        place_kernel,
        out_shape=pltpu.HBM((cols // 128, 128), F32),
        in_specs=[pl.BlockSpec(memory_space=pltpu.VMEM)] * X,
        out_specs=pl.BlockSpec(memory_space=pltpu.HBM),
        scratch_shapes=[pltpu.SemaphoreType.DMA((X,))],
    )(*pieces)
    return (src_pot.reshape(rows), tgt_pot.reshape(cols))


def solution(mesh):
    fine = Mesh(mesh.devices.reshape(Z, X, Y, C), ("z", "x", "y", "c"))
    row, col = ("z", "x"), ("y", "c")
    placed = (P(None, row), P(None, col), P(row), P(col))
    return jax.shard_map(
        on_device, mesh=fine, in_specs=placed, out_specs=(P(row), P(col)), check_vma=False
    )
```

```python
import functools
import math

import jax
import jax.numpy as jnp
from jax import lax
from jax.experimental import pallas as pl
from jax.experimental.pallas import tpu as pltpu
from jax.sharding import Mesh, PartitionSpec as P

EPSILON = 0.01
LN2 = math.log(2.0)
SCALE = 1.0 / (EPSILON * LN2)
CENTER = 0.5
FLOOR1 = 2.0**-60
FLOOR2 = 2.0**-40
BF16 = jnp.bfloat16
F32 = jnp.float32

Z, X, Y, C = 8, 4, 4, 2
NCOL = Y * C
GROUP = X * NCOL


def pieces(v):
    p1 = v.astype(BF16).astype(F32)
    r = v - p1
    p2 = r.astype(BF16).astype(F32)
    p3 = (r - p2).astype(BF16).astype(F32)
    return p1, p2, p3


def stack_src(v):
    p1, p2, p3 = pieces(v)
    return [
        jnp.concatenate([p1, p2], axis=0),
        jnp.concatenate([p3, p1], axis=0),
        jnp.concatenate([p2, p1], axis=0),
    ]


def stack_tgt(v):
    p1, p2, p3 = pieces(v)
    return [
        jnp.concatenate([p1, p1], axis=0),
        jnp.concatenate([p1, p2], axis=0),
        jnp.concatenate([p2, p3], axis=0),
    ]


def scores(lhs, rhs):
    return lax.dot_general(
        lhs, rhs, (((1,), (0,)), ((), ())), preferred_element_type=F32
    )


def fold(v, op):
    out = v[:, 0:128]
    for k in range(128, v.shape[1], 128):
        out = op(out, v[:, k : k + 128])
    return out


def src_side(x_ref, use_mass):
    n = x_ref.shape[1]
    x_ref[0:3, :] = x_ref[0:3, :] - CENTER
    a, b, c = x_ref[0:1, :], x_ref[1:2, :], x_ref[2:3, :]
    x_ref[3:4, :] = x_ref[3:4, :] - SCALE * (a * a + b * b + c * c)
    x_ref[0:3, :] = x_ref[0:3, :] * (2.0 * SCALE)
    x_ref[4:7, :] = jnp.ones((3, n), F32)
    x_ref[7:8, :] = jnp.full((1, n), use_mass, F32)
    stacked = jnp.concatenate(stack_src(x_ref[...]), axis=0)
    return jnp.transpose(stacked).astype(BF16)


def row_of(tile):
    return jnp.concatenate([tile[s : s + 1, :] for s in range(tile.shape[0])], axis=1)


def set_tile(ref, row):
    for s in range(row.shape[1] // 128):
        ref[s : s + 1, :] = row[:, 128 * s : 128 * s + 128]


def row_kernel(
    src_hbm,
    src_mass_hbm,
    tgt_hbm,
    mass_hbm,
    out_ref,
    share_ref,
    log_ref,
    src_ref,
    src_mass_ref,
    tgt_ref,
    mass_ref,
    sem,
    x_ref,
    t_ref,
    w_ref,
    o_ref,
):
    n = tgt_ref.shape[1]
    rows = src_ref.shape[1]
    moves = [
        pltpu.make_async_copy(a, b, sem.at[i])
        for i, (a, b) in enumerate(
            [
                (src_hbm, src_ref),
                (src_mass_hbm, src_mass_ref),
                (tgt_hbm, tgt_ref),
                (mass_hbm, mass_ref),
            ]
        )
    ]
    for move in moves:
        move.start()
    moves[0].wait()
    x_ref[0:3, :] = src_ref[...]
    x_ref[3:4, :] = jnp.zeros((1, rows), F32)
    lhs = src_side(x_ref, 1.0)
    for move in moves[1:]:
        move.wait()
    points = tgt_ref[...] - CENTER
    t_ref[0:3, :] = points
    t_ref[3:4, :] = jnp.ones((1, n), F32)
    t_ref[4:7, :] = points * points * -SCALE
    t_ref[7:8, :] = jnp.log2(mass_ref[...])
    for k, part in enumerate(stack_tgt(t_ref[...])):
        w_ref[16 * k : 16 * k + 16, :] = part.astype(BF16)
    acc = fold(jnp.exp2(scores(lhs, w_ref[...])), jnp.add)
    total = jnp.sum(jnp.transpose(acc), axis=0, keepdims=True)
    o_ref[...] = jnp.zeros((8, 128), F32)
    set_tile(o_ref, jnp.log2(total))

    @pl.when(jnp.min(total) < FLOOR1)
    def _():
        small = 1024

        def block(k):
            return scores(lhs, w_ref[:, pl.ds(pl.multiple_of(k * small, small), small)])

        def top(k, m):
            return jnp.maximum(m, fold(block(k), jnp.maximum))

        m = lax.fori_loop(0, n // small, top, jnp.full((rows, 128), -jnp.inf, F32))
        m = jnp.max(m, axis=1, keepdims=True)

        def shifted(k, acc):
            return acc + fold(jnp.exp2(block(k) - m), jnp.add)

        acc = lax.fori_loop(0, n // small, shifted, jnp.zeros((rows, 128), F32))
        total = jnp.sum(jnp.transpose(acc), axis=0, keepdims=True)
        peak = jnp.transpose(jnp.broadcast_to(m, (rows, 128)))[0:1, :]
        set_tile(o_ref, jnp.log2(total) + peak)

    col = lax.axis_index("y") * C + lax.axis_index("c")
    info = src_mass_ref[...]
    for d in range(3):
        info = jnp.where(col == d, src_ref[d : d + 1, :], info)
    for s in range(rows // 128):
        o_ref[2 + s : 3 + s, :] = info[:, 128 * s : 128 * s + 128]
    for p in range(out_ref.shape[0]):
        out_ref[p] = o_ref[...]
    share = share_ref.shape[1]
    mine = pl.ds(pl.multiple_of(lax.axis_index("x") * share, share), share)
    share_ref[...] = w_ref[:, mine]
    log_ref[...] = t_ref[7:8, mine]


def set_src(first_ref, x_ref):
    logs, masses = [], []
    for x in range(X):
        parts = [first_ref[x * NCOL + q] for q in range(NCOL)]
        peak = functools.reduce(jnp.maximum, parts)
        total = functools.reduce(jnp.add, [jnp.exp2(v - peak) for v in parts])
        log_sum = peak + jnp.log2(total)
        for s in range(2):
            lanes = slice(256 * x + 128 * s, 256 * x + 128 * s + 128)
            for d in range(3):
                x_ref[d : d + 1, lanes] = parts[d][2 + s : 3 + s, :]
            logs.append(log_sum[s : s + 1, :])
            masses.append(parts[3][2 + s : 3 + s, :])
    mass = jnp.concatenate(masses, axis=1)
    return jnp.log2(mass), mass, jnp.concatenate(logs, axis=1)


def col_kernel(
    first_ref, w_ref, qa_ref, qb_ref, out_ref, shift_ref, src_ref, x_ref, s_ref
):
    chunk = s_ref.shape[1]
    log_mass, mass, log_sum = set_src(first_ref, x_ref)
    src_ref[...] = jnp.zeros(src_ref.shape, F32)
    src_ref[0:1, :] = log_mass - log_sum
    src_ref[1:2, :] = mass
    x_ref[3:4, :] = log_mass - log_sum
    lhs = src_side(x_ref, 0.0)

    def block(k):
        return scores(lhs, w_ref[:, pl.ds(pl.multiple_of(k * chunk, chunk), chunk)])

    for half, q_ref in enumerate((qa_ref, qb_ref)):

        def step(k, carry, half=half, q_ref=q_ref):
            q = jnp.exp2(block(4 * half + k))
            q_ref[:, pl.ds(pl.multiple_of(k * chunk, chunk), chunk)] = q
            s_ref[pl.ds(4 * half + k, 1), :] = jnp.sum(q, axis=0, keepdims=True)
            return carry

        lax.fori_loop(0, 4, step, 0, unroll=4)
    total = s_ref[...]
    s_ref[...] = jnp.log2(total)
    shift_ref[...] = jnp.zeros(shift_ref.shape, F32)

    @pl.when(jnp.min(total) < FLOOR2)
    def _():
        for half, q_ref in enumerate((qa_ref, qb_ref)):

            def shifted(k, carry, half=half, q_ref=q_ref):
                s = block(4 * half + k)
                m = jnp.max(s, axis=0, keepdims=True)
                q = jnp.exp2(s - m)
                q_ref[:, pl.ds(pl.multiple_of(k * chunk, chunk), chunk)] = q
                l = jnp.sum(q, axis=0, keepdims=True)
                s_ref[pl.ds(4 * half + k, 1), :] = m + jnp.log2(l)
                shift_ref[pl.ds(4 * half + k, 1), :] = m
                return carry

            lax.fori_loop(0, 4, shifted, 0)

    for p in range(Z):
        out_ref[p] = s_ref[...]


def mid_kernel(
    cols_ref, qa_ref, qb_ref, shift_ref, mass_ref, out_ref, scale_ref, log_ref, acc_ref, o_ref
):
    chunk = log_ref.shape[1]
    parts = [cols_ref[z] for z in range(Z)]
    peak = functools.reduce(jnp.maximum, parts)
    total = functools.reduce(jnp.add, [jnp.exp2(v - peak) for v in parts])
    log_col = peak + jnp.log2(total)
    log_ref[...] = log_col
    scale_ref[...] = shift_ref[...] - log_col
    acc_ref[...] = jnp.zeros(acc_ref.shape, F32)

    for half, q_ref in enumerate((qa_ref, qb_ref)):

        def step(k, carry, half=half, q_ref=q_ref):
            log_mass = mass_ref[:, pl.ds(pl.multiple_of((4 * half + k) * chunk, chunk), chunk)]
            w = jnp.exp2(log_mass + scale_ref[pl.ds(4 * half + k, 1), :])
            q = q_ref[:, pl.ds(pl.multiple_of(k * chunk, chunk), chunk)]
            acc_ref[...] += fold(q * w, jnp.add)
            return carry

        lax.fori_loop(0, 4, step, 0)
    scale_ref[...] = jnp.exp2(scale_ref[...])
    set_tile(o_ref, jnp.sum(jnp.transpose(acc_ref[...]), axis=0, keepdims=True))
    for p in range(out_ref.shape[0]):
        out_ref[p] = o_ref[...]


def last_kernel(ratio_ref, qa_ref, qb_ref, src_ref, scale_ref, out_ref, pot_ref, r_ref, s_ref):
    chunk = s_ref.shape[1]
    ratio = ratio_ref[0]
    for p in range(1, ratio_ref.shape[0]):
        ratio = ratio + ratio_ref[p]
    ratio = row_of(ratio)
    mass = src_ref[1:2, :]
    r_ref[...] = jnp.transpose(jnp.broadcast_to(mass / ratio, (128, ratio.shape[1])))
    s_ref[0:1, :] = LN2 * (src_ref[0:1, :] - jnp.log2(ratio))
    rows = pot_ref.shape[1]
    mine = pl.multiple_of(lax.axis_index("x") * rows, rows)
    pot_ref[...] = s_ref[0:1, pl.ds(mine, rows)]
    for half, q_ref in enumerate((qa_ref, qb_ref)):

        def step(k, carry, half=half, q_ref=q_ref):
            cols = pl.ds(pl.multiple_of(k * chunk, chunk), chunk)
            accs = [jnp.zeros((8, 128), F32)] * (chunk // 128)
            for h in range(0, r_ref.shape[0], 8):
                r = r_ref[h : h + 8, :]
                q = q_ref[h : h + 8, cols]
                for j in range(chunk // 128):
                    accs[j] = accs[j] + q[:, 128 * j : 128 * j + 128] * r
            acc = jnp.concatenate(accs, axis=1)
            s_ref[pl.ds(4 * half + k, 1), :] = jnp.sum(acc, axis=0, keepdims=True)
            return carry

        lax.fori_loop(0, 4, step, 0)
    row = lax.broadcasted_iota(jnp.int32, (8, 128), 0)
    extra = jnp.where(row == 0, jnp.sum(mass), jnp.sum(ratio))
    sums = s_ref[...] * scale_ref[...]
    for p in range(Z):
        out_ref[p, :, 0:chunk] = sums
        out_ref[p, :, chunk : chunk + 128] = extra


def end_kernel(cols_ref, log_ref, pot_ref, out_ref, src_ref, o_ref):
    chunk = log_ref.shape[1]
    total = cols_ref[0]
    for z in range(1, Z):
        total = total + cols_ref[z]
    sums = jnp.log(total[:, chunk : chunk + 128])
    log_src, log_tgt = sums[0:1, 0:1], sums[1:2, 0:1]
    src_ref[...] = pot_ref[...] + (2.0 * log_tgt - log_src)
    pot = -LN2 * (jnp.log2(total[:, 0:chunk]) + log_ref[...]) + 2.0 * (log_src - log_tgt)
    per = chunk // 128
    for k in range(8):
        for s in range(per):
            o_ref[per * k + s : per * k + s + 1, :] = pot[k : k + 1, 128 * s : 128 * s + 128]
    for p in range(X):
        out_ref[p] = o_ref[...]


def kernel_call(body, out_shape, scratch, args, space=pltpu.VMEM, megabytes=8):
    vmem = pl.BlockSpec(memory_space=pltpu.VMEM)
    return pl.pallas_call(
        body,
        out_shape=[
            jax.ShapeDtypeStruct(s, F32) if isinstance(s, tuple) else s for s in out_shape
        ],
        in_specs=[pl.BlockSpec(memory_space=space)] * len(args),
        out_specs=[vmem] * len(out_shape),
        scratch_shapes=scratch,
        compiler_params=pltpu.CompilerParams(vmem_limit_bytes=megabytes * 2**20),
    )(*args)


def trade(v, axes):
    return lax.all_to_all(v, axes, 0, 0)


def on_device(src_points, tgt_points, src_mass, tgt_mass):
    rows = src_points.shape[1]
    cols = tgt_points.shape[1]
    nsrc = rows * X
    ntgt = cols // X
    chunk = ntgt // 8

    first, share, log_mass = kernel_call(
        row_kernel,
        [(GROUP, 8, 128), jax.ShapeDtypeStruct((48, ntgt), BF16), (1, ntgt)],
        [
            pltpu.VMEM((3, rows), F32),
            pltpu.VMEM((1, rows), F32),
            pltpu.VMEM((3, cols), F32),
            pltpu.VMEM((1, cols), F32),
            pltpu.SemaphoreType.DMA((4,)),
            pltpu.VMEM((8, rows), F32),
            pltpu.VMEM((8, cols), F32),
            pltpu.VMEM((48, cols), BF16),
            pltpu.VMEM((8, 128), F32),
        ],
        [
            pltpu.with_memory_space_constraint(v, pltpu.HBM)
            for v in (src_points, src_mass.reshape(1, rows), tgt_points, tgt_mass.reshape(1, cols))
        ],
        space=pltpu.HBM,
        megabytes=50,
    )
    first = trade(first, ("x", "y", "c"))
    half = pltpu.VMEM((nsrc, ntgt // 2), F32)
    *q, logs, shift, src_rows = kernel_call(
        col_kernel,
        [half, half, (Z, 8, chunk), (8, chunk), (8, nsrc)],
        [
            pltpu.VMEM((8, nsrc), F32),
            pltpu.VMEM((8, chunk), F32),
        ],
        (first, share),
    )
    q = [pltpu.with_memory_space_constraint(v, pltpu.VMEM) for v in q]
    logs = trade(logs, "z")
    ratio, scale, log_col = kernel_call(
        mid_kernel,
        [(GROUP, 8, 128), (8, chunk), (8, chunk)],
        [pltpu.VMEM((nsrc, 128), F32), pltpu.VMEM((8, 128), F32)],
        (logs, *q, shift, log_mass),
        megabytes=4,
    )
    ratio = trade(ratio, ("x", "y", "c"))
    col_sums, pot = kernel_call(
        last_kernel,
        [(Z, 8, chunk + 128), (1, rows)],
        [pltpu.VMEM((nsrc, 128), F32), pltpu.VMEM((8, chunk), F32)],
        (ratio, *q, src_rows, scale),
        megabytes=4,
    )
    col_sums = trade(col_sums, "z")
    tgt_pot, src_pot = kernel_call(
        end_kernel,
        [(X, ntgt // 128, 128), (1, rows)],
        [pltpu.VMEM((ntgt // 128, 128), F32)],
        (col_sums, log_col, pot),
        megabytes=4,
    )
    return (src_pot.reshape(rows), trade(tgt_pot, "x").reshape(cols))


def solution(mesh):
    fine = Mesh(mesh.devices.reshape(Z, X, Y, C), ("z", "x", "y", "c"))
    row, col = ("z", "x"), ("y", "c")
    placed = (P(None, row), P(None, col), P(row), P(col))
    return jax.shard_map(
        on_device, mesh=fine, in_specs=placed, out_specs=(P(row), P(col)), check_vma=False
    )
```

```python
import functools
import math

import jax
import jax.numpy as jnp
from jax import lax
from jax.experimental import pallas as pl
from jax.experimental.pallas import tpu as pltpu
from jax.sharding import Mesh, PartitionSpec as P

EPSILON = 0.01
LN2 = math.log(2.0)
SCALE = 1.0 / (EPSILON * LN2)
CENTER = 0.5
FLOOR1 = 2.0**-60
FLOOR2 = 2.0**-40
BF16 = jnp.bfloat16
F32 = jnp.float32

Z, X, Y, C = 8, 4, 4, 2
NCOL = Y * C
GROUP = X * NCOL


def pieces(v):
    p1 = v.astype(BF16).astype(F32)
    r = v - p1
    p2 = r.astype(BF16).astype(F32)
    p3 = (r - p2).astype(BF16).astype(F32)
    return p1, p2, p3


def stack_src(v):
    p1, p2, p3 = pieces(v)
    return [
        jnp.concatenate([p1, p2], axis=0),
        jnp.concatenate([p3, p1], axis=0),
        jnp.concatenate([p2, p1], axis=0),
    ]


def stack_tgt(v):
    p1, p2, p3 = pieces(v)
    return [
        jnp.concatenate([p1, p1], axis=0),
        jnp.concatenate([p1, p2], axis=0),
        jnp.concatenate([p2, p3], axis=0),
    ]


def scores(lhs, rhs):
    return lax.dot_general(
        lhs, rhs, (((1,), (0,)), ((), ())), preferred_element_type=F32
    )


def fold(v, op):
    out = v[:, 0:128]
    for k in range(128, v.shape[1], 128):
        out = op(out, v[:, k : k + 128])
    return out


def src_side(x_ref, use_mass):
    n = x_ref.shape[1]
    x_ref[0:3, :] = x_ref[0:3, :] - CENTER
    a, b, c = x_ref[0:1, :], x_ref[1:2, :], x_ref[2:3, :]
    x_ref[3:4, :] = x_ref[3:4, :] - SCALE * (a * a + b * b + c * c)
    x_ref[0:3, :] = x_ref[0:3, :] * (2.0 * SCALE)
    x_ref[4:7, :] = jnp.ones((3, n), F32)
    x_ref[7:8, :] = jnp.full((1, n), use_mass, F32)
    stacked = jnp.concatenate(stack_src(x_ref[...]), axis=0)
    return jnp.transpose(stacked).astype(BF16)


def row_of(tile):
    return jnp.concatenate([tile[s : s + 1, :] for s in range(tile.shape[0])], axis=1)


def set_tile(ref, row):
    for s in range(row.shape[1] // 128):
        ref[s : s + 1, :] = row[:, 128 * s : 128 * s + 128]


def row_kernel(
    src_hbm,
    src_mass_hbm,
    tgt_hbm,
    mass_hbm,
    out_ref,
    share_ref,
    log_ref,
    src_ref,
    src_mass_ref,
    tgt_ref,
    mass_ref,
    sem,
    x_ref,
    t_ref,
    w_ref,
    o_ref,
):
    n = tgt_ref.shape[1]
    rows = src_ref.shape[1]
    moves = [
        pltpu.make_async_copy(a, b, sem.at[i])
        for i, (a, b) in enumerate(
            [
                (src_hbm, src_ref),
                (src_mass_hbm, src_mass_ref),
                (tgt_hbm, tgt_ref),
                (mass_hbm, mass_ref),
            ]
        )
    ]
    for move in moves:
        move.start()
    moves[0].wait()
    x_ref[0:3, :] = src_ref[...]
    x_ref[3:4, :] = jnp.zeros((1, rows), F32)
    lhs = src_side(x_ref, 1.0)
    for move in moves[1:]:
        move.wait()
    points = tgt_ref[...] - CENTER
    t_ref[0:3, :] = points
    t_ref[3:4, :] = jnp.ones((1, n), F32)
    t_ref[4:7, :] = points * points * -SCALE
    t_ref[7:8, :] = jnp.log2(mass_ref[...])
    for k, part in enumerate(stack_tgt(t_ref[...])):
        w_ref[16 * k : 16 * k + 16, :] = part.astype(BF16)
    acc = fold(jnp.exp2(scores(lhs, w_ref[...])), jnp.add)
    total = jnp.sum(jnp.transpose(acc), axis=0, keepdims=True)
    o_ref[...] = jnp.zeros((8, 128), F32)
    set_tile(o_ref, jnp.log2(total))
    low = jnp.min(total)
    col = lax.axis_index("y") * C + lax.axis_index("c")
    info = src_mass_ref[...]
    for d in range(3):
        info = jnp.where(col == d, src_ref[d : d + 1, :], info)
    for s in range(rows // 128):
        o_ref[2 + s : 3 + s, :] = info[:, 128 * s : 128 * s + 128]
    for p in range(out_ref.shape[0]):
        out_ref[p] = o_ref[...]
    share = share_ref.shape[1]
    mine = pl.ds(pl.multiple_of(lax.axis_index("x") * share, share), share)
    share_ref[...] = w_ref[:, mine]
    log_ref[...] = t_ref[7:8, mine]

    @pl.when(low < FLOOR1)
    def _():
        small = 1024

        def block(k):
            return scores(lhs, w_ref[:, pl.ds(pl.multiple_of(k * small, small), small)])

        def top(k, m):
            return jnp.maximum(m, fold(block(k), jnp.maximum))

        m = lax.fori_loop(0, n // small, top, jnp.full((rows, 128), -jnp.inf, F32))
        m = jnp.max(m, axis=1, keepdims=True)

        def shifted(k, acc):
            return acc + fold(jnp.exp2(block(k) - m), jnp.add)

        acc = lax.fori_loop(0, n // small, shifted, jnp.zeros((rows, 128), F32))
        total = jnp.sum(jnp.transpose(acc), axis=0, keepdims=True)
        peak = jnp.transpose(jnp.broadcast_to(m, (rows, 128)))[0:1, :]
        set_tile(o_ref, jnp.log2(total) + peak)
        for p in range(out_ref.shape[0]):
            out_ref[p] = o_ref[...]


def set_src(first_ref, x_ref):
    logs, masses = [], []
    for x in range(X):
        parts = [first_ref[x * NCOL + q] for q in range(NCOL)]
        peak = functools.reduce(jnp.maximum, parts)
        total = functools.reduce(jnp.add, [jnp.exp2(v - peak) for v in parts])
        log_sum = peak + jnp.log2(total)
        for s in range(2):
            lanes = slice(256 * x + 128 * s, 256 * x + 128 * s + 128)
            for d in range(3):
                x_ref[d : d + 1, lanes] = parts[d][2 + s : 3 + s, :]
            logs.append(log_sum[s : s + 1, :])
            masses.append(parts[3][2 + s : 3 + s, :])
    mass = jnp.concatenate(masses, axis=1)
    return jnp.log2(mass), mass, jnp.concatenate(logs, axis=1)


def col_kernel(
    first_ref, w_ref, qa_ref, qb_ref, out_ref, shift_ref, src_ref, x_ref, s_ref
):
    chunk = s_ref.shape[1]
    log_mass, mass, log_sum = set_src(first_ref, x_ref)
    src_ref[...] = jnp.zeros(src_ref.shape, F32)
    src_ref[0:1, :] = log_mass - log_sum
    src_ref[1:2, :] = mass
    x_ref[3:4, :] = log_mass - log_sum
    lhs = src_side(x_ref, 0.0)

    def block(k):
        return scores(lhs, w_ref[:, pl.ds(pl.multiple_of(k * chunk, chunk), chunk)])

    for half, q_ref in enumerate((qa_ref, qb_ref)):

        def step(k, carry, half=half, q_ref=q_ref):
            q = jnp.exp2(block(4 * half + k))
            q_ref[:, pl.ds(pl.multiple_of(k * chunk, chunk), chunk)] = q
            s_ref[pl.ds(4 * half + k, 1), :] = jnp.sum(q, axis=0, keepdims=True)
            return carry

        lax.fori_loop(0, 4, step, 0, unroll=4)
    total = s_ref[...]
    low = jnp.min(total)
    for p in range(Z):
        out_ref[p] = jnp.log2(total)
    shift_ref[...] = jnp.zeros(shift_ref.shape, F32)

    @pl.when(low < FLOOR2)
    def _():
        for half, q_ref in enumerate((qa_ref, qb_ref)):

            def shifted(k, carry, half=half, q_ref=q_ref):
                s = block(4 * half + k)
                m = jnp.max(s, axis=0, keepdims=True)
                q = jnp.exp2(s - m)
                q_ref[:, pl.ds(pl.multiple_of(k * chunk, chunk), chunk)] = q
                l = jnp.sum(q, axis=0, keepdims=True)
                s_ref[pl.ds(4 * half + k, 1), :] = m + jnp.log2(l)
                shift_ref[pl.ds(4 * half + k, 1), :] = m
                return carry

            lax.fori_loop(0, 4, shifted, 0)
        for p in range(Z):
            out_ref[p] = s_ref[...]


def mid_kernel(
    cols_ref, qa_ref, qb_ref, shift_ref, mass_ref, out_ref, scale_ref, log_ref, acc_ref, o_ref
):
    chunk = log_ref.shape[1]
    parts = [cols_ref[z] for z in range(Z)]
    peak = functools.reduce(jnp.maximum, parts)
    total = functools.reduce(jnp.add, [jnp.exp2(v - peak) for v in parts])
    log_col = peak + jnp.log2(total)
    log_ref[...] = log_col
    scale_ref[...] = shift_ref[...] - log_col
    acc_ref[...] = jnp.zeros(acc_ref.shape, F32)

    for half, q_ref in enumerate((qa_ref, qb_ref)):

        def step(k, carry, half=half, q_ref=q_ref):
            log_mass = mass_ref[:, pl.ds(pl.multiple_of((4 * half + k) * chunk, chunk), chunk)]
            w = jnp.exp2(log_mass + scale_ref[pl.ds(4 * half + k, 1), :])
            q = q_ref[:, pl.ds(pl.multiple_of(k * chunk, chunk), chunk)]
            acc_ref[...] += fold(q * w, jnp.add)
            return carry

        lax.fori_loop(0, 4, step, 0)
    scale_ref[...] = jnp.exp2(scale_ref[...])
    set_tile(o_ref, jnp.sum(jnp.transpose(acc_ref[...]), axis=0, keepdims=True))
    for p in range(out_ref.shape[0]):
        out_ref[p] = o_ref[...]


def last_kernel(ratio_ref, qa_ref, qb_ref, src_ref, scale_ref, out_ref, pot_ref, r_ref, s_ref):
    chunk = s_ref.shape[1]
    ratio = ratio_ref[0]
    for p in range(1, ratio_ref.shape[0]):
        ratio = ratio + ratio_ref[p]
    ratio = row_of(ratio)
    mass = src_ref[1:2, :]
    r_ref[...] = jnp.transpose(jnp.broadcast_to(mass / ratio, (128, ratio.shape[1])))
    s_ref[0:1, :] = LN2 * (src_ref[0:1, :] - jnp.log2(ratio))
    rows = pot_ref.shape[1]
    mine = pl.multiple_of(lax.axis_index("x") * rows, rows)
    pot_ref[...] = s_ref[0:1, pl.ds(mine, rows)]
    for half, q_ref in enumerate((qa_ref, qb_ref)):

        def step(k, carry, half=half, q_ref=q_ref):
            cols = pl.ds(pl.multiple_of(k * chunk, chunk), chunk)
            accs = [jnp.zeros((8, 128), F32)] * (chunk // 128)
            for h in range(0, r_ref.shape[0], 8):
                r = r_ref[h : h + 8, :]
                q = q_ref[h : h + 8, cols]
                for j in range(chunk // 128):
                    accs[j] = accs[j] + q[:, 128 * j : 128 * j + 128] * r
            acc = jnp.concatenate(accs, axis=1)
            s_ref[pl.ds(4 * half + k, 1), :] = jnp.sum(acc, axis=0, keepdims=True)
            return carry

        lax.fori_loop(0, 4, step, 0)
    row = lax.broadcasted_iota(jnp.int32, (8, 128), 0)
    extra = jnp.where(row == 0, jnp.sum(mass), jnp.sum(ratio))
    sums = s_ref[...] * scale_ref[...]
    for p in range(Z):
        out_ref[p, :, 0:chunk] = sums
        out_ref[p, :, chunk : chunk + 128] = extra


def end_kernel(cols_ref, log_ref, pot_ref, out_ref, src_ref, o_ref):
    chunk = log_ref.shape[1]
    total = cols_ref[0]
    for z in range(1, Z):
        total = total + cols_ref[z]
    sums = jnp.log(total[:, chunk : chunk + 128])
    log_src, log_tgt = sums[0:1, 0:1], sums[1:2, 0:1]
    src_ref[...] = pot_ref[...] + (2.0 * log_tgt - log_src)
    pot = -LN2 * (jnp.log2(total[:, 0:chunk]) + log_ref[...]) + 2.0 * (log_src - log_tgt)
    per = chunk // 128
    for k in range(8):
        for s in range(per):
            o_ref[per * k + s : per * k + s + 1, :] = pot[k : k + 1, 128 * s : 128 * s + 128]
    for p in range(X):
        out_ref[p] = o_ref[...]


def kernel_call(body, out_shape, scratch, args, space=pltpu.VMEM, megabytes=8):
    vmem = pl.BlockSpec(memory_space=pltpu.VMEM)
    return pl.pallas_call(
        body,
        out_shape=[
            jax.ShapeDtypeStruct(s, F32) if isinstance(s, tuple) else s for s in out_shape
        ],
        in_specs=[pl.BlockSpec(memory_space=space)] * len(args),
        out_specs=[vmem] * len(out_shape),
        scratch_shapes=scratch,
        compiler_params=pltpu.CompilerParams(vmem_limit_bytes=megabytes * 2**20),
    )(*args)


def trade(v, axes):
    return lax.all_to_all(v, axes, 0, 0)


def on_device(src_points, tgt_points, src_mass, tgt_mass):
    rows = src_points.shape[1]
    cols = tgt_points.shape[1]
    nsrc = rows * X
    ntgt = cols // X
    chunk = ntgt // 8

    first, share, log_mass = kernel_call(
        row_kernel,
        [(GROUP, 8, 128), jax.ShapeDtypeStruct((48, ntgt), BF16), (1, ntgt)],
        [
            pltpu.VMEM((3, rows), F32),
            pltpu.VMEM((1, rows), F32),
            pltpu.VMEM((3, cols), F32),
            pltpu.VMEM((1, cols), F32),
            pltpu.SemaphoreType.DMA((4,)),
            pltpu.VMEM((8, rows), F32),
            pltpu.VMEM((8, cols), F32),
            pltpu.VMEM((48, cols), BF16),
            pltpu.VMEM((8, 128), F32),
        ],
        [
            pltpu.with_memory_space_constraint(v, pltpu.HBM)
            for v in (src_points, src_mass.reshape(1, rows), tgt_points, tgt_mass.reshape(1, cols))
        ],
        space=pltpu.HBM,
        megabytes=50,
    )
    first = trade(first, ("x", "y", "c"))
    half = pltpu.VMEM((nsrc, ntgt // 2), F32)
    *q, logs, shift, src_rows = kernel_call(
        col_kernel,
        [half, half, (Z, 8, chunk), (8, chunk), (8, nsrc)],
        [
            pltpu.VMEM((8, nsrc), F32),
            pltpu.VMEM((8, chunk), F32),
        ],
        (first, share),
    )
    q = [pltpu.with_memory_space_constraint(v, pltpu.VMEM) for v in q]
    logs = trade(logs, "z")
    ratio, scale, log_col = kernel_call(
        mid_kernel,
        [(GROUP, 8, 128), (8, chunk), (8, chunk)],
        [pltpu.VMEM((nsrc, 128), F32), pltpu.VMEM((8, 128), F32)],
        (logs, *q, shift, log_mass),
        megabytes=4,
    )
    ratio = trade(ratio, ("x", "y", "c"))
    col_sums, pot = kernel_call(
        last_kernel,
        [(Z, 8, chunk + 128), (1, rows)],
        [pltpu.VMEM((nsrc, 128), F32), pltpu.VMEM((8, chunk), F32)],
        (ratio, *q, src_rows, scale),
        megabytes=4,
    )
    col_sums = trade(col_sums, "z")
    tgt_pot, src_pot = kernel_call(
        end_kernel,
        [(X, ntgt // 128, 128), (1, rows)],
        [pltpu.VMEM((ntgt // 128, 128), F32)],
        (col_sums, log_col, pot),
        megabytes=4,
    )
    return (src_pot.reshape(rows), trade(tgt_pot, "x").reshape(cols))


def solution(mesh):
    fine = Mesh(mesh.devices.reshape(Z, X, Y, C), ("z", "x", "y", "c"))
    row, col = ("z", "x"), ("y", "c")
    placed = (P(None, row), P(None, col), P(row), P(col))
    return jax.shard_map(
        on_device, mesh=fine, in_specs=placed, out_specs=(P(row), P(col)), check_vma=False
    )
```

```python
import functools
import math

import jax
import jax.numpy as jnp
from jax import lax
from jax.experimental import pallas as pl
from jax.experimental.pallas import tpu as pltpu
from jax.sharding import Mesh, PartitionSpec as P

EPSILON = 0.01
LN2 = math.log(2.0)
SCALE = 1.0 / (EPSILON * LN2)
CENTER = 0.5
FLOOR1 = 2.0**-60
FLOOR2 = 2.0**-40
BF16 = jnp.bfloat16
F32 = jnp.float32

Z, X, Y, C = 8, 4, 4, 2
NCOL = Y * C
GROUP = X * NCOL


def pieces(v):
    p1 = v.astype(BF16).astype(F32)
    r = v - p1
    p2 = r.astype(BF16).astype(F32)
    p3 = (r - p2).astype(BF16).astype(F32)
    return p1, p2, p3


def stack_src(v):
    p1, p2, p3 = pieces(v)
    return [
        jnp.concatenate([p1, p2], axis=0),
        jnp.concatenate([p3, p1], axis=0),
        jnp.concatenate([p2, p1], axis=0),
    ]


def stack_tgt(v):
    p1, p2, p3 = pieces(v)
    return [
        jnp.concatenate([p1, p1], axis=0),
        jnp.concatenate([p1, p2], axis=0),
        jnp.concatenate([p2, p3], axis=0),
    ]


def scores(lhs, rhs):
    return lax.dot_general(
        lhs, rhs, (((1,), (0,)), ((), ())), preferred_element_type=F32
    )


def fold(v, op):
    out = v[:, 0:128]
    for k in range(128, v.shape[1], 128):
        out = op(out, v[:, k : k + 128])
    return out


def src_side(x_ref, use_mass):
    n = x_ref.shape[1]
    x_ref[0:3, :] = x_ref[0:3, :] - CENTER
    a, b, c = x_ref[0:1, :], x_ref[1:2, :], x_ref[2:3, :]
    x_ref[3:4, :] = x_ref[3:4, :] - SCALE * (a * a + b * b + c * c)
    x_ref[0:3, :] = x_ref[0:3, :] * (2.0 * SCALE)
    x_ref[4:7, :] = jnp.ones((3, n), F32)
    x_ref[7:8, :] = jnp.full((1, n), use_mass, F32)
    stacked = jnp.concatenate(stack_src(x_ref[...]), axis=0)
    return jnp.transpose(stacked).astype(BF16)


def row_of(tile):
    return jnp.concatenate([tile[s : s + 1, :] for s in range(tile.shape[0])], axis=1)


def set_tile(ref, row):
    for s in range(row.shape[1] // 128):
        ref[s : s + 1, :] = row[:, 128 * s : 128 * s + 128]


def row_kernel(
    src_hbm,
    src_mass_hbm,
    tgt_hbm,
    mass_hbm,
    out_ref,
    share_ref,
    log_ref,
    src_ref,
    src_mass_ref,
    tgt_ref,
    mass_ref,
    sem,
    x_ref,
    t_ref,
    w_ref,
    o_ref,
):
    n = tgt_ref.shape[1]
    rows = src_ref.shape[1]
    moves = [
        pltpu.make_async_copy(a, b, sem.at[i])
        for i, (a, b) in enumerate(
            [
                (src_hbm, src_ref),
                (src_mass_hbm, src_mass_ref),
                (tgt_hbm, tgt_ref),
                (mass_hbm, mass_ref),
            ]
        )
    ]
    for move in moves:
        move.start()
    moves[0].wait()
    x_ref[0:3, :] = src_ref[...]
    x_ref[3:4, :] = jnp.zeros((1, rows), F32)
    lhs = src_side(x_ref, 1.0)
    for move in moves[1:]:
        move.wait()
    points = tgt_ref[...] - CENTER
    t_ref[0:3, :] = points
    t_ref[3:4, :] = jnp.ones((1, n), F32)
    t_ref[4:7, :] = points * points * -SCALE
    t_ref[7:8, :] = jnp.log2(mass_ref[...])
    for k, part in enumerate(stack_tgt(t_ref[...])):
        w_ref[16 * k : 16 * k + 16, :] = part.astype(BF16)
    acc = fold(jnp.exp2(scores(lhs, w_ref[...])), jnp.add)
    total = jnp.sum(jnp.transpose(acc), axis=0, keepdims=True)
    o_ref[...] = jnp.zeros((8, 128), F32)
    set_tile(o_ref, jnp.log2(total))

    @pl.when(jnp.min(total) < FLOOR1)
    def _():
        small = 1024

        def block(k):
            return scores(lhs, w_ref[:, pl.ds(pl.multiple_of(k * small, small), small)])

        def top(k, m):
            return jnp.maximum(m, fold(block(k), jnp.maximum))

        m = lax.fori_loop(0, n // small, top, jnp.full((rows, 128), -jnp.inf, F32))
        m = jnp.max(m, axis=1, keepdims=True)

        def shifted(k, acc):
            return acc + fold(jnp.exp2(block(k) - m), jnp.add)

        acc = lax.fori_loop(0, n // small, shifted, jnp.zeros((rows, 128), F32))
        total = jnp.sum(jnp.transpose(acc), axis=0, keepdims=True)
        peak = jnp.transpose(jnp.broadcast_to(m, (rows, 128)))[0:1, :]
        set_tile(o_ref, jnp.log2(total) + peak)

    col = lax.axis_index("y") * C + lax.axis_index("c")
    info = src_mass_ref[...]
    for d in range(3):
        info = jnp.where(col == d, src_ref[d : d + 1, :], info)
    for s in range(rows // 128):
        o_ref[2 + s : 3 + s, :] = info[:, 128 * s : 128 * s + 128]
    for p in range(out_ref.shape[0]):
        out_ref[p] = o_ref[...]
    share = share_ref.shape[1]
    mine = pl.ds(pl.multiple_of(lax.axis_index("x") * share, share), share)
    share_ref[...] = w_ref[:, mine]
    log_ref[...] = t_ref[7:8, mine]


def set_src(first_ref, x_ref):
    logs, masses = [], []
    for x in range(X):
        parts = [first_ref[x * NCOL + q] for q in range(NCOL)]
        peak = functools.reduce(jnp.maximum, parts)
        total = functools.reduce(jnp.add, [jnp.exp2(v - peak) for v in parts])
        log_sum = peak + jnp.log2(total)
        for s in range(2):
            lanes = slice(256 * x + 128 * s, 256 * x + 128 * s + 128)
            for d in range(3):
                x_ref[d : d + 1, lanes] = parts[d][2 + s : 3 + s, :]
            logs.append(log_sum[s : s + 1, :])
            masses.append(parts[3][2 + s : 3 + s, :])
    mass = jnp.concatenate(masses, axis=1)
    return jnp.log2(mass), mass, jnp.concatenate(logs, axis=1)


def col_kernel(
    first_ref, w_ref, qa_ref, qb_ref, out_ref, shift_ref, src_ref, x_ref, s_ref
):
    chunk = s_ref.shape[1]
    log_mass, mass, log_sum = set_src(first_ref, x_ref)
    src_ref[...] = jnp.zeros(src_ref.shape, F32)
    src_ref[0:1, :] = log_mass - log_sum
    src_ref[1:2, :] = mass
    x_ref[3:4, :] = log_mass - log_sum
    lhs = src_side(x_ref, 0.0)

    def block(k):
        return scores(lhs, w_ref[:, pl.ds(pl.multiple_of(k * chunk, chunk), chunk)])

    for half, q_ref in enumerate((qa_ref, qb_ref)):

        def step(k, carry, half=half, q_ref=q_ref):
            q = jnp.exp2(block(4 * half + k))
            q_ref[:, pl.ds(pl.multiple_of(k * chunk, chunk), chunk)] = q
            s_ref[pl.ds(4 * half + k, 1), :] = jnp.sum(q, axis=0, keepdims=True)
            return carry

        lax.fori_loop(0, 4, step, 0, unroll=4)
    total = s_ref[...]
    s_ref[...] = jnp.log2(total)
    shift_ref[...] = jnp.zeros(shift_ref.shape, F32)

    @pl.when(jnp.min(total) < FLOOR2)
    def _():
        for half, q_ref in enumerate((qa_ref, qb_ref)):

            def shifted(k, carry, half=half, q_ref=q_ref):
                s = block(4 * half + k)
                m = jnp.max(s, axis=0, keepdims=True)
                q = jnp.exp2(s - m)
                q_ref[:, pl.ds(pl.multiple_of(k * chunk, chunk), chunk)] = q
                l = jnp.sum(q, axis=0, keepdims=True)
                s_ref[pl.ds(4 * half + k, 1), :] = m + jnp.log2(l)
                shift_ref[pl.ds(4 * half + k, 1), :] = m
                return carry

            lax.fori_loop(0, 4, shifted, 0)

    for p in range(Z):
        out_ref[p] = s_ref[...]


def mid_kernel(
    cols_ref, qa_ref, qb_ref, shift_ref, mass_ref, out_ref, scale_ref, log_ref, acc_ref, o_ref
):
    chunk = log_ref.shape[1]
    parts = [cols_ref[z] for z in range(Z)]
    peak = functools.reduce(jnp.maximum, parts)
    total = functools.reduce(jnp.add, [jnp.exp2(v - peak) for v in parts])
    log_col = peak + jnp.log2(total)
    log_ref[...] = log_col
    scale_ref[...] = shift_ref[...] - log_col
    acc_ref[...] = jnp.zeros(acc_ref.shape, F32)

    for half, q_ref in enumerate((qa_ref, qb_ref)):

        def step(k, carry, half=half, q_ref=q_ref):
            log_mass = mass_ref[:, pl.ds(pl.multiple_of((4 * half + k) * chunk, chunk), chunk)]
            w = jnp.exp2(log_mass + scale_ref[pl.ds(4 * half + k, 1), :])
            q = q_ref[:, pl.ds(pl.multiple_of(k * chunk, chunk), chunk)]
            acc_ref[...] += fold(q * w, jnp.add)
            return carry

        lax.fori_loop(0, 4, step, 0)
    scale_ref[...] = jnp.exp2(scale_ref[...])
    set_tile(o_ref, jnp.sum(jnp.transpose(acc_ref[...]), axis=0, keepdims=True))
    for p in range(out_ref.shape[0]):
        out_ref[p] = o_ref[...]


def last_kernel(ratio_ref, qa_ref, qb_ref, src_ref, scale_ref, out_ref, pot_ref, r_ref, s_ref):
    chunk = s_ref.shape[1]
    ratio = ratio_ref[0]
    for p in range(1, ratio_ref.shape[0]):
        ratio = ratio + ratio_ref[p]
    ratio = row_of(ratio)
    mass = src_ref[1:2, :]
    r_ref[...] = jnp.transpose(jnp.broadcast_to(mass / ratio, (128, ratio.shape[1])))
    s_ref[0:1, :] = LN2 * (src_ref[0:1, :] - jnp.log2(ratio))
    rows = pot_ref.shape[1]
    mine = pl.multiple_of(lax.axis_index("x") * rows, rows)
    pot_ref[...] = s_ref[0:1, pl.ds(mine, rows)]
    for half, q_ref in enumerate((qa_ref, qb_ref)):

        def step(k, carry, half=half, q_ref=q_ref):
            cols = pl.ds(pl.multiple_of(k * chunk, chunk), chunk)
            accs = [jnp.zeros((8, 128), F32)] * (chunk // 128)
            for h in range(0, r_ref.shape[0], 8):
                r = r_ref[h : h + 8, :]
                q = q_ref[h : h + 8, cols]
                for j in range(chunk // 128):
                    accs[j] = accs[j] + q[:, 128 * j : 128 * j + 128] * r
            acc = jnp.concatenate(accs, axis=1)
            s_ref[pl.ds(4 * half + k, 1), :] = jnp.sum(acc, axis=0, keepdims=True)
            return carry

        lax.fori_loop(0, 4, step, 0)
    lane = lax.broadcasted_iota(jnp.int32, (1, 128), 1)
    extra = jnp.where(lane == 0, jnp.sum(mass), jnp.sum(ratio))
    s_ref[...] = s_ref[...] * scale_ref[...]
    for k in range(8):
        row = s_ref[k : k + 1, :]
        for p in range(Z):
            out_ref[p, :, k * chunk : (k + 1) * chunk] = row
    for p in range(Z):
        out_ref[p, :, 8 * chunk : 8 * chunk + 128] = extra


def end_kernel(cols_ref, log_ref, pot_ref, out_ref, src_ref, o_ref, s_ref):
    chunk = log_ref.shape[1]
    def over_z(lanes):
        return functools.reduce(jnp.add, [cols_ref[z, :, lanes] for z in range(Z)])

    for k in range(8):
        s_ref[k : k + 1, :] = over_z(slice(k * chunk, (k + 1) * chunk))
    total = s_ref[...]
    sums = jnp.log(over_z(slice(8 * chunk, 8 * chunk + 128)))
    log_src, log_tgt = sums[:, 0:1], sums[:, 1:2]
    src_ref[...] = pot_ref[...] + (2.0 * log_tgt - log_src)
    pot = -LN2 * (jnp.log2(total) + log_ref[...]) + 2.0 * (log_src - log_tgt)
    per = chunk // 128
    for k in range(8):
        for s in range(per):
            o_ref[per * k + s : per * k + s + 1, :] = pot[k : k + 1, 128 * s : 128 * s + 128]
    for p in range(X):
        out_ref[p] = o_ref[...]


def kernel_call(body, out_shape, scratch, args, space=pltpu.VMEM, megabytes=8):
    vmem = pl.BlockSpec(memory_space=pltpu.VMEM)
    return pl.pallas_call(
        body,
        out_shape=[
            jax.ShapeDtypeStruct(s, F32) if isinstance(s, tuple) else s for s in out_shape
        ],
        in_specs=[pl.BlockSpec(memory_space=space)] * len(args),
        out_specs=[vmem] * len(out_shape),
        scratch_shapes=scratch,
        compiler_params=pltpu.CompilerParams(vmem_limit_bytes=megabytes * 2**20),
    )(*args)


def trade(v, axes):
    return lax.all_to_all(v, axes, 0, 0)


def on_device(src_points, tgt_points, src_mass, tgt_mass):
    rows = src_points.shape[1]
    cols = tgt_points.shape[1]
    nsrc = rows * X
    ntgt = cols // X
    chunk = ntgt // 8

    first, share, log_mass = kernel_call(
        row_kernel,
        [(GROUP, 8, 128), jax.ShapeDtypeStruct((48, ntgt), BF16), (1, ntgt)],
        [
            pltpu.VMEM((3, rows), F32),
            pltpu.VMEM((1, rows), F32),
            pltpu.VMEM((3, cols), F32),
            pltpu.VMEM((1, cols), F32),
            pltpu.SemaphoreType.DMA((4,)),
            pltpu.VMEM((8, rows), F32),
            pltpu.VMEM((8, cols), F32),
            pltpu.VMEM((48, cols), BF16),
            pltpu.VMEM((8, 128), F32),
        ],
        [
            pltpu.with_memory_space_constraint(v, pltpu.HBM)
            for v in (src_points, src_mass.reshape(1, rows), tgt_points, tgt_mass.reshape(1, cols))
        ],
        space=pltpu.HBM,
        megabytes=50,
    )
    first = trade(first, ("x", "y", "c"))
    half = pltpu.VMEM((nsrc, ntgt // 2), F32)
    *q, logs, shift, src_rows = kernel_call(
        col_kernel,
        [half, half, (Z, 8, chunk), (8, chunk), (8, nsrc)],
        [
            pltpu.VMEM((8, nsrc), F32),
            pltpu.VMEM((8, chunk), F32),
        ],
        (first, share),
    )
    q = [pltpu.with_memory_space_constraint(v, pltpu.VMEM) for v in q]
    logs = trade(logs, "z")
    ratio, scale, log_col = kernel_call(
        mid_kernel,
        [(GROUP, 8, 128), (8, chunk), (8, chunk)],
        [pltpu.VMEM((nsrc, 128), F32), pltpu.VMEM((8, 128), F32)],
        (logs, *q, shift, log_mass),
        megabytes=4,
    )
    ratio = trade(ratio, ("x", "y", "c"))
    col_sums, pot = kernel_call(
        last_kernel,
        [(Z, 1, ntgt + 128), (1, rows)],
        [pltpu.VMEM((nsrc, 128), F32), pltpu.VMEM((8, chunk), F32)],
        (ratio, *q, src_rows, scale),
        megabytes=4,
    )
    col_sums = trade(col_sums, "z")
    tgt_pot, src_pot = kernel_call(
        end_kernel,
        [(X, ntgt // 128, 128), (1, rows)],
        [pltpu.VMEM((ntgt // 128, 128), F32), pltpu.VMEM((8, chunk), F32)],
        (col_sums, log_col, pot),
        megabytes=4,
    )
    return (src_pot.reshape(rows), trade(tgt_pot, "x").reshape(cols))


def solution(mesh):
    fine = Mesh(mesh.devices.reshape(Z, X, Y, C), ("z", "x", "y", "c"))
    row, col = ("z", "x"), ("y", "c")
    placed = (P(None, row), P(None, col), P(row), P(col))
    return jax.shard_map(
        on_device, mesh=fine, in_specs=placed, out_specs=(P(row), P(col)), check_vma=False
    )
```

```python
import functools
import math

import jax
import jax.numpy as jnp
from jax import lax
from jax.experimental import pallas as pl
from jax.experimental.pallas import tpu as pltpu
from jax.sharding import Mesh, PartitionSpec as P

EPSILON = 0.01
LN2 = math.log(2.0)
SCALE = 1.0 / (EPSILON * LN2)
CENTER = 0.5
FLOOR1 = 2.0**-60
FLOOR2 = 2.0**-40
BF16 = jnp.bfloat16
F32 = jnp.float32

Z, X, Y, C = 8, 4, 4, 2
NCOL = Y * C
GROUP = X * NCOL


def pieces(v):
    p1 = v.astype(BF16).astype(F32)
    r = v - p1
    p2 = r.astype(BF16).astype(F32)
    p3 = (r - p2).astype(BF16).astype(F32)
    return p1, p2, p3


def stack_src(v):
    p1, p2, p3 = pieces(v)
    return [
        jnp.concatenate([p1, p2], axis=0),
        jnp.concatenate([p3, p1], axis=0),
        jnp.concatenate([p2, p1], axis=0),
    ]


def stack_tgt(v):
    p1, p2, p3 = pieces(v)
    return [
        jnp.concatenate([p1, p1], axis=0),
        jnp.concatenate([p1, p2], axis=0),
        jnp.concatenate([p2, p3], axis=0),
    ]


def scores(lhs, rhs):
    return lax.dot_general(
        lhs, rhs, (((1,), (0,)), ((), ())), preferred_element_type=F32
    )


def fold(v, op):
    out = v[:, 0:128]
    for k in range(128, v.shape[1], 128):
        out = op(out, v[:, k : k + 128])
    return out


def src_side(x_ref, use_mass):
    n = x_ref.shape[1]
    x_ref[0:3, :] = x_ref[0:3, :] - CENTER
    a, b, c = x_ref[0:1, :], x_ref[1:2, :], x_ref[2:3, :]
    x_ref[3:4, :] = x_ref[3:4, :] - SCALE * (a * a + b * b + c * c)
    x_ref[0:3, :] = x_ref[0:3, :] * (2.0 * SCALE)
    x_ref[4:7, :] = jnp.ones((3, n), F32)
    x_ref[7:8, :] = jnp.full((1, n), use_mass, F32)
    stacked = jnp.concatenate(stack_src(x_ref[...]), axis=0)
    return jnp.transpose(stacked).astype(BF16)


def row_of(tile):
    return jnp.concatenate([tile[s : s + 1, :] for s in range(tile.shape[0])], axis=1)


def set_tile(ref, row):
    for s in range(row.shape[1] // 128):
        ref[s : s + 1, :] = row[:, 128 * s : 128 * s + 128]


def row_kernel(
    src_hbm,
    src_mass_hbm,
    tgt_hbm,
    mass_hbm,
    out_ref,
    share_ref,
    log_ref,
    src_ref,
    src_mass_ref,
    tgt_ref,
    mass_ref,
    sem,
    x_ref,
    t_ref,
    w_ref,
    o_ref,
):
    n = tgt_ref.shape[1]
    rows = src_ref.shape[1]
    parts = [slice(0, n // 8), slice(n // 8, n)]
    pairs = [(src_hbm, src_ref), (src_mass_hbm, src_mass_ref)]
    for lanes in parts:
        pairs.append((tgt_hbm.at[:, lanes], tgt_ref.at[:, lanes]))
        pairs.append((mass_hbm.at[:, lanes], mass_ref.at[:, lanes]))
    moves = [pltpu.make_async_copy(a, b, sem.at[i]) for i, (a, b) in enumerate(pairs)]
    for move in moves:
        move.start()
    moves[0].wait()
    x_ref[0:3, :] = src_ref[...]
    x_ref[3:4, :] = jnp.zeros((1, rows), F32)
    lhs = src_side(x_ref, 1.0)
    moves[1].wait()
    acc = jnp.zeros((rows, 128), F32)
    for k, lanes in enumerate(parts):
        moves[2 * k + 2].wait()
        moves[2 * k + 3].wait()
        points = tgt_ref[:, lanes] - CENTER
        t_ref[0:3, lanes] = points
        t_ref[3:4, lanes] = jnp.ones((1, points.shape[1]), F32)
        t_ref[4:7, lanes] = points * points * -SCALE
        t_ref[7:8, lanes] = jnp.log2(mass_ref[:, lanes])
        for i, part in enumerate(stack_tgt(t_ref[:, lanes])):
            w_ref[16 * i : 16 * i + 16, lanes] = part.astype(BF16)
        acc = acc + fold(jnp.exp2(scores(lhs, w_ref[:, lanes])), jnp.add)
    total = jnp.sum(jnp.transpose(acc), axis=0, keepdims=True)
    set_tile(o_ref, jnp.log2(total))

    @pl.when(jnp.min(total) < FLOOR1)
    def _():
        small = 1024

        def block(k):
            return scores(lhs, w_ref[:, pl.ds(pl.multiple_of(k * small, small), small)])

        def top(k, m):
            return jnp.maximum(m, fold(block(k), jnp.maximum))

        m = lax.fori_loop(0, n // small, top, jnp.full((rows, 128), -jnp.inf, F32))
        m = jnp.max(m, axis=1, keepdims=True)

        def shifted(k, acc):
            return acc + fold(jnp.exp2(block(k) - m), jnp.add)

        acc = lax.fori_loop(0, n // small, shifted, jnp.zeros((rows, 128), F32))
        total = jnp.sum(jnp.transpose(acc), axis=0, keepdims=True)
        peak = jnp.transpose(jnp.broadcast_to(m, (rows, 128)))[0:1, :]
        set_tile(o_ref, jnp.log2(total) + peak)

    col = lax.axis_index("y") * C + lax.axis_index("c")
    info = src_mass_ref[...]
    for d in range(3):
        info = jnp.where(col == d, src_ref[d : d + 1, :], info)
    for s in range(rows // 128):
        o_ref[2 + s : 3 + s, :] = info[:, 128 * s : 128 * s + 128]
    for p in range(out_ref.shape[0]):
        out_ref[p] = o_ref[...]
    share = share_ref.shape[1]
    mine = pl.ds(pl.multiple_of(lax.axis_index("x") * share, share), share)
    share_ref[...] = w_ref[:, mine]
    log_ref[...] = t_ref[7:8, mine]


def set_src(first_ref, x_ref):
    logs, masses = [], []
    for x in range(X):
        parts = [first_ref[x * NCOL + q] for q in range(NCOL)]
        peak = functools.reduce(jnp.maximum, parts)
        total = functools.reduce(jnp.add, [jnp.exp2(v - peak) for v in parts])
        log_sum = peak + jnp.log2(total)
        for s in range(2):
            lanes = slice(256 * x + 128 * s, 256 * x + 128 * s + 128)
            for d in range(3):
                x_ref[d : d + 1, lanes] = parts[d][2 + s : 3 + s, :]
            logs.append(log_sum[s : s + 1, :])
            masses.append(parts[3][2 + s : 3 + s, :])
    mass = jnp.concatenate(masses, axis=1)
    return jnp.log2(mass), mass, jnp.concatenate(logs, axis=1)


def col_kernel(
    first_ref, w_ref, qa_ref, qb_ref, out_ref, shift_ref, src_ref, x_ref, s_ref
):
    chunk = s_ref.shape[1]
    log_mass, mass, log_sum = set_src(first_ref, x_ref)
    src_ref[...] = jnp.zeros(src_ref.shape, F32)
    src_ref[0:1, :] = log_mass - log_sum
    src_ref[1:2, :] = mass
    x_ref[3:4, :] = log_mass - log_sum
    lhs = src_side(x_ref, 0.0)

    def block(k):
        return scores(lhs, w_ref[:, pl.ds(pl.multiple_of(k * chunk, chunk), chunk)])

    for half, q_ref in enumerate((qa_ref, qb_ref)):

        def step(k, carry, half=half, q_ref=q_ref):
            q = jnp.exp2(block(4 * half + k))
            q_ref[:, pl.ds(pl.multiple_of(k * chunk, chunk), chunk)] = q
            s_ref[pl.ds(4 * half + k, 1), :] = jnp.sum(q, axis=0, keepdims=True)
            return carry

        lax.fori_loop(0, 4, step, 0, unroll=4)
    total = s_ref[...]
    s_ref[...] = jnp.log2(total)
    shift_ref[...] = jnp.zeros(shift_ref.shape, F32)

    @pl.when(jnp.min(total) < FLOOR2)
    def _():
        for half, q_ref in enumerate((qa_ref, qb_ref)):

            def shifted(k, carry, half=half, q_ref=q_ref):
                s = block(4 * half + k)
                m = jnp.max(s, axis=0, keepdims=True)
                q = jnp.exp2(s - m)
                q_ref[:, pl.ds(pl.multiple_of(k * chunk, chunk), chunk)] = q
                l = jnp.sum(q, axis=0, keepdims=True)
                s_ref[pl.ds(4 * half + k, 1), :] = m + jnp.log2(l)
                shift_ref[pl.ds(4 * half + k, 1), :] = m
                return carry

            lax.fori_loop(0, 4, shifted, 0)

    for p in range(Z):
        out_ref[p] = s_ref[...]


def mid_kernel(
    cols_ref, qa_ref, qb_ref, shift_ref, mass_ref, out_ref, scale_ref, log_ref, acc_ref, o_ref
):
    chunk = log_ref.shape[1]
    parts = [cols_ref[z] for z in range(Z)]
    peak = functools.reduce(jnp.maximum, parts)
    total = functools.reduce(jnp.add, [jnp.exp2(v - peak) for v in parts])
    log_col = peak + jnp.log2(total)
    log_ref[...] = log_col
    scale_ref[...] = shift_ref[...] - log_col
    acc_ref[...] = jnp.zeros(acc_ref.shape, F32)

    for half, q_ref in enumerate((qa_ref, qb_ref)):

        def step(k, carry, half=half, q_ref=q_ref):
            log_mass = mass_ref[:, pl.ds(pl.multiple_of((4 * half + k) * chunk, chunk), chunk)]
            w = jnp.exp2(log_mass + scale_ref[pl.ds(4 * half + k, 1), :])
            q = q_ref[:, pl.ds(pl.multiple_of(k * chunk, chunk), chunk)]
            acc_ref[...] += fold(q * w, jnp.add)
            return carry

        lax.fori_loop(0, 4, step, 0)
    scale_ref[...] = jnp.exp2(scale_ref[...])
    set_tile(o_ref, jnp.sum(jnp.transpose(acc_ref[...]), axis=0, keepdims=True))
    for p in range(out_ref.shape[0]):
        out_ref[p] = o_ref[...]


def last_kernel(ratio_ref, qa_ref, qb_ref, src_ref, scale_ref, out_ref, pot_ref, r_ref, s_ref):
    chunk = s_ref.shape[1]
    ratio = ratio_ref[0]
    for p in range(1, ratio_ref.shape[0]):
        ratio = ratio + ratio_ref[p]
    ratio = row_of(ratio)
    mass = src_ref[1:2, :]
    r_ref[...] = jnp.transpose(jnp.broadcast_to(mass / ratio, (128, ratio.shape[1])))
    s_ref[0:1, :] = LN2 * (src_ref[0:1, :] - jnp.log2(ratio))
    rows = pot_ref.shape[1]
    mine = pl.multiple_of(lax.axis_index("x") * rows, rows)
    pot_ref[...] = s_ref[0:1, pl.ds(mine, rows)]
    for half, q_ref in enumerate((qa_ref, qb_ref)):

        def step(k, carry, half=half, q_ref=q_ref):
            cols = pl.ds(pl.multiple_of(k * chunk, chunk), chunk)
            accs = [jnp.zeros((8, 128), F32)] * (chunk // 128)
            for h in range(0, r_ref.shape[0], 8):
                r = r_ref[h : h + 8, :]
                q = q_ref[h : h + 8, cols]
                for j in range(chunk // 128):
                    accs[j] = accs[j] + q[:, 128 * j : 128 * j + 128] * r
            acc = jnp.concatenate(accs, axis=1)
            s_ref[pl.ds(4 * half + k, 1), :] = jnp.sum(acc, axis=0, keepdims=True)
            return carry

        lax.fori_loop(0, 4, step, 0)
    lane = lax.broadcasted_iota(jnp.int32, (1, 128), 1)
    extra = jnp.where(lane == 0, jnp.sum(mass), jnp.sum(ratio))
    s_ref[...] = s_ref[...] * scale_ref[...]
    for k in range(8):
        row = s_ref[k : k + 1, :]
        for p in range(Z):
            out_ref[p, :, k * chunk : (k + 1) * chunk] = row
    for p in range(Z):
        out_ref[p, :, 8 * chunk : 8 * chunk + 128] = extra


def end_kernel(cols_ref, log_ref, pot_ref, out_ref, src_ref, o_ref, s_ref):
    chunk = log_ref.shape[1]
    def over_z(lanes):
        return functools.reduce(jnp.add, [cols_ref[z, :, lanes] for z in range(Z)])

    for k in range(8):
        s_ref[k : k + 1, :] = over_z(slice(k * chunk, (k + 1) * chunk))
    total = s_ref[...]
    sums = jnp.log(over_z(slice(8 * chunk, 8 * chunk + 128)))
    log_src, log_tgt = sums[:, 0:1], sums[:, 1:2]
    src_ref[...] = pot_ref[...] + (2.0 * log_tgt - log_src)
    pot = -LN2 * (jnp.log2(total) + log_ref[...]) + 2.0 * (log_src - log_tgt)
    per = chunk // 128
    for k in range(8):
        for s in range(per):
            o_ref[per * k + s : per * k + s + 1, :] = pot[k : k + 1, 128 * s : 128 * s + 128]
    for p in range(X):
        out_ref[p] = o_ref[...]


def kernel_call(body, out_shape, scratch, args, space=pltpu.VMEM, megabytes=8):
    vmem = pl.BlockSpec(memory_space=pltpu.VMEM)
    return pl.pallas_call(
        body,
        out_shape=[
            jax.ShapeDtypeStruct(s, F32) if isinstance(s, tuple) else s for s in out_shape
        ],
        in_specs=[pl.BlockSpec(memory_space=space)] * len(args),
        out_specs=[vmem] * len(out_shape),
        scratch_shapes=scratch,
        compiler_params=pltpu.CompilerParams(vmem_limit_bytes=megabytes * 2**20),
    )(*args)


def trade(v, axes):
    return lax.all_to_all(v, axes, 0, 0)


def on_device(src_points, tgt_points, src_mass, tgt_mass):
    rows = src_points.shape[1]
    cols = tgt_points.shape[1]
    nsrc = rows * X
    ntgt = cols // X
    chunk = ntgt // 8

    first, share, log_mass = kernel_call(
        row_kernel,
        [(GROUP, 4, 128), jax.ShapeDtypeStruct((48, ntgt), BF16), (1, ntgt)],
        [
            pltpu.VMEM((3, rows), F32),
            pltpu.VMEM((1, rows), F32),
            pltpu.VMEM((3, cols), F32),
            pltpu.VMEM((1, cols), F32),
            pltpu.SemaphoreType.DMA((6,)),
            pltpu.VMEM((8, rows), F32),
            pltpu.VMEM((8, cols), F32),
            pltpu.VMEM((48, cols), BF16),
            pltpu.VMEM((4, 128), F32),
        ],
        [
            pltpu.with_memory_space_constraint(v, pltpu.HBM)
            for v in (src_points, src_mass.reshape(1, rows), tgt_points, tgt_mass.reshape(1, cols))
        ],
        space=pltpu.HBM,
        megabytes=50,
    )
    first = trade(first, ("x", "y", "c"))
    half = pltpu.VMEM((nsrc, ntgt // 2), F32)
    *q, logs, shift, src_rows = kernel_call(
        col_kernel,
        [half, half, (Z, 8, chunk), (8, chunk), (8, nsrc)],
        [
            pltpu.VMEM((8, nsrc), F32),
            pltpu.VMEM((8, chunk), F32),
        ],
        (first, share),
    )
    q = [pltpu.with_memory_space_constraint(v, pltpu.VMEM) for v in q]
    logs = trade(logs, "z")
    ratio, scale, log_col = kernel_call(
        mid_kernel,
        [(GROUP, 8, 128), (8, chunk), (8, chunk)],
        [pltpu.VMEM((nsrc, 128), F32), pltpu.VMEM((8, 128), F32)],
        (logs, *q, shift, log_mass),
        megabytes=4,
    )
    ratio = trade(ratio, ("x", "y", "c"))
    col_sums, pot = kernel_call(
        last_kernel,
        [(Z, 1, ntgt + 128), (1, rows)],
        [pltpu.VMEM((nsrc, 128), F32), pltpu.VMEM((8, chunk), F32)],
        (ratio, *q, src_rows, scale),
        megabytes=4,
    )
    col_sums = trade(col_sums, "z")
    tgt_pot, src_pot = kernel_call(
        end_kernel,
        [(X, ntgt // 128, 128), (1, rows)],
        [pltpu.VMEM((ntgt // 128, 128), F32), pltpu.VMEM((8, chunk), F32)],
        (col_sums, log_col, pot),
        megabytes=4,
    )
    return (src_pot.reshape(rows), trade(tgt_pot, "x").reshape(cols))


def solution(mesh):
    fine = Mesh(mesh.devices.reshape(Z, X, Y, C), ("z", "x", "y", "c"))
    row, col = ("z", "x"), ("y", "c")
    placed = (P(None, row), P(None, col), P(row), P(col))
    return jax.shard_map(
        on_device, mesh=fine, in_specs=placed, out_specs=(P(row), P(col)), check_vma=False
    )
```

```python
import functools
import math

import jax
import jax.numpy as jnp
from jax import lax
from jax.experimental import pallas as pl
from jax.experimental.pallas import tpu as pltpu
from jax.sharding import Mesh, PartitionSpec as P

EPSILON = 0.01
LN2 = math.log(2.0)
SCALE = 1.0 / (EPSILON * LN2)
CENTER = 0.5
FLOOR1 = 2.0**-60
FLOOR2 = 2.0**-40
BF16 = jnp.bfloat16
F32 = jnp.float32

Z, X, Y, C = 8, 4, 4, 2
NCOL = Y * C
GROUP = X * NCOL


def pieces(v):
    p1 = v.astype(BF16).astype(F32)
    r = v - p1
    p2 = r.astype(BF16).astype(F32)
    p3 = (r - p2).astype(BF16).astype(F32)
    return p1, p2, p3


def stack_src(v):
    p1, p2, p3 = pieces(v)
    return [
        jnp.concatenate([p1, p2], axis=0),
        jnp.concatenate([p3, p1], axis=0),
        jnp.concatenate([p2, p1], axis=0),
    ]


def stack_tgt(v):
    p1, p2, p3 = pieces(v)
    return [
        jnp.concatenate([p1, p1], axis=0),
        jnp.concatenate([p1, p2], axis=0),
        jnp.concatenate([p2, p3], axis=0),
    ]


def scores(lhs, rhs):
    return lax.dot_general(
        lhs, rhs, (((1,), (0,)), ((), ())), preferred_element_type=F32
    )


def fold(v, op):
    out = v[:, 0:128]
    for k in range(128, v.shape[1], 128):
        out = op(out, v[:, k : k + 128])
    return out


def src_side(x_ref, use_mass):
    n = x_ref.shape[1]
    x_ref[0:3, :] = x_ref[0:3, :] - CENTER
    a, b, c = x_ref[0:1, :], x_ref[1:2, :], x_ref[2:3, :]
    x_ref[3:4, :] = x_ref[3:4, :] - SCALE * (a * a + b * b + c * c)
    x_ref[0:3, :] = x_ref[0:3, :] * (2.0 * SCALE)
    x_ref[4:7, :] = jnp.ones((3, n), F32)
    x_ref[7:8, :] = jnp.full((1, n), use_mass, F32)
    stacked = jnp.concatenate(stack_src(x_ref[...]), axis=0)
    return jnp.transpose(stacked).astype(BF16)


def row_of(tile):
    return jnp.concatenate([tile[s : s + 1, :] for s in range(tile.shape[0])], axis=1)


def set_tile(ref, row):
    for s in range(row.shape[1] // 128):
        ref[s : s + 1, :] = row[:, 128 * s : 128 * s + 128]


def row_kernel(
    src_hbm,
    src_mass_hbm,
    tgt_hbm,
    mass_hbm,
    out_ref,
    share_ref,
    log_ref,
    src_ref,
    src_mass_ref,
    tgt_ref,
    mass_ref,
    sem,
    x_ref,
    t_ref,
    w_ref,
    o_ref,
):
    n = tgt_ref.shape[1]
    rows = src_ref.shape[1]
    parts = [slice(0, n // 8), slice(n // 8, n)]
    pairs = [(src_hbm, src_ref), (src_mass_hbm, src_mass_ref)]
    for lanes in parts:
        pairs.append((tgt_hbm.at[:, lanes], tgt_ref.at[:, lanes]))
        pairs.append((mass_hbm.at[:, lanes], mass_ref.at[:, lanes]))
    moves = [pltpu.make_async_copy(a, b, sem.at[i]) for i, (a, b) in enumerate(pairs)]
    for move in moves:
        move.start()
    moves[0].wait()
    x_ref[0:3, :] = src_ref[...]
    x_ref[3:4, :] = jnp.zeros((1, rows), F32)
    lhs = src_side(x_ref, 1.0)
    moves[1].wait()
    acc = jnp.zeros((rows, 128), F32)
    for k, lanes in enumerate(parts):
        moves[2 * k + 2].wait()
        moves[2 * k + 3].wait()
        points = tgt_ref[:, lanes] - CENTER
        t_ref[0:3, lanes] = points
        t_ref[3:4, lanes] = jnp.ones((1, points.shape[1]), F32)
        t_ref[4:7, lanes] = points * points * -SCALE
        t_ref[7:8, lanes] = jnp.log2(mass_ref[:, lanes])
        for i, part in enumerate(stack_tgt(t_ref[:, lanes])):
            w_ref[16 * i : 16 * i + 16, lanes] = part.astype(BF16)
        acc = acc + fold(jnp.exp2(scores(lhs, w_ref[:, lanes])), jnp.add)
    total = jnp.sum(jnp.transpose(acc), axis=0, keepdims=True)
    set_tile(o_ref, jnp.log2(total))

    @pl.when(jnp.min(total) < FLOOR1)
    def _():
        small = 1024

        def block(k):
            return scores(lhs, w_ref[:, pl.ds(pl.multiple_of(k * small, small), small)])

        def top(k, m):
            return jnp.maximum(m, fold(block(k), jnp.maximum))

        m = lax.fori_loop(0, n // small, top, jnp.full((rows, 128), -jnp.inf, F32))
        m = jnp.max(m, axis=1, keepdims=True)

        def shifted(k, acc):
            return acc + fold(jnp.exp2(block(k) - m), jnp.add)

        acc = lax.fori_loop(0, n // small, shifted, jnp.zeros((rows, 128), F32))
        total = jnp.sum(jnp.transpose(acc), axis=0, keepdims=True)
        peak = jnp.transpose(jnp.broadcast_to(m, (rows, 128)))[0:1, :]
        set_tile(o_ref, jnp.log2(total) + peak)

    col = lax.axis_index("y") * C + lax.axis_index("c")
    info = src_mass_ref[...]
    for d in range(3):
        info = jnp.where(col == d, src_ref[d : d + 1, :], info)
    for s in range(rows // 128):
        o_ref[2 + s : 3 + s, :] = info[:, 128 * s : 128 * s + 128]
    for p in range(out_ref.shape[0]):
        out_ref[p] = o_ref[...]
    share = share_ref.shape[1]
    mine = pl.ds(pl.multiple_of(lax.axis_index("x") * share, share), share)
    share_ref[...] = w_ref[:, mine]
    log_ref[...] = t_ref[7:8, mine]


def set_src(first_ref, x_ref):
    logs, masses = [], []
    for x in range(X):
        parts = [first_ref[x * NCOL + q] for q in range(NCOL)]
        peak = functools.reduce(jnp.maximum, parts)
        total = functools.reduce(jnp.add, [jnp.exp2(v - peak) for v in parts])
        log_sum = peak + jnp.log2(total)
        for s in range(2):
            lanes = slice(256 * x + 128 * s, 256 * x + 128 * s + 128)
            for d in range(3):
                x_ref[d : d + 1, lanes] = parts[d][2 + s : 3 + s, :]
            logs.append(log_sum[s : s + 1, :])
            masses.append(parts[3][2 + s : 3 + s, :])
    mass = jnp.concatenate(masses, axis=1)
    return jnp.log2(mass), mass, jnp.concatenate(logs, axis=1)


def col_kernel(
    first_ref, w_ref, qa_ref, qb_ref, out_ref, shift_ref, src_ref, x_ref, s_ref
):
    chunk = s_ref.shape[1]
    log_mass, mass, log_sum = set_src(first_ref, x_ref)
    src_ref[...] = jnp.zeros(src_ref.shape, F32)
    src_ref[0:1, :] = log_mass - log_sum
    src_ref[1:2, :] = mass
    x_ref[3:4, :] = log_mass - log_sum
    lhs = src_side(x_ref, 0.0)

    def block(k):
        return scores(lhs, w_ref[:, pl.ds(pl.multiple_of(k * chunk, chunk), chunk)])

    for half, q_ref in enumerate((qa_ref, qb_ref)):

        def step(k, carry, half=half, q_ref=q_ref):
            q = jnp.exp2(block(4 * half + k))
            q_ref[:, pl.ds(pl.multiple_of(k * chunk, chunk), chunk)] = q
            s_ref[pl.ds(4 * half + k, 1), :] = jnp.sum(q, axis=0, keepdims=True)
            return carry

        lax.fori_loop(0, 4, step, 0, unroll=4)
    total = s_ref[...]
    s_ref[...] = jnp.log2(total)
    shift_ref[...] = jnp.zeros(shift_ref.shape, F32)

    @pl.when(jnp.min(total) < FLOOR2)
    def _():
        for half, q_ref in enumerate((qa_ref, qb_ref)):

            def shifted(k, carry, half=half, q_ref=q_ref):
                s = block(4 * half + k)
                m = jnp.max(s, axis=0, keepdims=True)
                q = jnp.exp2(s - m)
                q_ref[:, pl.ds(pl.multiple_of(k * chunk, chunk), chunk)] = q
                l = jnp.sum(q, axis=0, keepdims=True)
                s_ref[pl.ds(4 * half + k, 1), :] = m + jnp.log2(l)
                shift_ref[pl.ds(4 * half + k, 1), :] = m
                return carry

            lax.fori_loop(0, 4, shifted, 0)

    for p in range(Z):
        out_ref[p] = s_ref[...]


def mid_kernel(
    cols_ref, qa_ref, qb_ref, shift_ref, mass_ref, out_ref, scale_ref, log_ref, acc_ref, o_ref
):
    chunk = log_ref.shape[1]
    parts = [cols_ref[z] for z in range(Z)]
    peak = functools.reduce(jnp.maximum, parts)
    total = functools.reduce(jnp.add, [jnp.exp2(v - peak) for v in parts])
    log_col = peak + jnp.log2(total)
    log_ref[...] = log_col
    scale_ref[...] = shift_ref[...] - log_col
    acc_ref[...] = jnp.zeros(acc_ref.shape, F32)

    for half, q_ref in enumerate((qa_ref, qb_ref)):

        def step(k, carry, half=half, q_ref=q_ref):
            log_mass = mass_ref[:, pl.ds(pl.multiple_of((4 * half + k) * chunk, chunk), chunk)]
            w = jnp.exp2(log_mass + scale_ref[pl.ds(4 * half + k, 1), :])
            q = q_ref[:, pl.ds(pl.multiple_of(k * chunk, chunk), chunk)]
            acc_ref[...] += fold(q * w, jnp.add)
            return carry

        lax.fori_loop(0, 4, step, 0)
    scale_ref[...] = jnp.exp2(scale_ref[...])
    set_tile(o_ref, jnp.sum(jnp.transpose(acc_ref[...]), axis=0, keepdims=True))
    for p in range(out_ref.shape[0]):
        out_ref[p] = o_ref[...]


def last_kernel(ratio_ref, qa_ref, qb_ref, src_ref, scale_ref, out_ref, pot_ref, r_ref, s_ref):
    chunk = s_ref.shape[1]
    ratio = ratio_ref[0]
    for p in range(1, ratio_ref.shape[0]):
        ratio = ratio + ratio_ref[p]
    ratio = row_of(ratio)
    mass = src_ref[1:2, :]
    r_ref[...] = jnp.transpose(jnp.broadcast_to(mass / ratio, (128, ratio.shape[1])))
    s_ref[0:1, :] = LN2 * (src_ref[0:1, :] - jnp.log2(ratio))
    rows = pot_ref.shape[1]
    mine = pl.multiple_of(lax.axis_index("x") * rows, rows)
    pot_ref[...] = s_ref[0:1, pl.ds(mine, rows)]
    for half, q_ref in enumerate((qa_ref, qb_ref)):

        def step(k, carry, half=half, q_ref=q_ref):
            cols = pl.ds(pl.multiple_of(k * chunk, chunk), chunk)
            accs = [jnp.zeros((8, 128), F32)] * (chunk // 128)
            for h in range(0, r_ref.shape[0], 8):
                r = r_ref[h : h + 8, :]
                q = q_ref[h : h + 8, cols]
                for j in range(chunk // 128):
                    accs[j] = accs[j] + q[:, 128 * j : 128 * j + 128] * r
            acc = jnp.concatenate(accs, axis=1)
            s_ref[pl.ds(4 * half + k, 1), :] = jnp.sum(acc, axis=0, keepdims=True)
            return carry

        lax.fori_loop(0, 4, step, 0)
    lane = lax.broadcasted_iota(jnp.int32, (1, 128), 1)
    extra = jnp.where(lane == 0, jnp.sum(mass), jnp.sum(ratio))
    s_ref[...] = s_ref[...] * scale_ref[...]
    for k in range(8):
        row = s_ref[k : k + 1, :]
        for p in range(Z):
            out_ref[p, :, k * chunk : (k + 1) * chunk] = row
    for p in range(Z):
        out_ref[p, :, 8 * chunk : 8 * chunk + 128] = extra


def end_kernel(cols_ref, log_ref, out_ref, const_ref, o_ref, s_ref):
    chunk = log_ref.shape[1]
    def over_z(lanes):
        return functools.reduce(jnp.add, [cols_ref[z, :, lanes] for z in range(Z)])

    for k in range(8):
        s_ref[k : k + 1, :] = over_z(slice(k * chunk, (k + 1) * chunk))
    total = s_ref[...]
    sums = jnp.log(over_z(slice(8 * chunk, 8 * chunk + 128)))
    log_src, log_tgt = sums[:, 0:1], sums[:, 1:2]
    const_ref[...] = jnp.broadcast_to(2.0 * log_tgt - log_src, const_ref.shape)
    pot = -LN2 * (jnp.log2(total) + log_ref[...]) + 2.0 * (log_src - log_tgt)
    per = chunk // 128
    for k in range(8):
        for s in range(per):
            o_ref[per * k + s : per * k + s + 1, :] = pot[k : k + 1, 128 * s : 128 * s + 128]
    for p in range(X):
        out_ref[p] = o_ref[...]


def kernel_call(body, out_shape, scratch, args, space=pltpu.VMEM, megabytes=8):
    vmem = pl.BlockSpec(memory_space=pltpu.VMEM)
    return pl.pallas_call(
        body,
        out_shape=[
            jax.ShapeDtypeStruct(s, F32) if isinstance(s, tuple) else s for s in out_shape
        ],
        in_specs=[pl.BlockSpec(memory_space=space)] * len(args),
        out_specs=[vmem] * len(out_shape),
        scratch_shapes=scratch,
        compiler_params=pltpu.CompilerParams(vmem_limit_bytes=megabytes * 2**20),
    )(*args)


def trade(v, axes):
    return lax.all_to_all(v, axes, 0, 0)


def on_device(src_points, tgt_points, src_mass, tgt_mass):
    rows = src_points.shape[1]
    cols = tgt_points.shape[1]
    nsrc = rows * X
    ntgt = cols // X
    chunk = ntgt // 8

    first, share, log_mass = kernel_call(
        row_kernel,
        [(GROUP, 4, 128), jax.ShapeDtypeStruct((48, ntgt), BF16), (1, ntgt)],
        [
            pltpu.VMEM((3, rows), F32),
            pltpu.VMEM((1, rows), F32),
            pltpu.VMEM((3, cols), F32),
            pltpu.VMEM((1, cols), F32),
            pltpu.SemaphoreType.DMA((6,)),
            pltpu.VMEM((8, rows), F32),
            pltpu.VMEM((8, cols), F32),
            pltpu.VMEM((48, cols), BF16),
            pltpu.VMEM((4, 128), F32),
        ],
        [
            pltpu.with_memory_space_constraint(v, pltpu.HBM)
            for v in (src_points, src_mass.reshape(1, rows), tgt_points, tgt_mass.reshape(1, cols))
        ],
        space=pltpu.HBM,
        megabytes=50,
    )
    first = trade(first, ("x", "y", "c"))
    half = pltpu.VMEM((nsrc, ntgt // 2), F32)
    *q, logs, shift, src_rows = kernel_call(
        col_kernel,
        [half, half, (Z, 8, chunk), (8, chunk), (8, nsrc)],
        [
            pltpu.VMEM((8, nsrc), F32),
            pltpu.VMEM((8, chunk), F32),
        ],
        (first, share),
    )
    q = [pltpu.with_memory_space_constraint(v, pltpu.VMEM) for v in q]
    logs = trade(logs, "z")
    ratio, scale, log_col = kernel_call(
        mid_kernel,
        [(GROUP, 8, 128), (8, chunk), (8, chunk)],
        [pltpu.VMEM((nsrc, 128), F32), pltpu.VMEM((8, 128), F32)],
        (logs, *q, shift, log_mass),
        megabytes=4,
    )
    ratio = trade(ratio, ("x", "y", "c"))
    col_sums, pot = kernel_call(
        last_kernel,
        [(Z, 1, ntgt + 128), (1, rows)],
        [pltpu.VMEM((nsrc, 128), F32), pltpu.VMEM((8, chunk), F32)],
        (ratio, *q, src_rows, scale),
        megabytes=4,
    )
    col_sums = trade(col_sums, "z")
    tgt_pot, const = kernel_call(
        end_kernel,
        [(X, ntgt // 128, 128), (1, rows)],
        [pltpu.VMEM((ntgt // 128, 128), F32), pltpu.VMEM((8, chunk), F32)],
        (col_sums, log_col),
        megabytes=4,
    )
    src_pot = (pot + const).reshape(rows)
    return (src_pot, trade(tgt_pot, "x").reshape(cols))


def solution(mesh):
    fine = Mesh(mesh.devices.reshape(Z, X, Y, C), ("z", "x", "y", "c"))
    row, col = ("z", "x"), ("y", "c")
    placed = (P(None, row), P(None, col), P(row), P(col))
    return jax.shard_map(
        on_device, mesh=fine, in_specs=placed, out_specs=(P(row), P(col)), check_vma=False
    )
```

```python
import functools
import math

import jax
import jax.numpy as jnp
from jax import lax
from jax.experimental import pallas as pl
from jax.experimental.pallas import tpu as pltpu
from jax.sharding import Mesh, PartitionSpec as P

EPSILON = 0.01
LN2 = math.log(2.0)
SCALE = 1.0 / (EPSILON * LN2)
CENTER = 0.5
FLOOR1 = 2.0**-60
FLOOR2 = 2.0**-40
BF16 = jnp.bfloat16
F32 = jnp.float32

Z, X, Y, C = 8, 4, 4, 2
NCOL = Y * C
GROUP = X * NCOL


def pieces(v):
    p1 = v.astype(BF16).astype(F32)
    r = v - p1
    p2 = r.astype(BF16).astype(F32)
    p3 = (r - p2).astype(BF16).astype(F32)
    return p1, p2, p3


def stack_src(v):
    p1, p2, p3 = pieces(v)
    return [
        jnp.concatenate([p1, p2], axis=0),
        jnp.concatenate([p3, p1], axis=0),
        jnp.concatenate([p2, p1], axis=0),
    ]


def stack_tgt(v):
    p1, p2, p3 = pieces(v)
    return [
        jnp.concatenate([p1, p1], axis=0),
        jnp.concatenate([p1, p2], axis=0),
        jnp.concatenate([p2, p3], axis=0),
    ]


def scores(lhs, rhs):
    return lax.dot_general(
        lhs, rhs, (((1,), (0,)), ((), ())), preferred_element_type=F32
    )


def fold(v, op):
    out = v[:, 0:128]
    for k in range(128, v.shape[1], 128):
        out = op(out, v[:, k : k + 128])
    return out


def src_side(x_ref, use_mass):
    n = x_ref.shape[1]
    x_ref[0:3, :] = x_ref[0:3, :] - CENTER
    a, b, c = x_ref[0:1, :], x_ref[1:2, :], x_ref[2:3, :]
    x_ref[3:4, :] = x_ref[3:4, :] - SCALE * (a * a + b * b + c * c)
    x_ref[0:3, :] = x_ref[0:3, :] * (2.0 * SCALE)
    x_ref[4:7, :] = jnp.ones((3, n), F32)
    x_ref[7:8, :] = jnp.full((1, n), use_mass, F32)
    stacked = jnp.concatenate(stack_src(x_ref[...]), axis=0)
    return jnp.transpose(stacked).astype(BF16)


def row_of(tile):
    return jnp.concatenate([tile[s : s + 1, :] for s in range(tile.shape[0])], axis=1)


def set_tile(ref, row):
    for s in range(row.shape[1] // 128):
        ref[s : s + 1, :] = row[:, 128 * s : 128 * s + 128]


def row_kernel(
    src_hbm,
    src_mass_hbm,
    tgt_hbm,
    mass_hbm,
    out_ref,
    share_ref,
    log_ref,
    src_ref,
    src_mass_ref,
    tgt_ref,
    mass_ref,
    sem,
    x_ref,
    t_ref,
    w_ref,
    o_ref,
):
    n = tgt_ref.shape[1]
    rows = src_ref.shape[1]
    parts = [slice(0, n // 8), slice(n // 8, n)]
    pairs = [(src_hbm, src_ref), (src_mass_hbm, src_mass_ref)]
    for lanes in parts:
        pairs.append((tgt_hbm.at[:, lanes], tgt_ref.at[:, lanes]))
        pairs.append((mass_hbm.at[:, lanes], mass_ref.at[:, lanes]))
    moves = [pltpu.make_async_copy(a, b, sem.at[i]) for i, (a, b) in enumerate(pairs)]
    for move in moves:
        move.start()
    moves[0].wait()
    x_ref[0:3, :] = src_ref[...]
    x_ref[3:4, :] = jnp.zeros((1, rows), F32)
    lhs = src_side(x_ref, 1.0)
    moves[1].wait()
    acc = jnp.zeros((rows, 128), F32)
    for k, lanes in enumerate(parts):
        moves[2 * k + 2].wait()
        moves[2 * k + 3].wait()
        points = tgt_ref[:, lanes] - CENTER
        t_ref[0:3, lanes] = points
        t_ref[3:4, lanes] = jnp.ones((1, points.shape[1]), F32)
        t_ref[4:7, lanes] = points * points * -SCALE
        t_ref[7:8, lanes] = jnp.log2(mass_ref[:, lanes])
        for i, part in enumerate(stack_tgt(t_ref[:, lanes])):
            w_ref[16 * i : 16 * i + 16, lanes] = part.astype(BF16)
        acc = acc + fold(jnp.exp2(scores(lhs, w_ref[:, lanes])), jnp.add)
    total = jnp.sum(jnp.transpose(acc), axis=0, keepdims=True)
    set_tile(o_ref, jnp.log2(total))

    @pl.when(jnp.min(total) < FLOOR1)
    def _():
        small = 1024

        def block(k):
            return scores(lhs, w_ref[:, pl.ds(pl.multiple_of(k * small, small), small)])

        def top(k, m):
            return jnp.maximum(m, fold(block(k), jnp.maximum))

        m = lax.fori_loop(0, n // small, top, jnp.full((rows, 128), -jnp.inf, F32))
        m = jnp.max(m, axis=1, keepdims=True)

        def shifted(k, acc):
            return acc + fold(jnp.exp2(block(k) - m), jnp.add)

        acc = lax.fori_loop(0, n // small, shifted, jnp.zeros((rows, 128), F32))
        total = jnp.sum(jnp.transpose(acc), axis=0, keepdims=True)
        peak = jnp.transpose(jnp.broadcast_to(m, (rows, 128)))[0:1, :]
        set_tile(o_ref, jnp.log2(total) + peak)

    col = lax.axis_index("y") * C + lax.axis_index("c")
    info = src_mass_ref[...]
    for d in range(3):
        info = jnp.where(col == d, src_ref[d : d + 1, :], info)
    for s in range(rows // 128):
        o_ref[2 + s : 3 + s, :] = info[:, 128 * s : 128 * s + 128]
    for p in range(out_ref.shape[0]):
        out_ref[p] = o_ref[...]
    share = share_ref.shape[1]
    mine = pl.ds(pl.multiple_of(lax.axis_index("x") * share, share), share)
    share_ref[...] = w_ref[:, mine]
    log_ref[...] = t_ref[7:8, mine]


def set_src(first_ref, x_ref):
    logs, masses = [], []
    for x in range(X):
        parts = [first_ref[x * NCOL + q] for q in range(NCOL)]
        peak = functools.reduce(jnp.maximum, parts)
        total = functools.reduce(jnp.add, [jnp.exp2(v - peak) for v in parts])
        log_sum = peak + jnp.log2(total)
        for s in range(2):
            lanes = slice(256 * x + 128 * s, 256 * x + 128 * s + 128)
            for d in range(3):
                x_ref[d : d + 1, lanes] = parts[d][2 + s : 3 + s, :]
            logs.append(log_sum[s : s + 1, :])
            masses.append(parts[3][2 + s : 3 + s, :])
    mass = jnp.concatenate(masses, axis=1)
    return jnp.log2(mass), mass, jnp.concatenate(logs, axis=1)


def col_kernel(
    first_ref, w_ref, qa_ref, qb_ref, out_ref, shift_ref, src_ref, x_ref, s_ref
):
    chunk = s_ref.shape[1]
    log_mass, mass, log_sum = set_src(first_ref, x_ref)
    src_ref[...] = jnp.zeros(src_ref.shape, F32)
    src_ref[0:1, :] = log_mass - log_sum
    src_ref[1:2, :] = mass
    x_ref[3:4, :] = log_mass - log_sum
    lhs = src_side(x_ref, 0.0)

    def block(k):
        return scores(lhs, w_ref[:, pl.ds(pl.multiple_of(k * chunk, chunk), chunk)])

    for half, q_ref in enumerate((qa_ref, qb_ref)):

        def step(k, carry, half=half, q_ref=q_ref):
            q = jnp.exp2(block(4 * half + k))
            q_ref[:, pl.ds(pl.multiple_of(k * chunk, chunk), chunk)] = q
            s_ref[pl.ds(4 * half + k, 1), :] = jnp.sum(q, axis=0, keepdims=True)
            return carry

        lax.fori_loop(0, 4, step, 0, unroll=4)
    total = s_ref[...]
    s_ref[...] = jnp.log2(total)
    shift_ref[...] = jnp.zeros(shift_ref.shape, F32)

    @pl.when(jnp.min(total) < FLOOR2)
    def _():
        for half, q_ref in enumerate((qa_ref, qb_ref)):

            def shifted(k, carry, half=half, q_ref=q_ref):
                s = block(4 * half + k)
                m = jnp.max(s, axis=0, keepdims=True)
                q = jnp.exp2(s - m)
                q_ref[:, pl.ds(pl.multiple_of(k * chunk, chunk), chunk)] = q
                l = jnp.sum(q, axis=0, keepdims=True)
                s_ref[pl.ds(4 * half + k, 1), :] = m + jnp.log2(l)
                shift_ref[pl.ds(4 * half + k, 1), :] = m
                return carry

            lax.fori_loop(0, 4, shifted, 0)

    for p in range(Z):
        out_ref[p] = s_ref[...]


def mid_kernel(
    cols_ref, qa_ref, qb_ref, shift_ref, mass_ref, out_ref, scale_ref, log_ref, acc_ref, o_ref
):
    chunk = log_ref.shape[1]
    parts = [cols_ref[z] for z in range(Z)]
    peak = functools.reduce(jnp.maximum, parts)
    total = functools.reduce(jnp.add, [jnp.exp2(v - peak) for v in parts])
    log_col = peak + jnp.log2(total)
    log_ref[...] = log_col
    scale_ref[...] = shift_ref[...] - log_col
    acc_ref[...] = jnp.zeros(acc_ref.shape, F32)

    for half, q_ref in enumerate((qa_ref, qb_ref)):

        def step(k, carry, half=half, q_ref=q_ref):
            log_mass = mass_ref[:, pl.ds(pl.multiple_of((4 * half + k) * chunk, chunk), chunk)]
            w = jnp.exp2(log_mass + scale_ref[pl.ds(4 * half + k, 1), :])
            q = q_ref[:, pl.ds(pl.multiple_of(k * chunk, chunk), chunk)]
            acc_ref[...] += fold(q * w, jnp.add)
            return carry

        lax.fori_loop(0, 4, step, 0)
    scale_ref[...] = jnp.exp2(scale_ref[...])
    set_tile(o_ref, jnp.sum(jnp.transpose(acc_ref[...]), axis=0, keepdims=True))
    for p in range(out_ref.shape[0]):
        out_ref[p] = o_ref[...]


def last_kernel(ratio_ref, qa_ref, qb_ref, src_ref, scale_ref, out_ref, pot_ref, r_ref, s_ref):
    chunk = s_ref.shape[1]
    ratio = ratio_ref[0]
    for p in range(1, ratio_ref.shape[0]):
        ratio = ratio + ratio_ref[p]
    ratio = row_of(ratio)
    mass = src_ref[1:2, :]
    r_ref[...] = jnp.transpose(jnp.broadcast_to(mass / ratio, (128, ratio.shape[1])))
    s_ref[0:1, :] = LN2 * (src_ref[0:1, :] - jnp.log2(ratio))
    rows = pot_ref.shape[1]
    mine = pl.multiple_of(lax.axis_index("x") * rows, rows)
    pot_ref[...] = s_ref[0:1, pl.ds(mine, rows)]
    for half, q_ref in enumerate((qa_ref, qb_ref)):

        def step(k, carry, half=half, q_ref=q_ref):
            cols = pl.ds(pl.multiple_of(k * chunk, chunk), chunk)
            accs = [jnp.zeros((8, 128), F32)] * (chunk // 128)
            for h in range(0, r_ref.shape[0], 8):
                r = r_ref[h : h + 8, :]
                q = q_ref[h : h + 8, cols]
                for j in range(chunk // 128):
                    accs[j] = accs[j] + q[:, 128 * j : 128 * j + 128] * r
            acc = jnp.concatenate(accs, axis=1)
            s_ref[pl.ds(4 * half + k, 1), :] = jnp.sum(acc, axis=0, keepdims=True)
            return carry

        lax.fori_loop(0, 4, step, 0)
    lane = lax.broadcasted_iota(jnp.int32, (1, 128), 1)
    extra = jnp.where(lane == 0, jnp.sum(mass), jnp.sum(ratio))
    s_ref[...] = s_ref[...] * scale_ref[...]
    for k in range(8):
        row = s_ref[k : k + 1, :]
        for p in range(Z):
            out_ref[p, :, k * chunk : (k + 1) * chunk] = row
    for p in range(Z):
        out_ref[p, :, 8 * chunk : 8 * chunk + 128] = extra


def end_kernel(cols_ref, log_ref, pot_ref, out_ref, src_hbm, src_ref, sem, o_ref, s_ref):
    chunk = log_ref.shape[1]
    def over_z(lanes):
        return functools.reduce(jnp.add, [cols_ref[z, :, lanes] for z in range(Z)])

    sums = jnp.log(over_z(slice(8 * chunk, 8 * chunk + 128)))
    log_src, log_tgt = sums[:, 0:1], sums[:, 1:2]
    src_ref[...] = pot_ref[...] + (2.0 * log_tgt - log_src)
    move = pltpu.make_async_copy(src_ref, src_hbm, sem)
    move.start()
    for k in range(8):
        s_ref[k : k + 1, :] = over_z(slice(k * chunk, (k + 1) * chunk))
    total = s_ref[...]
    pot = -LN2 * (jnp.log2(total) + log_ref[...]) + 2.0 * (log_src - log_tgt)
    per = chunk // 128
    for k in range(8):
        for s in range(per):
            o_ref[per * k + s : per * k + s + 1, :] = pot[k : k + 1, 128 * s : 128 * s + 128]
    for p in range(X):
        out_ref[p] = o_ref[...]
    move.wait()


def kernel_call(body, out_shape, scratch, args, space=pltpu.VMEM, megabytes=8):
    vmem = pl.BlockSpec(memory_space=pltpu.VMEM)
    return pl.pallas_call(
        body,
        out_shape=[
            jax.ShapeDtypeStruct(s, F32) if isinstance(s, tuple) else s for s in out_shape
        ],
        in_specs=[pl.BlockSpec(memory_space=space)] * len(args),
        out_specs=[vmem] * len(out_shape),
        scratch_shapes=scratch,
        compiler_params=pltpu.CompilerParams(vmem_limit_bytes=megabytes * 2**20),
    )(*args)


def trade(v, axes):
    return lax.all_to_all(v, axes, 0, 0)


def on_device(src_points, tgt_points, src_mass, tgt_mass):
    rows = src_points.shape[1]
    cols = tgt_points.shape[1]
    nsrc = rows * X
    ntgt = cols // X
    chunk = ntgt // 8

    first, share, log_mass = kernel_call(
        row_kernel,
        [(GROUP, 4, 128), jax.ShapeDtypeStruct((48, ntgt), BF16), (1, ntgt)],
        [
            pltpu.VMEM((3, rows), F32),
            pltpu.VMEM((1, rows), F32),
            pltpu.VMEM((3, cols), F32),
            pltpu.VMEM((1, cols), F32),
            pltpu.SemaphoreType.DMA((6,)),
            pltpu.VMEM((8, rows), F32),
            pltpu.VMEM((8, cols), F32),
            pltpu.VMEM((48, cols), BF16),
            pltpu.VMEM((4, 128), F32),
        ],
        [
            pltpu.with_memory_space_constraint(v, pltpu.HBM)
            for v in (src_points, src_mass.reshape(1, rows), tgt_points, tgt_mass.reshape(1, cols))
        ],
        space=pltpu.HBM,
        megabytes=50,
    )
    first = trade(first, ("x", "y", "c"))
    half = pltpu.VMEM((nsrc, ntgt // 2), F32)
    *q, logs, shift, src_rows = kernel_call(
        col_kernel,
        [half, half, (Z, 8, chunk), (8, chunk), (8, nsrc)],
        [
            pltpu.VMEM((8, nsrc), F32),
            pltpu.VMEM((8, chunk), F32),
        ],
        (first, share),
    )
    q = [pltpu.with_memory_space_constraint(v, pltpu.VMEM) for v in q]
    logs = trade(logs, "z")
    ratio, scale, log_col = kernel_call(
        mid_kernel,
        [(GROUP, 8, 128), (8, chunk), (8, chunk)],
        [pltpu.VMEM((nsrc, 128), F32), pltpu.VMEM((8, 128), F32)],
        (logs, *q, shift, log_mass),
        megabytes=4,
    )
    ratio = trade(ratio, ("x", "y", "c"))
    col_sums, pot = kernel_call(
        last_kernel,
        [(Z, 1, ntgt + 128), (1, rows)],
        [pltpu.VMEM((nsrc, 128), F32), pltpu.VMEM((8, chunk), F32)],
        (ratio, *q, src_rows, scale),
        megabytes=4,
    )
    col_sums = trade(col_sums, "z")
    vmem = pl.BlockSpec(memory_space=pltpu.VMEM)
    tgt_pot, src_pot = pl.pallas_call(
        end_kernel,
        out_shape=[
            jax.ShapeDtypeStruct((X, ntgt // 128, 128), F32),
            pltpu.HBM((1, rows), F32),
        ],
        in_specs=[vmem] * 3,
        out_specs=[vmem, pl.BlockSpec(memory_space=pltpu.HBM)],
        scratch_shapes=[
            pltpu.VMEM((1, rows), F32),
            pltpu.SemaphoreType.DMA,
            pltpu.VMEM((ntgt // 128, 128), F32),
            pltpu.VMEM((8, chunk), F32),
        ],
        compiler_params=pltpu.CompilerParams(vmem_limit_bytes=4 * 2**20),
    )(col_sums, log_col, pot)
    return (src_pot.reshape(rows), trade(tgt_pot, "x").reshape(cols))


def solution(mesh):
    fine = Mesh(mesh.devices.reshape(Z, X, Y, C), ("z", "x", "y", "c"))
    row, col = ("z", "x"), ("y", "c")
    placed = (P(None, row), P(None, col), P(row), P(col))
    return jax.shard_map(
        on_device, mesh=fine, in_specs=placed, out_specs=(P(row), P(col)), check_vma=False
    )
```

```python
import functools
import math

import jax
import jax.numpy as jnp
from jax import lax
from jax.experimental import pallas as pl
from jax.experimental.pallas import tpu as pltpu
from jax.sharding import Mesh, PartitionSpec as P

EPSILON = 0.01
LN2 = math.log(2.0)
SCALE = 1.0 / (EPSILON * LN2)
CENTER = 0.5
FLOOR1 = 2.0**-60
FLOOR2 = 2.0**-40
BF16 = jnp.bfloat16
F32 = jnp.float32

Z, X, Y, C = 8, 4, 4, 2
NCOL = Y * C
GROUP = X * NCOL


def pieces(v):
    p1 = v.astype(BF16).astype(F32)
    r = v - p1
    p2 = r.astype(BF16).astype(F32)
    p3 = (r - p2).astype(BF16).astype(F32)
    return p1, p2, p3


def stack_src(v):
    p1, p2, p3 = pieces(v)
    return [
        jnp.concatenate([p1, p2], axis=0),
        jnp.concatenate([p3, p1], axis=0),
        jnp.concatenate([p2, p1], axis=0),
    ]


def stack_tgt(v):
    p1, p2, p3 = pieces(v)
    return [
        jnp.concatenate([p1, p1], axis=0),
        jnp.concatenate([p1, p2], axis=0),
        jnp.concatenate([p2, p3], axis=0),
    ]


def scores(lhs, rhs):
    return lax.dot_general(
        lhs, rhs, (((1,), (0,)), ((), ())), preferred_element_type=F32
    )


def fold(v, op):
    out = v[:, 0:128]
    for k in range(128, v.shape[1], 128):
        out = op(out, v[:, k : k + 128])
    return out


def src_side(x_ref, use_mass):
    n = x_ref.shape[1]
    x_ref[0:3, :] = x_ref[0:3, :] - CENTER
    a, b, c = x_ref[0:1, :], x_ref[1:2, :], x_ref[2:3, :]
    x_ref[3:4, :] = x_ref[3:4, :] - SCALE * (a * a + b * b + c * c)
    x_ref[0:3, :] = x_ref[0:3, :] * (2.0 * SCALE)
    x_ref[4:7, :] = jnp.ones((3, n), F32)
    x_ref[7:8, :] = jnp.full((1, n), use_mass, F32)
    stacked = jnp.concatenate(stack_src(x_ref[...]), axis=0)
    return jnp.transpose(stacked).astype(BF16)


def row_of(tile):
    return jnp.concatenate([tile[s : s + 1, :] for s in range(tile.shape[0])], axis=1)


def set_tile(ref, row):
    for s in range(row.shape[1] // 128):
        ref[s : s + 1, :] = row[:, 128 * s : 128 * s + 128]


def row_kernel(
    src_hbm,
    src_mass_hbm,
    tgt_hbm,
    mass_hbm,
    out_ref,
    share_ref,
    log_ref,
    src_ref,
    src_mass_ref,
    tgt_ref,
    mass_ref,
    sem,
    x_ref,
    t_ref,
    w_ref,
    o_ref,
):
    n = tgt_ref.shape[1]
    rows = src_ref.shape[1]
    parts = [slice(0, n // 8), slice(n // 8, n)]
    pairs = [(src_hbm, src_ref), (src_mass_hbm, src_mass_ref)]
    for lanes in parts:
        pairs.append((tgt_hbm.at[:, lanes], tgt_ref.at[:, lanes]))
        pairs.append((mass_hbm.at[:, lanes], mass_ref.at[:, lanes]))
    moves = [pltpu.make_async_copy(a, b, sem.at[i]) for i, (a, b) in enumerate(pairs)]
    for move in moves:
        move.start()
    moves[0].wait()
    x_ref[0:3, :] = src_ref[...]
    x_ref[3:4, :] = jnp.zeros((1, rows), F32)
    lhs = src_side(x_ref, 1.0)
    moves[1].wait()
    acc = jnp.zeros((rows, 128), F32)
    for k, lanes in enumerate(parts):
        moves[2 * k + 2].wait()
        moves[2 * k + 3].wait()
        points = tgt_ref[:, lanes] - CENTER
        t_ref[0:3, lanes] = points
        t_ref[3:4, lanes] = jnp.ones((1, points.shape[1]), F32)
        t_ref[4:7, lanes] = points * points * -SCALE
        t_ref[7:8, lanes] = jnp.log2(mass_ref[:, lanes])
        for i, part in enumerate(stack_tgt(t_ref[:, lanes])):
            w_ref[16 * i : 16 * i + 16, lanes] = part.astype(BF16)
        acc = acc + fold(jnp.exp2(scores(lhs, w_ref[:, lanes])), jnp.add)
    total = jnp.sum(jnp.transpose(acc), axis=0, keepdims=True)
    set_tile(o_ref, jnp.log2(total))

    @pl.when(jnp.min(total) < FLOOR1)
    def _():
        small = 1024

        def block(k):
            return scores(lhs, w_ref[:, pl.ds(pl.multiple_of(k * small, small), small)])

        def top(k, m):
            return jnp.maximum(m, fold(block(k), jnp.maximum))

        m = lax.fori_loop(0, n // small, top, jnp.full((rows, 128), -jnp.inf, F32))
        m = jnp.max(m, axis=1, keepdims=True)

        def shifted(k, acc):
            return acc + fold(jnp.exp2(block(k) - m), jnp.add)

        acc = lax.fori_loop(0, n // small, shifted, jnp.zeros((rows, 128), F32))
        total = jnp.sum(jnp.transpose(acc), axis=0, keepdims=True)
        peak = jnp.transpose(jnp.broadcast_to(m, (rows, 128)))[0:1, :]
        set_tile(o_ref, jnp.log2(total) + peak)

    col = lax.axis_index("y") * C + lax.axis_index("c")
    info = src_mass_ref[...]
    for d in range(3):
        info = jnp.where(col == d, src_ref[d : d + 1, :], info)
    for s in range(rows // 128):
        o_ref[2 + s : 3 + s, :] = info[:, 128 * s : 128 * s + 128]
    for p in range(out_ref.shape[0]):
        out_ref[p] = o_ref[...]
    share = share_ref.shape[1]
    mine = pl.ds(pl.multiple_of(lax.axis_index("x") * share, share), share)
    share_ref[...] = w_ref[:, mine]
    log_ref[...] = t_ref[7:8, mine]


def set_src(first_ref, x_ref):
    logs, masses = [], []
    for x in range(X):
        parts = [first_ref[x * NCOL + q] for q in range(NCOL)]
        peak = functools.reduce(jnp.maximum, parts)
        total = functools.reduce(jnp.add, [jnp.exp2(v - peak) for v in parts])
        log_sum = peak + jnp.log2(total)
        for s in range(2):
            lanes = slice(256 * x + 128 * s, 256 * x + 128 * s + 128)
            for d in range(3):
                x_ref[d : d + 1, lanes] = parts[d][2 + s : 3 + s, :]
            logs.append(log_sum[s : s + 1, :])
            masses.append(parts[3][2 + s : 3 + s, :])
    mass = jnp.concatenate(masses, axis=1)
    return jnp.log2(mass), mass, jnp.concatenate(logs, axis=1)


def col_kernel(
    first_ref, w_ref, qa_ref, qb_ref, out_ref, shift_ref, src_ref, x_ref, s_ref
):
    chunk = s_ref.shape[1]
    log_mass, mass, log_sum = set_src(first_ref, x_ref)
    src_ref[...] = jnp.zeros(src_ref.shape, F32)
    src_ref[0:1, :] = log_mass - log_sum
    src_ref[1:2, :] = mass
    x_ref[3:4, :] = log_mass - log_sum
    lhs = src_side(x_ref, 0.0)

    def block(k):
        return scores(lhs, w_ref[:, pl.ds(pl.multiple_of(k * chunk, chunk), chunk)])

    for half, q_ref in enumerate((qa_ref, qb_ref)):

        def step(k, carry, half=half, q_ref=q_ref):
            q = jnp.exp2(block(4 * half + k))
            q_ref[:, pl.ds(pl.multiple_of(k * chunk, chunk), chunk)] = q
            s_ref[pl.ds(4 * half + k, 1), :] = jnp.sum(q, axis=0, keepdims=True)
            return carry

        lax.fori_loop(0, 4, step, 0, unroll=4)
    total = s_ref[...]
    s_ref[...] = jnp.log2(total)
    shift_ref[...] = jnp.zeros(shift_ref.shape, F32)

    @pl.when(jnp.min(total) < FLOOR2)
    def _():
        for half, q_ref in enumerate((qa_ref, qb_ref)):

            def shifted(k, carry, half=half, q_ref=q_ref):
                s = block(4 * half + k)
                m = jnp.max(s, axis=0, keepdims=True)
                q = jnp.exp2(s - m)
                q_ref[:, pl.ds(pl.multiple_of(k * chunk, chunk), chunk)] = q
                l = jnp.sum(q, axis=0, keepdims=True)
                s_ref[pl.ds(4 * half + k, 1), :] = m + jnp.log2(l)
                shift_ref[pl.ds(4 * half + k, 1), :] = m
                return carry

            lax.fori_loop(0, 4, shifted, 0)

    for p in range(Z):
        out_ref[p] = s_ref[...]


def mid_kernel(
    cols_ref, qa_ref, qb_ref, shift_ref, mass_ref, out_ref, scale_ref, log_ref, acc_ref, o_ref
):
    chunk = log_ref.shape[1]
    parts = [cols_ref[z] for z in range(Z)]
    peak = functools.reduce(jnp.maximum, parts)
    total = functools.reduce(jnp.add, [jnp.exp2(v - peak) for v in parts])
    log_col = peak + jnp.log2(total)
    log_ref[...] = log_col
    scale_ref[...] = shift_ref[...] - log_col
    acc_ref[...] = jnp.zeros(acc_ref.shape, F32)

    for half, q_ref in enumerate((qa_ref, qb_ref)):

        def step(k, carry, half=half, q_ref=q_ref):
            weights = []
            for e in range(2):
                row = 4 * half + 2 * k + e
                log_mass = mass_ref[:, pl.ds(pl.multiple_of(row * chunk, chunk), chunk)]
                w = jnp.exp2(log_mass + scale_ref[pl.ds(row, 1), :])
                for j in range(0, chunk, 128):
                    weights.append(jnp.broadcast_to(w[:, j : j + 128], (8, 128)))
            cols = pl.ds(pl.multiple_of(2 * k * chunk, 2 * chunk), 2 * chunk)
            for h in range(0, acc_ref.shape[0], 8):
                q = q_ref[h : h + 8, cols]
                terms = [q[:, 128 * j : 128 * j + 128] * w for j, w in enumerate(weights)]
                while len(terms) > 1:
                    terms = [u + v for u, v in zip(terms[::2], terms[1::2])]
                acc_ref[h : h + 8, :] += terms[0]
            return carry

        lax.fori_loop(0, 2, step, 0)
    scale_ref[...] = jnp.exp2(scale_ref[...])
    set_tile(o_ref, jnp.sum(jnp.transpose(acc_ref[...]), axis=0, keepdims=True))
    for p in range(out_ref.shape[0]):
        out_ref[p] = o_ref[...]


def last_kernel(ratio_ref, qa_ref, qb_ref, src_ref, scale_ref, out_ref, pot_ref, r_ref, s_ref):
    chunk = s_ref.shape[1]
    ratio = ratio_ref[0]
    for p in range(1, ratio_ref.shape[0]):
        ratio = ratio + ratio_ref[p]
    ratio = row_of(ratio)
    mass = src_ref[1:2, :]
    r_ref[...] = jnp.transpose(jnp.broadcast_to(mass / ratio, (128, ratio.shape[1])))
    s_ref[0:1, :] = LN2 * (src_ref[0:1, :] - jnp.log2(ratio))
    rows = pot_ref.shape[1]
    mine = pl.multiple_of(lax.axis_index("x") * rows, rows)
    pot_ref[...] = s_ref[0:1, pl.ds(mine, rows)]
    for half, q_ref in enumerate((qa_ref, qb_ref)):

        def step(k, carry, half=half, q_ref=q_ref):
            cols = pl.ds(pl.multiple_of(k * chunk, chunk), chunk)
            accs = [jnp.zeros((8, 128), F32)] * (chunk // 128)
            for h in range(0, r_ref.shape[0], 8):
                r = r_ref[h : h + 8, :]
                q = q_ref[h : h + 8, cols]
                for j in range(chunk // 128):
                    accs[j] = accs[j] + q[:, 128 * j : 128 * j + 128] * r
            acc = jnp.concatenate(accs, axis=1)
            s_ref[pl.ds(4 * half + k, 1), :] = jnp.sum(acc, axis=0, keepdims=True)
            return carry

        lax.fori_loop(0, 4, step, 0)
    lane = lax.broadcasted_iota(jnp.int32, (1, 128), 1)
    extra = jnp.where(lane == 0, jnp.sum(mass), jnp.sum(ratio))
    s_ref[...] = s_ref[...] * scale_ref[...]
    for k in range(8):
        row = s_ref[k : k + 1, :]
        for p in range(Z):
            out_ref[p, :, k * chunk : (k + 1) * chunk] = row
    for p in range(Z):
        out_ref[p, :, 8 * chunk : 8 * chunk + 128] = extra


def end_kernel(cols_ref, log_ref, pot_ref, out_ref, src_hbm, src_ref, sem, o_ref, s_ref):
    chunk = log_ref.shape[1]
    def over_z(lanes):
        return functools.reduce(jnp.add, [cols_ref[z, :, lanes] for z in range(Z)])

    sums = jnp.log(over_z(slice(8 * chunk, 8 * chunk + 128)))
    log_src, log_tgt = sums[:, 0:1], sums[:, 1:2]
    src_ref[...] = pot_ref[...] + (2.0 * log_tgt - log_src)
    move = pltpu.make_async_copy(src_ref, src_hbm, sem)
    move.start()
    for k in range(8):
        s_ref[k : k + 1, :] = over_z(slice(k * chunk, (k + 1) * chunk))
    total = s_ref[...]
    pot = -LN2 * (jnp.log2(total) + log_ref[...]) + 2.0 * (log_src - log_tgt)
    per = chunk // 128
    for k in range(8):
        for s in range(per):
            o_ref[per * k + s : per * k + s + 1, :] = pot[k : k + 1, 128 * s : 128 * s + 128]
    for p in range(X):
        out_ref[p] = o_ref[...]
    move.wait()


def kernel_call(body, out_shape, scratch, args, space=pltpu.VMEM, megabytes=8):
    vmem = pl.BlockSpec(memory_space=pltpu.VMEM)
    return pl.pallas_call(
        body,
        out_shape=[
            jax.ShapeDtypeStruct(s, F32) if isinstance(s, tuple) else s for s in out_shape
        ],
        in_specs=[pl.BlockSpec(memory_space=space)] * len(args),
        out_specs=[vmem] * len(out_shape),
        scratch_shapes=scratch,
        compiler_params=pltpu.CompilerParams(vmem_limit_bytes=megabytes * 2**20),
    )(*args)


def trade(v, axes):
    return lax.all_to_all(v, axes, 0, 0)


def on_device(src_points, tgt_points, src_mass, tgt_mass):
    rows = src_points.shape[1]
    cols = tgt_points.shape[1]
    nsrc = rows * X
    ntgt = cols // X
    chunk = ntgt // 8

    first, share, log_mass = kernel_call(
        row_kernel,
        [(GROUP, 4, 128), jax.ShapeDtypeStruct((48, ntgt), BF16), (1, ntgt)],
        [
            pltpu.VMEM((3, rows), F32),
            pltpu.VMEM((1, rows), F32),
            pltpu.VMEM((3, cols), F32),
            pltpu.VMEM((1, cols), F32),
            pltpu.SemaphoreType.DMA((6,)),
            pltpu.VMEM((8, rows), F32),
            pltpu.VMEM((8, cols), F32),
            pltpu.VMEM((48, cols), BF16),
            pltpu.VMEM((4, 128), F32),
        ],
        [
            pltpu.with_memory_space_constraint(v, pltpu.HBM)
            for v in (src_points, src_mass.reshape(1, rows), tgt_points, tgt_mass.reshape(1, cols))
        ],
        space=pltpu.HBM,
        megabytes=50,
    )
    first = trade(first, ("x", "y", "c"))
    half = pltpu.VMEM((nsrc, ntgt // 2), F32)
    *q, logs, shift, src_rows = kernel_call(
        col_kernel,
        [half, half, (Z, 8, chunk), (8, chunk), (8, nsrc)],
        [
            pltpu.VMEM((8, nsrc), F32),
            pltpu.VMEM((8, chunk), F32),
        ],
        (first, share),
    )
    q = [pltpu.with_memory_space_constraint(v, pltpu.VMEM) for v in q]
    logs = trade(logs, "z")
    ratio, scale, log_col = kernel_call(
        mid_kernel,
        [(GROUP, 8, 128), (8, chunk), (8, chunk)],
        [pltpu.VMEM((nsrc, 128), F32), pltpu.VMEM((8, 128), F32)],
        (logs, *q, shift, log_mass),
        megabytes=4,
    )
    ratio = trade(ratio, ("x", "y", "c"))
    col_sums, pot = kernel_call(
        last_kernel,
        [(Z, 1, ntgt + 128), (1, rows)],
        [pltpu.VMEM((nsrc, 128), F32), pltpu.VMEM((8, chunk), F32)],
        (ratio, *q, src_rows, scale),
        megabytes=4,
    )
    col_sums = trade(col_sums, "z")
    vmem = pl.BlockSpec(memory_space=pltpu.VMEM)
    tgt_pot, src_pot = pl.pallas_call(
        end_kernel,
        out_shape=[
            jax.ShapeDtypeStruct((X, ntgt // 128, 128), F32),
            pltpu.HBM((1, rows), F32),
        ],
        in_specs=[vmem] * 3,
        out_specs=[vmem, pl.BlockSpec(memory_space=pltpu.HBM)],
        scratch_shapes=[
            pltpu.VMEM((1, rows), F32),
            pltpu.SemaphoreType.DMA,
            pltpu.VMEM((ntgt // 128, 128), F32),
            pltpu.VMEM((8, chunk), F32),
        ],
        compiler_params=pltpu.CompilerParams(vmem_limit_bytes=4 * 2**20),
    )(col_sums, log_col, pot)
    return (src_pot.reshape(rows), trade(tgt_pot, "x").reshape(cols))


def solution(mesh):
    fine = Mesh(mesh.devices.reshape(Z, X, Y, C), ("z", "x", "y", "c"))
    row, col = ("z", "x"), ("y", "c")
    placed = (P(None, row), P(None, col), P(row), P(col))
    return jax.shard_map(
        on_device, mesh=fine, in_specs=placed, out_specs=(P(row), P(col)), check_vma=False
    )
```

```python
import functools
import math

import jax
import jax.numpy as jnp
from jax import lax
from jax.experimental import pallas as pl
from jax.experimental.pallas import tpu as pltpu
from jax.sharding import Mesh, PartitionSpec as P

EPSILON = 0.01
LN2 = math.log(2.0)
SCALE = 1.0 / (EPSILON * LN2)
CENTER = 0.5
FLOOR1 = 2.0**-60
FLOOR2 = 2.0**-40
BF16 = jnp.bfloat16
F32 = jnp.float32

Z, X, Y, C = 8, 4, 4, 2
NCOL = Y * C
GROUP = X * NCOL


def pieces(v):
    p1 = v.astype(BF16).astype(F32)
    r = v - p1
    p2 = r.astype(BF16).astype(F32)
    p3 = (r - p2).astype(BF16).astype(F32)
    return p1, p2, p3


def stack_src(v):
    p1, p2, p3 = pieces(v)
    return [
        jnp.concatenate([p1, p2], axis=0),
        jnp.concatenate([p3, p1], axis=0),
        jnp.concatenate([p2, p1], axis=0),
    ]


def stack_tgt(v):
    p1, p2, p3 = pieces(v)
    return [
        jnp.concatenate([p1, p1], axis=0),
        jnp.concatenate([p1, p2], axis=0),
        jnp.concatenate([p2, p3], axis=0),
    ]


def scores(lhs, rhs):
    return lax.dot_general(
        lhs, rhs, (((1,), (0,)), ((), ())), preferred_element_type=F32
    )


def fold(v, op):
    out = v[:, 0:128]
    for k in range(128, v.shape[1], 128):
        out = op(out, v[:, k : k + 128])
    return out


def src_side(x_ref, use_mass):
    n = x_ref.shape[1]
    x_ref[0:3, :] = x_ref[0:3, :] - CENTER
    a, b, c = x_ref[0:1, :], x_ref[1:2, :], x_ref[2:3, :]
    x_ref[3:4, :] = x_ref[3:4, :] - SCALE * (a * a + b * b + c * c)
    x_ref[0:3, :] = x_ref[0:3, :] * (2.0 * SCALE)
    x_ref[4:7, :] = jnp.ones((3, n), F32)
    x_ref[7:8, :] = jnp.full((1, n), use_mass, F32)
    stacked = jnp.concatenate(stack_src(x_ref[...]), axis=0)
    return jnp.transpose(stacked).astype(BF16)


def row_of(tile):
    return jnp.concatenate([tile[s : s + 1, :] for s in range(tile.shape[0])], axis=1)


def set_tile(ref, row):
    for s in range(row.shape[1] // 128):
        ref[s : s + 1, :] = row[:, 128 * s : 128 * s + 128]


def row_kernel(
    src_hbm,
    src_mass_hbm,
    tgt_hbm,
    mass_hbm,
    out_ref,
    w_ref,
    log_ref,
    src_ref,
    src_mass_ref,
    tgt_ref,
    mass_ref,
    sem,
    x_ref,
    t_ref,
    o_ref,
):
    n = tgt_ref.shape[1]
    rows = src_ref.shape[1]
    parts = [slice(0, n // 8), slice(n // 8, n)]
    pairs = [(src_hbm, src_ref), (src_mass_hbm, src_mass_ref)]
    for lanes in parts:
        pairs.append((tgt_hbm.at[:, lanes], tgt_ref.at[:, lanes]))
        pairs.append((mass_hbm.at[:, lanes], mass_ref.at[:, lanes]))
    moves = [pltpu.make_async_copy(a, b, sem.at[i]) for i, (a, b) in enumerate(pairs)]
    for move in moves:
        move.start()
    moves[0].wait()
    x_ref[0:3, :] = src_ref[...]
    x_ref[3:4, :] = jnp.zeros((1, rows), F32)
    lhs = src_side(x_ref, 1.0)
    moves[1].wait()
    acc = jnp.zeros((rows, 128), F32)
    for k, lanes in enumerate(parts):
        moves[2 * k + 2].wait()
        moves[2 * k + 3].wait()
        points = tgt_ref[:, lanes] - CENTER
        t_ref[0:3, lanes] = points
        t_ref[3:4, lanes] = jnp.ones((1, points.shape[1]), F32)
        t_ref[4:7, lanes] = points * points * -SCALE
        t_ref[7:8, lanes] = jnp.log2(mass_ref[:, lanes])
        for i, part in enumerate(stack_tgt(t_ref[:, lanes])):
            w_ref[16 * i : 16 * i + 16, lanes] = part.astype(BF16)
        acc = acc + fold(jnp.exp2(scores(lhs, w_ref[:, lanes])), jnp.add)
    total = jnp.sum(jnp.transpose(acc), axis=0, keepdims=True)
    set_tile(o_ref, jnp.log2(total))

    @pl.when(jnp.min(total) < FLOOR1)
    def _():
        small = 1024

        def block(k):
            return scores(lhs, w_ref[:, pl.ds(pl.multiple_of(k * small, small), small)])

        def top(k, m):
            return jnp.maximum(m, fold(block(k), jnp.maximum))

        m = lax.fori_loop(0, n // small, top, jnp.full((rows, 128), -jnp.inf, F32))
        m = jnp.max(m, axis=1, keepdims=True)

        def shifted(k, acc):
            return acc + fold(jnp.exp2(block(k) - m), jnp.add)

        acc = lax.fori_loop(0, n // small, shifted, jnp.zeros((rows, 128), F32))
        total = jnp.sum(jnp.transpose(acc), axis=0, keepdims=True)
        peak = jnp.transpose(jnp.broadcast_to(m, (rows, 128)))[0:1, :]
        set_tile(o_ref, jnp.log2(total) + peak)

    col = lax.axis_index("y") * C + lax.axis_index("c")
    info = src_mass_ref[...]
    for d in range(3):
        info = jnp.where(col == d, src_ref[d : d + 1, :], info)
    for s in range(rows // 128):
        o_ref[2 + s : 3 + s, :] = info[:, 128 * s : 128 * s + 128]
    for p in range(out_ref.shape[0]):
        out_ref[p] = o_ref[...]
    share = log_ref.shape[1]
    log_ref[...] = t_ref[7:8, pl.ds(pl.multiple_of(lax.axis_index("x") * share, share), share)]


def set_src(first_ref, x_ref):
    logs, masses = [], []
    for x in range(X):
        parts = [first_ref[x * NCOL + q] for q in range(NCOL)]
        peak = functools.reduce(jnp.maximum, parts)
        total = functools.reduce(jnp.add, [jnp.exp2(v - peak) for v in parts])
        log_sum = peak + jnp.log2(total)
        for s in range(2):
            lanes = slice(256 * x + 128 * s, 256 * x + 128 * s + 128)
            for d in range(3):
                x_ref[d : d + 1, lanes] = parts[d][2 + s : 3 + s, :]
            logs.append(log_sum[s : s + 1, :])
            masses.append(parts[3][2 + s : 3 + s, :])
    mass = jnp.concatenate(masses, axis=1)
    return jnp.log2(mass), mass, jnp.concatenate(logs, axis=1)


def col_kernel(
    first_ref, w_ref, qa_ref, qb_ref, out_ref, shift_ref, src_ref, x_ref, s_ref
):
    chunk = s_ref.shape[1]
    log_mass, mass, log_sum = set_src(first_ref, x_ref)
    src_ref[...] = jnp.zeros(src_ref.shape, F32)
    src_ref[0:1, :] = log_mass - log_sum
    src_ref[1:2, :] = mass
    x_ref[3:4, :] = log_mass - log_sum
    lhs = src_side(x_ref, 0.0)

    begin = lax.axis_index("x") * (8 * chunk)

    def block(k):
        return scores(lhs, w_ref[:, pl.ds(pl.multiple_of(begin + k * chunk, chunk), chunk)])

    for half, q_ref in enumerate((qa_ref, qb_ref)):

        def step(k, carry, half=half, q_ref=q_ref):
            q = jnp.exp2(block(4 * half + k))
            q_ref[:, pl.ds(pl.multiple_of(k * chunk, chunk), chunk)] = q
            s_ref[pl.ds(4 * half + k, 1), :] = jnp.sum(q, axis=0, keepdims=True)
            return carry

        lax.fori_loop(0, 4, step, 0, unroll=4)
    total = s_ref[...]
    s_ref[...] = jnp.log2(total)
    shift_ref[...] = jnp.zeros(shift_ref.shape, F32)

    @pl.when(jnp.min(total) < FLOOR2)
    def _():
        for half, q_ref in enumerate((qa_ref, qb_ref)):

            def shifted(k, carry, half=half, q_ref=q_ref):
                s = block(4 * half + k)
                m = jnp.max(s, axis=0, keepdims=True)
                q = jnp.exp2(s - m)
                q_ref[:, pl.ds(pl.multiple_of(k * chunk, chunk), chunk)] = q
                l = jnp.sum(q, axis=0, keepdims=True)
                s_ref[pl.ds(4 * half + k, 1), :] = m + jnp.log2(l)
                shift_ref[pl.ds(4 * half + k, 1), :] = m
                return carry

            lax.fori_loop(0, 4, shifted, 0)

    for p in range(Z):
        out_ref[p] = s_ref[...]


def mid_kernel(
    cols_ref, qa_ref, qb_ref, shift_ref, mass_ref, out_ref, scale_ref, log_ref, acc_ref, o_ref
):
    chunk = log_ref.shape[1]
    parts = [cols_ref[z] for z in range(Z)]
    peak = functools.reduce(jnp.maximum, parts)
    total = functools.reduce(jnp.add, [jnp.exp2(v - peak) for v in parts])
    log_col = peak + jnp.log2(total)
    log_ref[...] = log_col
    scale_ref[...] = shift_ref[...] - log_col
    acc_ref[...] = jnp.zeros(acc_ref.shape, F32)

    for half, q_ref in enumerate((qa_ref, qb_ref)):

        def step(k, carry, half=half, q_ref=q_ref):
            weights = []
            for e in range(2):
                row = 4 * half + 2 * k + e
                log_mass = mass_ref[:, pl.ds(pl.multiple_of(row * chunk, chunk), chunk)]
                w = jnp.exp2(log_mass + scale_ref[pl.ds(row, 1), :])
                for j in range(0, chunk, 128):
                    weights.append(jnp.broadcast_to(w[:, j : j + 128], (8, 128)))
            cols = pl.ds(pl.multiple_of(2 * k * chunk, 2 * chunk), 2 * chunk)
            for h in range(0, acc_ref.shape[0], 8):
                q = q_ref[h : h + 8, cols]
                terms = [q[:, 128 * j : 128 * j + 128] * w for j, w in enumerate(weights)]
                while len(terms) > 1:
                    terms = [u + v for u, v in zip(terms[::2], terms[1::2])]
                acc_ref[h : h + 8, :] += terms[0]
            return carry

        lax.fori_loop(0, 2, step, 0)
    scale_ref[...] = jnp.exp2(scale_ref[...])
    set_tile(o_ref, jnp.sum(jnp.transpose(acc_ref[...]), axis=0, keepdims=True))
    for p in range(out_ref.shape[0]):
        out_ref[p] = o_ref[...]


def last_kernel(ratio_ref, qa_ref, qb_ref, src_ref, scale_ref, out_ref, pot_ref, r_ref, s_ref):
    chunk = s_ref.shape[1]
    ratio = ratio_ref[0]
    for p in range(1, ratio_ref.shape[0]):
        ratio = ratio + ratio_ref[p]
    ratio = row_of(ratio)
    mass = src_ref[1:2, :]
    r_ref[...] = jnp.transpose(jnp.broadcast_to(mass / ratio, (128, ratio.shape[1])))
    s_ref[0:1, :] = LN2 * (src_ref[0:1, :] - jnp.log2(ratio))
    rows = pot_ref.shape[1]
    mine = pl.multiple_of(lax.axis_index("x") * rows, rows)
    pot_ref[...] = s_ref[0:1, pl.ds(mine, rows)]
    for half, q_ref in enumerate((qa_ref, qb_ref)):

        def step(k, carry, half=half, q_ref=q_ref):
            cols = pl.ds(pl.multiple_of(k * chunk, chunk), chunk)
            accs = [jnp.zeros((8, 128), F32)] * (chunk // 128)
            for h in range(0, r_ref.shape[0], 8):
                r = r_ref[h : h + 8, :]
                q = q_ref[h : h + 8, cols]
                for j in range(chunk // 128):
                    accs[j] = accs[j] + q[:, 128 * j : 128 * j + 128] * r
            acc = jnp.concatenate(accs, axis=1)
            s_ref[pl.ds(4 * half + k, 1), :] = jnp.sum(acc, axis=0, keepdims=True)
            return carry

        lax.fori_loop(0, 4, step, 0)
    lane = lax.broadcasted_iota(jnp.int32, (1, 128), 1)
    extra = jnp.where(lane == 0, jnp.sum(mass), jnp.sum(ratio))
    s_ref[...] = s_ref[...] * scale_ref[...]
    for k in range(8):
        row = s_ref[k : k + 1, :]
        for p in range(Z):
            out_ref[p, :, k * chunk : (k + 1) * chunk] = row
    for p in range(Z):
        out_ref[p, :, 8 * chunk : 8 * chunk + 128] = extra


def end_kernel(cols_ref, log_ref, pot_ref, out_ref, src_hbm, src_ref, sem, o_ref, s_ref):
    chunk = log_ref.shape[1]
    def over_z(lanes):
        return functools.reduce(jnp.add, [cols_ref[z, :, lanes] for z in range(Z)])

    sums = jnp.log(over_z(slice(8 * chunk, 8 * chunk + 128)))
    log_src, log_tgt = sums[:, 0:1], sums[:, 1:2]
    src_ref[...] = pot_ref[...] + (2.0 * log_tgt - log_src)
    move = pltpu.make_async_copy(src_ref, src_hbm, sem)
    move.start()
    for k in range(8):
        s_ref[k : k + 1, :] = over_z(slice(k * chunk, (k + 1) * chunk))
    total = s_ref[...]
    pot = -LN2 * (jnp.log2(total) + log_ref[...]) + 2.0 * (log_src - log_tgt)
    per = chunk // 128
    for k in range(8):
        for s in range(per):
            o_ref[per * k + s : per * k + s + 1, :] = pot[k : k + 1, 128 * s : 128 * s + 128]
    for p in range(X):
        out_ref[p] = o_ref[...]
    move.wait()


def kernel_call(body, out_shape, scratch, args, space=pltpu.VMEM, megabytes=8):
    vmem = pl.BlockSpec(memory_space=pltpu.VMEM)
    return pl.pallas_call(
        body,
        out_shape=[
            jax.ShapeDtypeStruct(s, F32) if isinstance(s, tuple) else s for s in out_shape
        ],
        in_specs=[pl.BlockSpec(memory_space=space)] * len(args),
        out_specs=[vmem] * len(out_shape),
        scratch_shapes=scratch,
        compiler_params=pltpu.CompilerParams(vmem_limit_bytes=megabytes * 2**20),
    )(*args)


def trade(v, axes):
    return lax.all_to_all(v, axes, 0, 0)


def on_device(src_points, tgt_points, src_mass, tgt_mass):
    rows = src_points.shape[1]
    cols = tgt_points.shape[1]
    nsrc = rows * X
    ntgt = cols // X
    chunk = ntgt // 8

    first, pieces_all, log_mass = kernel_call(
        row_kernel,
        [(GROUP, 4, 128), pltpu.VMEM((48, cols), BF16), (1, ntgt)],
        [
            pltpu.VMEM((3, rows), F32),
            pltpu.VMEM((1, rows), F32),
            pltpu.VMEM((3, cols), F32),
            pltpu.VMEM((1, cols), F32),
            pltpu.SemaphoreType.DMA((6,)),
            pltpu.VMEM((8, rows), F32),
            pltpu.VMEM((8, cols), F32),
            pltpu.VMEM((4, 128), F32),
        ],
        [
            pltpu.with_memory_space_constraint(v, pltpu.HBM)
            for v in (src_points, src_mass.reshape(1, rows), tgt_points, tgt_mass.reshape(1, cols))
        ],
        space=pltpu.HBM,
        megabytes=50,
    )
    first = trade(first, ("x", "y", "c"))
    half = pltpu.VMEM((nsrc, ntgt // 2), F32)
    *q, logs, shift, src_rows = kernel_call(
        col_kernel,
        [half, half, (Z, 8, chunk), (8, chunk), (8, nsrc)],
        [
            pltpu.VMEM((8, nsrc), F32),
            pltpu.VMEM((8, chunk), F32),
        ],
        (first, pltpu.with_memory_space_constraint(pieces_all, pltpu.VMEM)),
    )
    q = [pltpu.with_memory_space_constraint(v, pltpu.VMEM) for v in q]
    logs = trade(logs, "z")
    ratio, scale, log_col = kernel_call(
        mid_kernel,
        [(GROUP, 8, 128), (8, chunk), (8, chunk)],
        [pltpu.VMEM((nsrc, 128), F32), pltpu.VMEM((8, 128), F32)],
        (logs, *q, shift, log_mass),
        megabytes=4,
    )
    ratio = trade(ratio, ("x", "y", "c"))
    col_sums, pot = kernel_call(
        last_kernel,
        [(Z, 1, ntgt + 128), (1, rows)],
        [pltpu.VMEM((nsrc, 128), F32), pltpu.VMEM((8, chunk), F32)],
        (ratio, *q, src_rows, scale),
        megabytes=4,
    )
    col_sums = trade(col_sums, "z")
    vmem = pl.BlockSpec(memory_space=pltpu.VMEM)
    tgt_pot, src_pot = pl.pallas_call(
        end_kernel,
        out_shape=[
            jax.ShapeDtypeStruct((X, ntgt // 128, 128), F32),
            pltpu.HBM((1, rows), F32),
        ],
        in_specs=[vmem] * 3,
        out_specs=[vmem, pl.BlockSpec(memory_space=pltpu.HBM)],
        scratch_shapes=[
            pltpu.VMEM((1, rows), F32),
            pltpu.SemaphoreType.DMA,
            pltpu.VMEM((ntgt // 128, 128), F32),
            pltpu.VMEM((8, chunk), F32),
        ],
        compiler_params=pltpu.CompilerParams(vmem_limit_bytes=4 * 2**20),
    )(col_sums, log_col, pot)
    return (src_pot.reshape(rows), trade(tgt_pot, "x").reshape(cols))


def solution(mesh):
    fine = Mesh(mesh.devices.reshape(Z, X, Y, C), ("z", "x", "y", "c"))
    row, col = ("z", "x"), ("y", "c")
    placed = (P(None, row), P(None, col), P(row), P(col))
    return jax.shard_map(
        on_device, mesh=fine, in_specs=placed, out_specs=(P(row), P(col)), check_vma=False
    )
```

```python
import functools
import math

import jax
import jax.numpy as jnp
from jax import lax
from jax.experimental import pallas as pl
from jax.experimental.pallas import tpu as pltpu
from jax.sharding import Mesh, PartitionSpec as P

EPSILON = 0.01
LN2 = math.log(2.0)
SCALE = 1.0 / (EPSILON * LN2)
CENTER = 0.5
FLOOR1 = 2.0**-60
FLOOR2 = 2.0**-40
BF16 = jnp.bfloat16
F32 = jnp.float32

Z, X, Y, C = 8, 4, 4, 2
NCOL = Y * C
GROUP = X * NCOL


def pieces(v):
    p1 = v.astype(BF16).astype(F32)
    r = v - p1
    p2 = r.astype(BF16).astype(F32)
    p3 = (r - p2).astype(BF16).astype(F32)
    return p1, p2, p3


def stack_src(v):
    p1, p2, p3 = pieces(v)
    return [
        jnp.concatenate([p1, p2], axis=0),
        jnp.concatenate([p3, p1], axis=0),
        jnp.concatenate([p2, p1], axis=0),
    ]


def stack_tgt(v):
    p1, p2, p3 = pieces(v)
    return [
        jnp.concatenate([p1, p1], axis=0),
        jnp.concatenate([p1, p2], axis=0),
        jnp.concatenate([p2, p3], axis=0),
    ]


def scores(lhs, rhs):
    return lax.dot_general(
        lhs, rhs, (((1,), (0,)), ((), ())), preferred_element_type=F32
    )


def fold(v, op):
    out = v[:, 0:128]
    for k in range(128, v.shape[1], 128):
        out = op(out, v[:, k : k + 128])
    return out


def src_side(x_ref, use_mass):
    n = x_ref.shape[1]
    x_ref[0:3, :] = x_ref[0:3, :] - CENTER
    a, b, c = x_ref[0:1, :], x_ref[1:2, :], x_ref[2:3, :]
    x_ref[3:4, :] = x_ref[3:4, :] - SCALE * (a * a + b * b + c * c)
    x_ref[0:3, :] = x_ref[0:3, :] * (2.0 * SCALE)
    x_ref[4:7, :] = jnp.ones((3, n), F32)
    x_ref[7:8, :] = jnp.full((1, n), use_mass, F32)
    stacked = jnp.concatenate(stack_src(x_ref[...]), axis=0)
    return jnp.transpose(stacked).astype(BF16)


def row_of(tile):
    return jnp.concatenate([tile[s : s + 1, :] for s in range(tile.shape[0])], axis=1)


def set_tile(ref, row):
    for s in range(row.shape[1] // 128):
        ref[s : s + 1, :] = row[:, 128 * s : 128 * s + 128]


def row_kernel(
    src_hbm,
    src_mass_hbm,
    tgt_hbm,
    mass_hbm,
    out_ref,
    w_ref,
    log_ref,
    src_ref,
    src_mass_ref,
    tgt_ref,
    mass_ref,
    sem,
    x_ref,
    t_ref,
    o_ref,
):
    n = tgt_ref.shape[1]
    rows = src_ref.shape[1]
    parts = [slice(0, n // 8), slice(n // 8, n)]
    pairs = [(src_hbm, src_ref), (src_mass_hbm, src_mass_ref)]
    for lanes in parts:
        pairs.append((tgt_hbm.at[:, lanes], tgt_ref.at[:, lanes]))
        pairs.append((mass_hbm.at[:, lanes], mass_ref.at[:, lanes]))
    moves = [pltpu.make_async_copy(a, b, sem.at[i]) for i, (a, b) in enumerate(pairs)]
    for i in (2, 3, 0, 4, 5, 1):
        moves[i].start()
    moves[0].wait()
    x_ref[0:3, :] = src_ref[...]
    x_ref[3:4, :] = jnp.zeros((1, rows), F32)
    lhs = src_side(x_ref, 1.0)
    moves[1].wait()
    acc = jnp.zeros((rows, 128), F32)
    for k, lanes in enumerate(parts):
        moves[2 * k + 2].wait()
        moves[2 * k + 3].wait()
        points = tgt_ref[:, lanes] - CENTER
        t_ref[0:3, lanes] = points
        t_ref[3:4, lanes] = jnp.ones((1, points.shape[1]), F32)
        t_ref[4:7, lanes] = points * points * -SCALE
        t_ref[7:8, lanes] = jnp.log2(mass_ref[:, lanes])
        for i, part in enumerate(stack_tgt(t_ref[:, lanes])):
            w_ref[16 * i : 16 * i + 16, lanes] = part.astype(BF16)
        acc = acc + fold(jnp.exp2(scores(lhs, w_ref[:, lanes])), jnp.add)
    total = jnp.sum(jnp.transpose(acc), axis=0, keepdims=True)
    set_tile(o_ref, jnp.log2(total))

    @pl.when(jnp.min(total) < FLOOR1)
    def _():
        small = 1024

        def block(k):
            return scores(lhs, w_ref[:, pl.ds(pl.multiple_of(k * small, small), small)])

        def top(k, m):
            return jnp.maximum(m, fold(block(k), jnp.maximum))

        m = lax.fori_loop(0, n // small, top, jnp.full((rows, 128), -jnp.inf, F32))
        m = jnp.max(m, axis=1, keepdims=True)

        def shifted(k, acc):
            return acc + fold(jnp.exp2(block(k) - m), jnp.add)

        acc = lax.fori_loop(0, n // small, shifted, jnp.zeros((rows, 128), F32))
        total = jnp.sum(jnp.transpose(acc), axis=0, keepdims=True)
        peak = jnp.transpose(jnp.broadcast_to(m, (rows, 128)))[0:1, :]
        set_tile(o_ref, jnp.log2(total) + peak)

    col = lax.axis_index("y") * C + lax.axis_index("c")
    info = src_mass_ref[...]
    for d in range(3):
        info = jnp.where(col == d, src_ref[d : d + 1, :], info)
    for s in range(rows // 128):
        o_ref[2 + s : 3 + s, :] = info[:, 128 * s : 128 * s + 128]
    for p in range(out_ref.shape[0]):
        out_ref[p] = o_ref[...]
    share = log_ref.shape[1]
    log_ref[...] = t_ref[7:8, pl.ds(pl.multiple_of(lax.axis_index("x") * share, share), share)]


def set_src(first_ref, x_ref):
    logs, masses = [], []
    for x in range(X):
        parts = [first_ref[x * NCOL + q] for q in range(NCOL)]
        peak = functools.reduce(jnp.maximum, parts)
        total = functools.reduce(jnp.add, [jnp.exp2(v - peak) for v in parts])
        log_sum = peak + jnp.log2(total)
        for s in range(2):
            lanes = slice(256 * x + 128 * s, 256 * x + 128 * s + 128)
            for d in range(3):
                x_ref[d : d + 1, lanes] = parts[d][2 + s : 3 + s, :]
            logs.append(log_sum[s : s + 1, :])
            masses.append(parts[3][2 + s : 3 + s, :])
    mass = jnp.concatenate(masses, axis=1)
    return jnp.log2(mass), mass, jnp.concatenate(logs, axis=1)


def col_kernel(
    first_ref, w_ref, qa_ref, qb_ref, out_ref, shift_ref, src_ref, x_ref, s_ref
):
    chunk = s_ref.shape[1]
    log_mass, mass, log_sum = set_src(first_ref, x_ref)
    src_ref[...] = jnp.zeros(src_ref.shape, F32)
    src_ref[0:1, :] = log_mass - log_sum
    src_ref[1:2, :] = mass
    x_ref[3:4, :] = log_mass - log_sum
    lhs = src_side(x_ref, 0.0)

    begin = lax.axis_index("x") * (8 * chunk)

    def block(k):
        return scores(lhs, w_ref[:, pl.ds(pl.multiple_of(begin + k * chunk, chunk), chunk)])

    for half, q_ref in enumerate((qa_ref, qb_ref)):

        def step(k, carry, half=half, q_ref=q_ref):
            q = jnp.exp2(block(4 * half + k))
            q_ref[:, pl.ds(pl.multiple_of(k * chunk, chunk), chunk)] = q
            s_ref[pl.ds(4 * half + k, 1), :] = jnp.sum(q, axis=0, keepdims=True)
            return carry

        lax.fori_loop(0, 4, step, 0, unroll=4)
    total = s_ref[...]
    s_ref[...] = jnp.log2(total)
    shift_ref[...] = jnp.zeros(shift_ref.shape, F32)

    @pl.when(jnp.min(total) < FLOOR2)
    def _():
        for half, q_ref in enumerate((qa_ref, qb_ref)):

            def shifted(k, carry, half=half, q_ref=q_ref):
                s = block(4 * half + k)
                m = jnp.max(s, axis=0, keepdims=True)
                q = jnp.exp2(s - m)
                q_ref[:, pl.ds(pl.multiple_of(k * chunk, chunk), chunk)] = q
                l = jnp.sum(q, axis=0, keepdims=True)
                s_ref[pl.ds(4 * half + k, 1), :] = m + jnp.log2(l)
                shift_ref[pl.ds(4 * half + k, 1), :] = m
                return carry

            lax.fori_loop(0, 4, shifted, 0)

    for p in range(Z):
        out_ref[p] = s_ref[...]


def mid_kernel(
    cols_ref, qa_ref, qb_ref, shift_ref, mass_ref, out_ref, scale_ref, log_ref, acc_ref, o_ref
):
    chunk = log_ref.shape[1]
    parts = [cols_ref[z] for z in range(Z)]
    peak = functools.reduce(jnp.maximum, parts)
    total = functools.reduce(jnp.add, [jnp.exp2(v - peak) for v in parts])
    log_col = peak + jnp.log2(total)
    log_ref[...] = log_col
    scale_ref[...] = shift_ref[...] - log_col
    acc_ref[...] = jnp.zeros(acc_ref.shape, F32)

    for half, q_ref in enumerate((qa_ref, qb_ref)):

        def step(k, carry, half=half, q_ref=q_ref):
            weights = []
            for e in range(2):
                row = 4 * half + 2 * k + e
                log_mass = mass_ref[:, pl.ds(pl.multiple_of(row * chunk, chunk), chunk)]
                w = jnp.exp2(log_mass + scale_ref[pl.ds(row, 1), :])
                for j in range(0, chunk, 128):
                    weights.append(jnp.broadcast_to(w[:, j : j + 128], (8, 128)))
            cols = pl.ds(pl.multiple_of(2 * k * chunk, 2 * chunk), 2 * chunk)
            for h in range(0, acc_ref.shape[0], 8):
                q = q_ref[h : h + 8, cols]
                terms = [q[:, 128 * j : 128 * j + 128] * w for j, w in enumerate(weights)]
                while len(terms) > 1:
                    terms = [u + v for u, v in zip(terms[::2], terms[1::2])]
                acc_ref[h : h + 8, :] += terms[0]
            return carry

        lax.fori_loop(0, 2, step, 0)
    scale_ref[...] = jnp.exp2(scale_ref[...])
    set_tile(o_ref, jnp.sum(jnp.transpose(acc_ref[...]), axis=0, keepdims=True))
    for p in range(out_ref.shape[0]):
        out_ref[p] = o_ref[...]


def last_kernel(ratio_ref, qa_ref, qb_ref, src_ref, scale_ref, out_ref, pot_ref, r_ref, s_ref):
    chunk = s_ref.shape[1]
    ratio = ratio_ref[0]
    for p in range(1, ratio_ref.shape[0]):
        ratio = ratio + ratio_ref[p]
    ratio = row_of(ratio)
    mass = src_ref[1:2, :]
    r_ref[...] = jnp.transpose(jnp.broadcast_to(mass / ratio, (128, ratio.shape[1])))
    s_ref[0:1, :] = LN2 * (src_ref[0:1, :] - jnp.log2(ratio))
    rows = pot_ref.shape[1]
    mine = pl.multiple_of(lax.axis_index("x") * rows, rows)
    pot_ref[...] = s_ref[0:1, pl.ds(mine, rows)]
    for half, q_ref in enumerate((qa_ref, qb_ref)):

        def step(k, carry, half=half, q_ref=q_ref):
            cols = pl.ds(pl.multiple_of(k * chunk, chunk), chunk)
            accs = [jnp.zeros((8, 128), F32)] * (chunk // 128)
            for h in range(0, r_ref.shape[0], 8):
                r = r_ref[h : h + 8, :]
                q = q_ref[h : h + 8, cols]
                for j in range(chunk // 128):
                    accs[j] = accs[j] + q[:, 128 * j : 128 * j + 128] * r
            acc = jnp.concatenate(accs, axis=1)
            s_ref[pl.ds(4 * half + k, 1), :] = jnp.sum(acc, axis=0, keepdims=True)
            return carry

        lax.fori_loop(0, 4, step, 0)
    lane = lax.broadcasted_iota(jnp.int32, (1, 128), 1)
    extra = jnp.where(lane == 0, jnp.sum(mass), jnp.sum(ratio))
    s_ref[...] = s_ref[...] * scale_ref[...]
    for k in range(8):
        row = s_ref[k : k + 1, :]
        for p in range(Z):
            out_ref[p, :, k * chunk : (k + 1) * chunk] = row
    for p in range(Z):
        out_ref[p, :, 8 * chunk : 8 * chunk + 128] = extra


def end_kernel(cols_ref, log_ref, pot_ref, out_ref, src_hbm, src_ref, sem, o_ref, s_ref):
    chunk = log_ref.shape[1]
    def over_z(lanes):
        return functools.reduce(jnp.add, [cols_ref[z, :, lanes] for z in range(Z)])

    sums = jnp.log(over_z(slice(8 * chunk, 8 * chunk + 128)))
    log_src, log_tgt = sums[:, 0:1], sums[:, 1:2]
    src_ref[...] = pot_ref[...] + (2.0 * log_tgt - log_src)
    move = pltpu.make_async_copy(src_ref, src_hbm, sem)
    move.start()
    for k in range(8):
        s_ref[k : k + 1, :] = over_z(slice(k * chunk, (k + 1) * chunk))
    total = s_ref[...]
    pot = -LN2 * (jnp.log2(total) + log_ref[...]) + 2.0 * (log_src - log_tgt)
    per = chunk // 128
    for k in range(8):
        for s in range(per):
            o_ref[per * k + s : per * k + s + 1, :] = pot[k : k + 1, 128 * s : 128 * s + 128]
    for p in range(X):
        out_ref[p] = o_ref[...]
    move.wait()


def kernel_call(body, out_shape, scratch, args, space=pltpu.VMEM, megabytes=8):
    vmem = pl.BlockSpec(memory_space=pltpu.VMEM)
    return pl.pallas_call(
        body,
        out_shape=[
            jax.ShapeDtypeStruct(s, F32) if isinstance(s, tuple) else s for s in out_shape
        ],
        in_specs=[pl.BlockSpec(memory_space=space)] * len(args),
        out_specs=[vmem] * len(out_shape),
        scratch_shapes=scratch,
        compiler_params=pltpu.CompilerParams(vmem_limit_bytes=megabytes * 2**20),
    )(*args)


def trade(v, axes):
    return lax.all_to_all(v, axes, 0, 0)


def on_device(src_points, tgt_points, src_mass, tgt_mass):
    rows = src_points.shape[1]
    cols = tgt_points.shape[1]
    nsrc = rows * X
    ntgt = cols // X
    chunk = ntgt // 8

    first, pieces_all, log_mass = kernel_call(
        row_kernel,
        [(GROUP, 4, 128), pltpu.VMEM((48, cols), BF16), (1, ntgt)],
        [
            pltpu.VMEM((3, rows), F32),
            pltpu.VMEM((1, rows), F32),
            pltpu.VMEM((3, cols), F32),
            pltpu.VMEM((1, cols), F32),
            pltpu.SemaphoreType.DMA((6,)),
            pltpu.VMEM((8, rows), F32),
            pltpu.VMEM((8, cols), F32),
            pltpu.VMEM((4, 128), F32),
        ],
        [
            pltpu.with_memory_space_constraint(v, pltpu.HBM)
            for v in (src_points, src_mass.reshape(1, rows), tgt_points, tgt_mass.reshape(1, cols))
        ],
        space=pltpu.HBM,
        megabytes=50,
    )
    first = trade(first, ("x", "y", "c"))
    half = pltpu.VMEM((nsrc, ntgt // 2), F32)
    *q, logs, shift, src_rows = kernel_call(
        col_kernel,
        [half, half, (Z, 8, chunk), (8, chunk), (8, nsrc)],
        [
            pltpu.VMEM((8, nsrc), F32),
            pltpu.VMEM((8, chunk), F32),
        ],
        (first, pltpu.with_memory_space_constraint(pieces_all, pltpu.VMEM)),
    )
    q = [pltpu.with_memory_space_constraint(v, pltpu.VMEM) for v in q]
    logs = trade(logs, "z")
    ratio, scale, log_col = kernel_call(
        mid_kernel,
        [(GROUP, 8, 128), (8, chunk), (8, chunk)],
        [pltpu.VMEM((nsrc, 128), F32), pltpu.VMEM((8, 128), F32)],
        (logs, *q, shift, log_mass),
        megabytes=4,
    )
    ratio = trade(ratio, ("x", "y", "c"))
    col_sums, pot = kernel_call(
        last_kernel,
        [(Z, 1, ntgt + 128), (1, rows)],
        [pltpu.VMEM((nsrc, 128), F32), pltpu.VMEM((8, chunk), F32)],
        (ratio, *q, src_rows, scale),
        megabytes=4,
    )
    col_sums = trade(col_sums, "z")
    vmem = pl.BlockSpec(memory_space=pltpu.VMEM)
    tgt_pot, src_pot = pl.pallas_call(
        end_kernel,
        out_shape=[
            jax.ShapeDtypeStruct((X, ntgt // 128, 128), F32),
            pltpu.HBM((1, rows), F32),
        ],
        in_specs=[vmem] * 3,
        out_specs=[vmem, pl.BlockSpec(memory_space=pltpu.HBM)],
        scratch_shapes=[
            pltpu.VMEM((1, rows), F32),
            pltpu.SemaphoreType.DMA,
            pltpu.VMEM((ntgt // 128, 128), F32),
            pltpu.VMEM((8, chunk), F32),
        ],
        compiler_params=pltpu.CompilerParams(vmem_limit_bytes=4 * 2**20),
    )(col_sums, log_col, pot)
    return (src_pot.reshape(rows), trade(tgt_pot, "x").reshape(cols))


def solution(mesh):
    fine = Mesh(mesh.devices.reshape(Z, X, Y, C), ("z", "x", "y", "c"))
    row, col = ("z", "x"), ("y", "c")
    placed = (P(None, row), P(None, col), P(row), P(col))
    return jax.shard_map(
        on_device, mesh=fine, in_specs=placed, out_specs=(P(row), P(col)), check_vma=False
    )
```
